512 devices in a mesh: box: 32 (over z_lo, y), dir: 16 (over x, z_hi, core).
Axes of the slice: x: 4, y: 4, z: 16 (z_hi: 2, z_lo: 8; z = z_hi * 8 + z_lo), core: 2. Of those that a mesh axis runs over, the one named last changes fastest.
Arguments:
- source: bfloat16 [64, 2, 2, 256, 128], P(None, None, None, 'box'), may hold values from -6 to 6
- near_blocks: bfloat16 [27, 2, 64, 64], P(None, None, 'dir'), may hold values from -0.109375 to 0.109375
- near_mask: int32 [27, 256, 128], P(None, 'box'), may hold values 0 or 1
- radiate: bfloat16 [2, 8, 16, 64], P(None, None, 'dir'), may hold values from -0.5 to 0.5
- receive: bfloat16 [2, 8, 16, 64], P(None, None, None, 'dir'), may hold values from -0.375 to 0.375
- theta_one: float32 [16, 8], replicated, may hold values from -0.75 to 0.75
- theta_two: float32 [32, 16], replicated, may hold values from -0.5 to 0.5
- theta_three: float32 [64, 32], replicated, may hold values from -0.375 to 0.375
- phi_taps: float32 [3, 2, 3], replicated, may hold values from -3.5 to 3.5
- shift_one: float32 [8, 16, 32], P(None, None, 'dir'), may hold values from -3.140625 to 3.140625
- shift_two: float32 [8, 32, 64], P(None, None, 'dir'), may hold values from -3.140625 to 3.140625
- shift_three: float32 [8, 64, 128], P(None, None, 'dir'), may hold values from -3.140625 to 3.140625
- trans_one: float32 [32, 2, 16, 32], P(None, None, None, 'dir'), may hold values from -0.75 to 0.75
- trans_two: float32 [32, 2, 32, 64], P(None, None, None, 'dir'), may hold values from -0.75 to 0.75
- trans_three: float32 [32, 2, 64, 128], P(None, None, None, 'dir'), may hold values from -0.75 to 0.75
- far_lists: int32 [3, 32, 3], replicated, may hold values from -2 to 2, as said below
Outputs:
- product: float32 [64, 2, 2, 256, 128], P('dir', None, None, 'box')
The draws below stay inside these ranges and needn't reach their ends.
Inputs may be any that keep to these rules, and one draw needn't show every extreme that they name: `far_lists`: for each of the 3 levels the 32 rows are distinct offsets (dx, dy, dz) with every component in -2..2 and at least one component equal to -2 or 2; each level's list holds (-2, 0, 0) and (2, 0, 0).
All inputs are finite; a program needn't handle non-finite values. No bound on the sum of `near_mask` on one device may be relied on, other than what follows from the above.
Results may differ from the reference program's by a relative error of at most 0.0003.
Values may be sent and summed in bfloat16 or wider, within the bound.
A program may use at most 128 MiB of HBM per device.

```python
import jax
import jax.numpy as jnp
import numpy as np
from jax import lax

U = 64
RHS = 2
NEAR = 27
K = 32
NT0 = 8
NP0 = 16
GY = 8
GZ = 16
GX = 256
PLANE = 128
NT1 = 16
NT2 = 32
NT3 = 64
NP1 = 32
NP2 = 64
NP3 = 128


def far_offsets():
    span_values = np.arange(-2, 3)
    mesh_grid = np.stack(np.meshgrid(span_values, span_values, span_values, indexing='ij'), -1).reshape(-1, 3)
    keeping = np.abs(mesh_grid).max(axis=1) == 2
    return mesh_grid[keeping].astype(np.int32)


def axis_offsets():
    table = far_offsets()
    along = (table[:, 1] == 0) & (table[:, 2] == 0)
    return (table[along], table[~along])


def draw_far_lists(key, part):
    key = jax.random.fold_in(key, 7)
    fixed_rows, other_rows = axis_offsets()
    fixed_table = jnp.asarray(fixed_rows)
    other_table = jnp.asarray(other_rows)
    chosen = []
    for level in range(3):
        level_key = jax.random.fold_in(key, level)
        picks = jax.random.permutation(level_key, other_table.shape[0])[:K - 2]
        rows = jnp.concatenate([fixed_table, other_table[picks]], axis=0)
        order = jax.random.permutation(jax.random.fold_in(level_key, 11), K)
        chosen.append(rows[order])
    return jnp.stack(chosen).astype(jnp.int32)


def place_ends(drawn, key, smallest, top_value):
    longest = drawn.shape.index(max(drawn.shape))
    spots = []
    for shift in (0, 1):
        where = [jax.random.randint(jax.random.fold_in(key, axis), (), 0, length) for axis, length in enumerate(drawn.shape)]
        where[longest] = (where[longest] + shift) % drawn.shape[longest]
        spots.append(tuple(where))
    return drawn.at[spots[0]].set(smallest).at[spots[1]].set(top_value)


def block_levels(key, extent, cuts, smallest, high):
    level = 1.0
    for position, parts in cuts:
        draws = jax.random.uniform(jax.random.fold_in(jax.random.fold_in(key, 6), position), (parts,), jnp.float32, smallest / len(cuts), high / len(cuts))
        level = level * jnp.repeat(jnp.exp(draws), extent[position] // parts).reshape((-1,) + (1,) * (len(extent) - 1 - position))
    return level


def scatter_about(key, dims, scale, bound, cuts=(), held_as=jnp.bfloat16):
    drawn = jax.random.normal(key, dims, jnp.float32) * scale
    if len(cuts) > 0:
        drawn = block_levels(key, dims, cuts, -0.22, 0.18) * drawn
    return jnp.clip(drawn, min=-bound, max=bound).astype(held_as)


def setup_inputs(seed: int = 0) -> dict:
    seeds = jax.random.split(jax.random.key(seed), 17)
    source = scatter_about(seeds[0], (U, 2, RHS, GX, PLANE), 1.0, 6.0, ((3, 32),))
    near_blocks = scatter_about(seeds[1], (NEAR, 2, U, U), (2 * NEAR * U) ** -0.5, 0.109375, ((2, 16),))
    near_mask = place_ends((jax.random.randint(seeds[2], (NEAR, GX, PLANE), 0, 4) < 3).astype(jnp.int32), jax.random.fold_in(seeds[2], 1), 0, 1)
    radiate = scatter_about(seeds[3], (2, NT0, NP0, U), (2 * U) ** -0.5, 0.5, ((2, 16),))
    receive = scatter_about(seeds[4], (2, NT0, NP0, U), (2 * NT0 * NP0) ** -0.5, 0.375, ((3, 16),))
    theta_one = scatter_about(seeds[5], (NT1, NT0), (8 * NT0) ** -0.5, 0.75, (), jnp.float32)
    theta_two = scatter_about(seeds[6], (NT2, NT1), (8 * NT1) ** -0.5, 0.5, (), jnp.float32)
    theta_three = scatter_about(seeds[7], (NT3, NT2), (8 * NT2) ** -0.5, 0.375, (), jnp.float32)
    phi_taps = scatter_about(seeds[8], (3, 2, 3), 3 ** -0.5, 3.5, (), jnp.float32)
    shift_one = jnp.clip(jax.random.uniform(seeds[9], (8, NT1, NP1), jnp.float32, -3.140625, 3.140625), -3.140625, 3.140625)
    shift_two = jnp.clip(jax.random.uniform(seeds[10], (8, NT2, NP2), jnp.float32, -3.140625, 3.140625), -3.140625, 3.140625)
    shift_three = jnp.clip(jax.random.uniform(seeds[11], (8, NT3, NP3), jnp.float32, -3.140625, 3.140625), -3.140625, 3.140625)
    trans_one = scatter_about(seeds[12], (K, 2, NT1, NP1), (2 * K) ** -0.5, 0.75, ((3, 16),), jnp.float32)
    trans_two = scatter_about(seeds[13], (K, 2, NT2, NP2), (2 * K) ** -0.5, 0.75, ((3, 16),), jnp.float32)
    trans_three = scatter_about(seeds[14], (K, 2, NT3, NP3), (2 * K) ** -0.5, 0.75, ((3, 16),), jnp.float32)
    far_lists = draw_far_lists(jax.random.fold_in(seeds[16], 71), 0)
    return {"source": source, "near_blocks": near_blocks, "near_mask": near_mask, "radiate": radiate, "receive": receive, "theta_one": theta_one, "theta_two": theta_two, "theta_three": theta_three, "phi_taps": phi_taps, "shift_one": shift_one, "shift_two": shift_two, "shift_three": shift_three, "trans_one": trans_one, "trans_two": trans_two, "trans_three": trans_three, "far_lists": far_lists}


HIGHEST = lax.Precision.HIGHEST


def near_offsets():
    offset_list = []
    for shift_x in range(-1, 2):
        for shift_y in range(-1, 2):
            for shift_z in range(-1, 2):
                offset_list.append((shift_x, shift_y, shift_z))
    return offset_list


def phi_up(pattern, taps):
    extended = jnp.concatenate([pattern[:, :, :, -1:], pattern, pattern[:, :, :, :1]], axis=3)
    count = pattern.shape[3]
    doubled = jnp.repeat(extended, 2, axis=3)
    weights = jnp.tile(taps, (count, 1))
    result = jnp.zeros(pattern.shape[:3] + (2 * count,) + pattern.shape[4:], jnp.float32)
    for tap_index in range(3):
        window = doubled[:, :, :, 2 * tap_index:2 * tap_index + 2 * count]
        result = result + weights[:, tap_index].reshape(1, 1, 1, -1, 1, 1, 1) * window
    return result


def phi_down(pattern, taps):
    count = pattern.shape[3] // 2
    pieces = []
    for tap_index in range(3):
        weighted = jnp.tile(taps[:, tap_index], count).reshape(1, 1, 1, -1, 1, 1, 1) * pattern
        pieces.append(weighted.reshape(pattern.shape[:3] + (count, 2) + pattern.shape[4:]).sum(axis=4))
    stacked = jnp.concatenate(pieces, axis=0)
    extended = jnp.concatenate([stacked[:, :, :, -1:], stacked, stacked[:, :, :, :1]], axis=3)
    result = jnp.zeros(pattern.shape[:3] + (count,) + pattern.shape[4:], jnp.float32)
    for tap_index in range(3):
        result = result + extended[2 * tap_index:2 * tap_index + 2, :, :, 2 - tap_index:2 - tap_index + count]
    return result


def theta_apply(matrix, pattern):
    return jnp.einsum("st,crtpxyz->crspxyz", matrix, pattern, precision=HIGHEST)


def theta_back(matrix, pattern):
    return jnp.einsum("st,crspxyz->crtpxyz", matrix, pattern, precision=HIGHEST)


def gather_children(pattern, angles):
    shape_now = pattern.shape
    theta_count, phi_count = shape_now[2], shape_now[3]
    split = pattern.reshape(shape_now[:4] + (shape_now[4] // 2, 2, shape_now[5] // 2, 2, shape_now[6] // 2, 2))
    cosine = jnp.cos(angles).reshape(2, 2, 2, theta_count, phi_count)
    sine = jnp.sin(angles).reshape(2, 2, 2, theta_count, phi_count)
    form = "rtpaxbyez,xyztp->rtpabe"
    real_part = jnp.einsum(form, split[0], cosine, precision=HIGHEST) - jnp.einsum(form, split[1], sine, precision=HIGHEST)
    imag_part = jnp.einsum(form, split[1], cosine, precision=HIGHEST) + jnp.einsum(form, split[0], sine, precision=HIGHEST)
    return jnp.stack([real_part, imag_part])


def spread_children(pattern, angles):
    shape_now = pattern.shape
    theta_count, phi_count = shape_now[2], shape_now[3]
    cosine = jnp.cos(angles).reshape(2, 2, 2, theta_count, phi_count)
    sine = jnp.sin(angles).reshape(2, 2, 2, theta_count, phi_count)
    form = "rtpabe,xyztp->rtpaxbyez"
    real_part = jnp.einsum(form, pattern[0], cosine, precision=HIGHEST) + jnp.einsum(form, pattern[1], sine, precision=HIGHEST)
    imag_part = jnp.einsum(form, pattern[1], cosine, precision=HIGHEST) - jnp.einsum(form, pattern[0], sine, precision=HIGHEST)
    full_shape = shape_now[1:4] + (2 * shape_now[4], 2 * shape_now[5], 2 * shape_now[6])
    return jnp.stack([real_part.reshape(full_shape), imag_part.reshape(full_shape)])


def reference(source, near_blocks, near_mask, radiate, receive, theta_one, theta_two, theta_three, phi_taps, shift_one, shift_two, shift_three, trans_one, trans_two, trans_three, far_lists):
    boxes = GX * GY * GZ
    source_full = source.astype(jnp.float32).reshape(U, 2, RHS, GX, GY, GZ)
    padded = jnp.pad(source_full, ((0, 0),) * 3 + ((1, 1),) * 3)
    blocks = near_blocks.astype(jnp.float32)
    mask_float = near_mask.astype(jnp.float32).reshape(NEAR, boxes)
    near_total = jnp.zeros((U, 2, RHS, boxes), jnp.float32)
    for index_k, (shift_x, shift_y, shift_z) in enumerate(near_offsets()):
        moved = padded[:, :, :, 1 + shift_x:1 + shift_x + GX, 1 + shift_y:1 + shift_y + GY, 1 + shift_z:1 + shift_z + GZ].reshape(U, 2, RHS, boxes)
        product = jnp.einsum("cvu,udrb->cdvrb", blocks[index_k], moved, precision=HIGHEST)
        term = jnp.stack([product[0, 0] - product[1, 1], product[0, 1] + product[1, 0]], axis=1)
        near_total = near_total + mask_float[index_k] * term
    flat_radiate = radiate.astype(jnp.float32).reshape(2, NT0 * NP0, U)
    leaf_product = jnp.einsum("cqu,udrb->cdrqb", flat_radiate, source_full.reshape(U, 2, RHS, boxes), precision=HIGHEST)
    leaf = jnp.stack([leaf_product[0, 0] - leaf_product[1, 1], leaf_product[0, 1] + leaf_product[1, 0]])
    leaf = leaf.reshape(2, RHS, NT0, NP0, GX, GY, GZ)
    thetas = (theta_one, theta_two, theta_three)
    shifts = (shift_one, shift_two, shift_three)
    tables = (trans_one, trans_two, trans_three)
    patterns = [leaf]
    for level in range(3):
        moved = theta_apply(thetas[level], phi_up(patterns[-1], phi_taps[level]))
        patterns.append(gather_children(moved, shifts[level]))
    fields = []
    for level in range(3):
        table = tables[level]
        total = jnp.zeros(patterns[level + 1].shape, jnp.float32)
        pattern = patterns[level + 1]
        padded_level = jnp.pad(pattern, ((0, 0),) * 4 + ((2, 2), (2, 2), (2, 2)))
        zero = jnp.int32(0)
        for index_k in range(K):
            offset = far_lists[level, index_k].astype(jnp.int32)
            start = (zero, zero, zero, zero, offset[0] + 2, offset[1] + 2, offset[2] + 2)
            window = lax.dynamic_slice(padded_level, start, pattern.shape)
            table_real = table[index_k, 0][:, :, None, None, None]
            table_imag = table[index_k, 1][:, :, None, None, None]
            real_part = table_real * window[0] - table_imag * window[1]
            imag_part = table_real * window[1] + table_imag * window[0]
            total = total + jnp.stack([real_part, imag_part])
        fields.append(total)
    incoming = fields[2]
    for level in (2, 1, 0):
        spread = spread_children(incoming, shifts[level])
        spread = theta_back(thetas[level], spread)
        spread = phi_down(spread, phi_taps[level])
        if level > 0:
            incoming = fields[level - 1] + spread
        else:
            incoming = spread
    flat_in = incoming.reshape(2, RHS, NT0, NP0, boxes)
    columns = receive.astype(jnp.float32)
    form = "tnu,rtnb->urb"
    real_part = jnp.einsum(form, columns[0], flat_in[0], precision=HIGHEST) - jnp.einsum(form, columns[1], flat_in[1], precision=HIGHEST)
    imag_part = jnp.einsum(form, columns[0], flat_in[1], precision=HIGHEST) + jnp.einsum(form, columns[1], flat_in[0], precision=HIGHEST)
    far = jnp.stack([real_part, imag_part], axis=1)
    return (near_total + far).reshape(U, 2, RHS, GX, GY * GZ)
```

```python
import functools

import jax
import jax.numpy as jnp
import numpy as np
from jax import lax
from jax.experimental import pallas as pl
from jax.experimental.pallas import tpu as pltpu
from jax.sharding import PartitionSpec as P

MESH = pl.DeviceIdType.MESH
F32 = jnp.float32
BF16 = jnp.bfloat16
VMEM_LIMIT = 56 * 1024 * 1024


def iota(shape, dim):
    return lax.broadcasted_iota(jnp.int32, shape, dim)


def split(a):
    high = a.astype(BF16)
    return high, (a - high.astype(F32)).astype(BF16)


def dot(a, b, dims=((1,), (0,))):
    return lax.dot_general(a, b, (dims, ((), ())), preferred_element_type=F32)


def dot3(a, b, dims=((1,), (0,))):
    a_high, a_low = split(a)
    b_high, b_low = split(b)
    return dot(a_high, b_high, dims) + (dot(a_high, b_low, dims) + dot(a_low, b_high, dims))


def dot_left(a, b, dims=((1,), (0,))):
    a_high, a_low = split(a)
    return dot(a_high, b, dims) + dot(a_low, b, dims)


def dot_right(a, b, dims=((1,), (0,))):
    b_high, b_low = split(b)
    return dot(a, b_high, dims) + dot(a, b_low, dims)


def onehot(condition):
    return jnp.where(condition, 1.0, 0.0).astype(BF16)


def interpolation(taps, level, theta, fine, coarse, wide, first, transposed):
    (fine_p, fine_t), (coarse_p, coarse_t) = fine, coarse
    if transposed:
        spread = onehot(iota((fine_t, fine_p * fine_t), 1) % fine_t == iota((fine_t, fine_p * fine_t), 0))
        tiled = jnp.concatenate([dot_left(theta, spread)] * coarse_p, axis=0)
        fine_dim, coarse_dim = 1, 0
    else:
        spread = onehot(
            iota((coarse_t, coarse_p * coarse_t), 1) % coarse_t == iota((coarse_t, coarse_p * coarse_t), 0)
        )
        tiled = jnp.concatenate([dot_left(theta, spread)] * fine_p, axis=0)
        fine_dim, coarse_dim = 0, 1
    p = iota(tiled.shape, fine_dim) // fine_t
    tap = iota(tiled.shape, coarse_dim) // coarse_t - first(p)
    even = wide(p) % 2 == 0
    weight = jnp.zeros(tiled.shape, F32)
    for j in range(3):
        value = jnp.where(even, taps[6 * level + j], taps[6 * level + 3 + j])
        weight = jnp.where(tap == j, value, weight)
    return weight * tiled


def turned(x):
    even = iota(x.shape, 1) % 2 == 0
    count = x.shape[1]
    return jnp.where(even, -pltpu.roll(x, count - 1, 1), pltpu.roll(x, 1, 1))


def child_of_box(index):
    return 4 * (index // 32 % 2) + 2 * (index // 8 % 2) + index % 2


def parent_of_box(index):
    return index // 64 * 8 + index // 16 % 2 * 4 + index // 2 % 4


def upward(
    where, taps, source, shuffle, tables, rims, own_one, own_two, phase_three,
    theta_one, theta_two, theta_two_t, theta_three_t,
    one_ref, two_ref, three_ref, back_two_ref, up_three_ref, phase_two_ref, far_high_ref, far_low_ref,
    leaf, shape_high, shape_low,
):
    me = where[0]
    up_one = interpolation(
        taps, 0, theta_one[...], (6, 16), (5, 8), lambda p: p, lambda p: p // 2, False
    )
    up_two = interpolation(
        taps, 1, theta_two[...], (6, 32), (6, 16), lambda p: p + 1, lambda p: (p + 1) // 2, False
    )
    back_two_ref[...] = interpolation(
        taps, 1, theta_two_t[...], (6, 32), (6, 16), lambda p: p + 1, lambda p: (p + 1) // 2, True
    )
    up_three = interpolation(
        taps, 2, theta_three_t[...], (8, 64), (6, 32), lambda p: p, lambda p: p // 2, True
    )
    up_three_ref[...] = up_three

    gathered = tables[...].astype(F32)
    radiate = jnp.concatenate([gathered[(a - 2) % 16, 8:16] for a in range(5)], axis=0)
    blocks = jnp.concatenate([gathered[e, 0:8] for e in range(16)], axis=0)
    lane = iota((128, 640), 1)
    pick = onehot(iota((128, 640), 0) == lane // 128 * 8 + lane % 8)
    sender = (iota((128, 640), 0) // 8 + me) % 16
    placed = jnp.where(lane % 128 // 8 == sender, dot(blocks.astype(BF16), pick), 0.0)
    summed = placed[0:8]
    for e in range(1, 16):
        summed = summed + placed[8 * e : 8 * e + 8]
    receive = jnp.concatenate([summed[:, 128 * a : 128 * a + 128] for a in range(5)], axis=0)
    send_real = dot_left(up_one, radiate.astype(BF16))
    take_real = dot_left(up_one, receive.astype(BF16))
    send_turned = turned(send_real)
    take_turned = turned(take_real)
    angles = jnp.concatenate([rims[0], own_one[...], rims[1]], axis=0)
    even = iota((96, 128), 1) % 2 == 0
    for o in range(8):
        cosine = angles[:, o : o + 1]
        sine = angles[:, 8 + o : 9 + o]
        moved = cosine * send_real + sine * send_turned
        swapped = jnp.where(even, pltpu.roll(moved, 127, 1), pltpu.roll(moved, 1, 1))
        rows = jnp.concatenate([jnp.where(even, moved, -moved), swapped], axis=0)
        high, low = split(rows)
        shape_high[:, 128 * o : 128 * o + 128] = high
        shape_low[:, 128 * o : 128 * o + 128] = low
        moved = cosine * take_real - sine * take_turned
        columns = jnp.concatenate([moved, turned(moved)], axis=0)
        high, low = split(columns.T)
        far_high_ref[128 * o : 128 * o + 128, :] = high
        far_low_ref[128 * o : 128 * o + 128, :] = low
    for r in range(2):
        for ox in range(2):
            mixed = dot(source[r, ox], shuffle[...]).astype(BF16)
            for o in range(4):
                row = 128 * (4 * ox + o)
                leaf[row : row + 128, 128 * r : 128 * r + 128] = mixed[:, 128 * o : 128 * o + 128]
    level_one = dot(shape_high[...], leaf[...]) + dot(shape_low[...], leaf[...])
    own = jnp.concatenate(
        [level_one[96 * c + 32 : 96 * c + 64, 128 * r : 128 * r + 128] for c in range(2) for r in range(2)],
        axis=0,
    )
    one_ref[...] = own.T

    edges = [pltpu.roll(rims[side], 112, 1) for side in range(2)]
    angles = jnp.concatenate([edges[0], own_two[...], edges[1]], axis=0)
    lane = iota((128, 256), 1)
    kind = child_of_box(lane % 128) + 8 * (lane // 128)
    phases = dot_left(angles, onehot(iota((128, 256), 0) == kind))
    phase_two_ref[...] = phases
    cosine, sine = phases[:, :128], phases[:, 128:]
    parent = onehot(parent_of_box(iota((16, 128), 1)) == iota((16, 128), 0))
    real = dot3(up_two, level_one[:96])
    imag = dot3(up_two, level_one[96:])
    parts = []
    for c in range(2):
        for r in range(2):
            x, y = real[:, 128 * r : 128 * r + 128], imag[:, 128 * r : 128 * r + 128]
            value = x * cosine - y * sine if c == 0 else y * cosine + x * sine
            parts.append(dot_right(parent, value, ((1,), (1,))))
    for index in range(4):
        two_ref[:, 128 * index : 128 * index + 128] = parts[index][:, 32:160]
    level_two = jnp.concatenate(parts, axis=0)
    upper = dot3(level_two, up_three)
    cosine, sine = phase_three[0:16], phase_three[16:32]
    parts = []
    for c in range(2):
        for r in range(2):
            x, y = upper[16 * r : 16 * r + 16], upper[32 + 16 * r : 48 + 16 * r]
            parts.append(x * cosine - y * sine if c == 0 else y * cosine + x * sine)
    row = iota((8, 64), 1)
    together = onehot(row // 16 * 2 + row // 2 % 2 == iota((8, 64), 0))
    three_ref[...] = dot_right(together, jnp.concatenate(parts, axis=0))


def near_part(where, source, halo, blocks, mask, near_ref, products, rolled):
    first, last = where[1] == 0, where[2] == 0
    lane = iota((8, 128), 1)
    for k in range(27):
        dy, dz = k // 3 % 3 - 1, k % 3 - 1
        y, z = lane // 16 + dy, lane % 16 + dz
        valid = (y >= 0) & (y < 8) & (z >= 0) & (z < 16)
        values = jnp.where(valid, mask[k].astype(F32), 0.0)
        rolled[k] = pltpu.roll(values, (16 * dy + dz) % 128, 1)
    for r in range(2):
        for side in range(2):
            edge = dot(blocks[...], halo[side, r])
            products[r, 9 * side] = jnp.where(last if side else first, 0.0, edge)
        for ox in range(2):
            layers = dot(blocks[...], source[r, ox])
            for x in range(4):
                products[r, 1 + 2 * x + ox] = layers[:, 128 * x : 128 * x + 128]
    for r in range(2):
        for x in range(8):
            total = jnp.zeros((8, 128), F32)
            for inner in range(9):
                dy, dz = inner // 3 - 1, inner % 3 - 1
                term = jnp.zeros((8, 128), F32)
                for dx in range(3):
                    k = 9 * dx + inner
                    term = term + products[r, x + dx, 8 * k : 8 * k + 8, :] * rolled[k, x : x + 1, :]
                total = total + pltpu.roll(term, (-16 * dy - dz) % 128, 1)
            near_ref[:, r, x, :] = total


def shifted_rows(block, shift, valid):
    moved = pltpu.roll(block, (-shift) % 8, 0) if shift % 8 else block
    return jnp.where(valid, moved, 0.0)


def downward(
    where, lists, one, halo_one, two, halo_two, three, halo_three, table_one, table_two, table_three,
    phase_three, back_two, up_three, phase_two, far_high, far_low,
    partial_ref,
    ext_one, ext_two, ext_three,
):
    first, last = where[1] == 0, where[2] == 0
    first_two, last_two = where[1] < 2, where[2] < 2
    zero = jnp.zeros((8, 128), F32)
    z = iota((8, 128), 0)
    for shift in range(5):
        dz = shift - 2
        valid = (z + dz >= 0) & (z + dz < 8)
        for x in range(8):
            for y in (0, 1, 6, 7):
                ext_one[shift, x, y] = zero
            for y in range(4):
                row = 8 * y + 32 * (x % 2)
                if x < 2:
                    block = jnp.where(first, 0.0, halo_one[0, row : row + 8, :])
                elif x > 5:
                    block = jnp.where(last, 0.0, halo_one[1, row : row + 8, :])
                else:
                    block = one[32 * (x - 2) + 8 * y : 32 * (x - 2) + 8 * y + 8, :]
                ext_one[shift, x, y + 2] = shifted_rows(block, dz, valid)
    zero = jnp.zeros((8, 512), F32)
    y, z = iota((8, 512), 0) // 4, iota((8, 512), 0) % 4
    for shift in range(25):
        dy, dz = shift // 5 - 2, shift % 5 - 2
        valid = (y + dy >= 0) & (y + dy < 2) & (z + dz >= 0) & (z + dz < 4)
        for x in range(6):
            if abs(dy) == 2:
                ext_two[shift, x] = zero
                continue
            row = 8 * (x % 2)
            if x < 2:
                block = jnp.where(first, 0.0, halo_two[0, row : row + 8, :])
            elif x > 3:
                block = jnp.where(last, 0.0, halo_two[1, row : row + 8, :])
            else:
                block = two[row : row + 8, :]
            ext_two[shift, x] = shifted_rows(block, 4 * dy + dz, valid)
    z = iota((8, 512), 0) % 2
    for x in range(5):
        if x == 2:
            block = three[...]
        else:
            missing = (first_two, first, None, last, last_two)[x]
            block = jnp.where(missing, 0.0, halo_three[(0, 1, None, 2, 3)[x]])
        for shift in range(3):
            dz = shift - 1
            ext_three[shift, x] = shifted_rows(block, dz, (z + dz >= 0) & (z + dz < 2))
        ext_three[3, x] = zero

    real = jnp.zeros((4, 4, 8, 128), F32)
    imag = jnp.zeros((4, 4, 8, 128), F32)
    for k in range(32):
        dx, dy, dz = lists[3 * k], lists[3 * k + 1], lists[3 * k + 2]
        window = ext_one[dz + 2, pl.ds(dx + 2, 4), pl.ds(dy + 2, 4)]
        real = real + window * table_one[2 * k : 2 * k + 1, :]
        imag = imag + window * table_one[2 * k + 1 : 2 * k + 2, :]
    imag = imag.reshape(128, 128)
    turned_imag = pltpu.roll(imag, 64, 1)
    field = real.reshape(128, 128) + jnp.where(iota((128, 128), 1) < 64, -turned_imag, turned_imag)
    field_one = field.T

    reals = [jnp.zeros((2, 8, 128), F32) for _ in range(4)]
    for k in range(32):
        dx, dy, dz = lists[96 + 3 * k], lists[97 + 3 * k], lists[98 + 3 * k]
        window = ext_two[5 * dy + dz + 12, pl.ds(dx + 2, 2)]
        x = table_two[2 * k : 2 * k + 1, :]
        y = table_two[2 * k + 1 : 2 * k + 2, :]
        parts = [window[:, :, 128 * i : 128 * i + 128] for i in range(4)]
        for r in range(2):
            reals[r] = reals[r] + (x * parts[r] - y * parts[2 + r])
            reals[2 + r] = reals[2 + r] + (x * parts[2 + r] + y * parts[r])
    side = jnp.zeros((64, 32), F32)
    field_two = jnp.concatenate([side, jnp.concatenate(reals, axis=0).reshape(64, 128), side], axis=1)

    real = jnp.zeros((8, 512), F32)
    imag = jnp.zeros((8, 512), F32)
    for k in range(32):
        dx, dy, dz = lists[192 + 3 * k], lists[193 + 3 * k], lists[194 + 3 * k]
        inside = (dy == 0) & (dz >= -1) & (dz <= 1)
        window = ext_three[jnp.where(inside, dz + 1, 3), dx + 2]
        real = real + window * table_three[2 * k : 2 * k + 1, :]
        imag = imag + window * table_three[2 * k + 1 : 2 * k + 2, :]
    imag = pltpu.roll(imag, 4, 0)
    incoming = real + jnp.where(iota((8, 512), 0) < 4, -imag, imag)

    row = iota((64, 8), 0)
    apart = onehot(row // 16 * 2 + row // 2 % 2 == iota((64, 8), 1))
    spread = dot_right(apart, incoming)
    cosine, sine = phase_three[0:16], phase_three[16:32]
    parts = []
    for c in range(2):
        for r in range(2):
            x, y = spread[16 * r : 16 * r + 16], spread[32 + 16 * r : 48 + 16 * r]
            parts.append(x * cosine + y * sine if c == 0 else y * cosine - x * sine)
    level_two = field_two + dot3(jnp.concatenate(parts, axis=0), up_three[...], ((1,), (1,)))
    parent = onehot(parent_of_box(iota((16, 128), 1)) == iota((16, 128), 0))
    columns = level_two.T
    spread = [dot_left(columns[:, 16 * i : 16 * i + 16], parent) for i in range(4)]
    cosine, sine = phase_two[:, :128], phase_two[:, 128:]
    real = jnp.concatenate([spread[r] * cosine + spread[2 + r] * sine for r in range(2)], axis=1)
    imag = jnp.concatenate([spread[2 + r] * cosine - spread[r] * sine for r in range(2)], axis=1)
    pad = jnp.zeros((32, 256), F32)
    level_one = []
    for c, value in enumerate((real, imag)):
        field = jnp.concatenate([field_one[64 * c + 32 * r : 64 * c + 32 * r + 32] for r in range(2)], axis=1)
        level_one.append(dot3(back_two[...], value) + jnp.concatenate([pad, field, pad], axis=0))
    high, low = split(jnp.concatenate(level_one, axis=0))
    for o in range(8):
        rows = slice(128 * o, 128 * o + 128)
        total = dot(far_high[rows], high) + (dot(far_high[rows], low) + dot(far_low[rows], high))
        for owner in range(16):
            partial_ref[owner % 2, owner // 4, owner // 2 % 2, 8 * o : 8 * o + 8, :] = total[
                8 * owner : 8 * owner + 8
            ]


def finish(far, near, unshuffle, out_ref):
    rows = []
    for r in range(2):
        for ox in range(2):
            pieces = [
                far[8 * (4 * ox + o) : 8 * (4 * ox + o) + 8, 128 * r : 128 * r + 128] for o in range(4)
            ]
            rows.append(jnp.concatenate(pieces, axis=1))
    leaf = dot_left(jnp.concatenate(rows, axis=0), unshuffle[...])
    for r in range(2):
        for ox in range(2):
            for x in range(4):
                row = 8 * (2 * r + ox)
                out_ref[:, r, 2 * x + ox, :] = (
                    near[:, r, 2 * x + ox, :] + leaf[row : row + 8, 128 * x : 128 * x + 128]
                )


def barrier(peers, maybe=()):
    sem = pltpu.get_barrier_semaphore()
    count = len(peers)
    for peer in peers:
        pl.semaphore_signal(sem, inc=1, device_id=peer, device_id_type=MESH)
    for condition, peer in maybe:
        @pl.when(condition)
        def _(peer=peer):
            pl.semaphore_signal(sem, inc=1, device_id=peer, device_id_type=MESH)

        count = count + jnp.where(condition, 1, 0)
    pl.semaphore_wait(sem, count)


def remote(source, target, send, receive, peer):
    return pltpu.make_async_remote_copy(
        src_ref=source, dst_ref=target, send_sem=send, recv_sem=receive, device_id=peer, device_id_type=MESH
    )


def gather_kernel(
    dirs, boxes, tables, to_next, to_previous, source,
    gathered, rims, halo,
    send, receive, rim_send, rim_receive, halo_send, halo_receive, local,
):
    me, box = lax.axis_index("dir"), lax.axis_index("box")
    peers = [{"dir": lax.rem(me + e, dirs)} for e in range(1, dirs)]
    has_left, has_right = box > 0, box < boxes - 1
    left, right = {"box": lax.rem(box + boxes - 1, boxes)}, {"box": lax.rem(box + 1, boxes)}
    own = pltpu.make_async_copy(tables.at[me], gathered.at[0], local)
    own.start()
    barrier(peers, ((has_left, left), (has_right, right)))
    to_right = remote(
        source.at[:, 1, :, pl.ds(384, 128)], halo.at[0], halo_send.at[0], halo_receive.at[0], right
    )
    to_left = remote(source.at[:, 0, :, pl.ds(0, 128)], halo.at[1], halo_send.at[1], halo_receive.at[1], left)
    copies = [
        remote(to_next, rims.at[0], rim_send.at[0], rim_receive.at[0], peers[0]),
        remote(to_previous, rims.at[1], rim_send.at[1], rim_receive.at[1], peers[-1]),
    ]
    for e in range(1, dirs):
        copies.append(
            remote(
                tables.at[lax.rem(me + e, dirs)], gathered.at[dirs - e], send.at[e], receive.at[dirs - e],
                peers[e - 1],
            )
        )
    for copy in copies:
        copy.start()
    pl.when(has_right)(to_right.start)
    pl.when(has_left)(to_left.start)
    for copy in copies:
        copy.wait_send()
    for copy in copies:
        copy.wait_recv()
    pl.when(has_right)(to_right.wait_send)
    pl.when(has_left)(to_left.wait_send)
    pl.when(has_left)(to_right.wait_recv)
    pl.when(has_right)(to_left.wait_recv)
    own.wait()


def halo_kernel(boxes, one, two, three, halo_one, halo_two, halo_three, send, receive):
    box = lax.axis_index("box")
    has = {-1: box > 0, 1: box < boxes - 1, -2: box > 1, 2: box < boxes - 2}
    peer = {e: {"box": lax.rem(box + boxes + e, boxes)} for e in has}
    barrier([], [(has[e], peer[e]) for e in has])
    copies = [
        (1, one.at[pl.ds(64, 64)], halo_one.at[0]),
        (-1, one.at[pl.ds(0, 64)], halo_one.at[1]),
        (1, two, halo_two.at[0]),
        (-1, two, halo_two.at[1]),
        (2, three, halo_three.at[0]),
        (1, three, halo_three.at[1]),
        (-1, three, halo_three.at[2]),
        (-2, three, halo_three.at[3]),
    ]
    made = [
        (e, remote(source, target, send.at[i], receive.at[i], peer[e]))
        for i, (e, source, target) in enumerate(copies)
    ]
    for e, copy in made:
        pl.when(has[e])(copy.start)
    for e, copy in made:
        pl.when(has[e])(copy.wait_send)
        pl.when(has[-e])(copy.wait_recv)


def sum_kernel(partial, total, got_core, held, got_x, held_x, got_z, send, receive):
    me = lax.axis_index("dir")
    x, z, core = me // 4, me // 2 % 2, me % 2
    sibling = {"dir": me + 1 - 2 * core}
    across = {"dir": me + 2 - 4 * z}
    others = [{"dir": lax.rem(me + 4 * e, 16)} for e in range(1, 4)]
    barrier([sibling, across] + others)
    copy = remote(partial.at[1 - core], got_core, send.at[0], receive.at[0], sibling)
    copy.start()
    copy.wait()
    held[...] = partial[core] + got_core[...]
    copies = [
        remote(held.at[lax.rem(x + e, 4)], got_x.at[3 - e], send.at[e], receive.at[4 - e], others[e - 1])
        for e in range(1, 4)
    ]
    for copy in copies:
        copy.start()
    for copy in copies:
        copy.wait_send()
    for copy in copies:
        copy.wait_recv()
    held_x[...] = held[x] + (got_x[0] + got_x[1] + got_x[2])
    copy = remote(held_x.at[1 - z], got_z, send.at[4], receive.at[4], across)
    copy.start()
    copy.wait()
    total[...] = held_x[z] + got_z[...]


ANY = pl.BlockSpec(memory_space=pl.ANY)
VMEM = pl.BlockSpec(memory_space=pltpu.VMEM)
SMEM = pl.BlockSpec(memory_space=pltpu.SMEM)
DMA = pltpu.SemaphoreType.DMA


def shape(*dims, dtype=F32):
    return jax.ShapeDtypeStruct(dims, dtype)


def communicate(kernel, collective_id, in_specs, out_specs, out_shape, scratch, *args):
    return pl.pallas_call(
        kernel,
        out_shape=out_shape,
        in_specs=in_specs,
        out_specs=out_specs,
        scratch_shapes=scratch,
        compiler_params=pltpu.CompilerParams(
            collective_id=collective_id, has_side_effects=True, vmem_limit_bytes=VMEM_LIMIT
        ),
    )(*args)


def compute(kernel, scalars, out_shape, scratch, *args):
    specs = [SMEM] * scalars + [VMEM] * (len(args) - scalars)
    return pl.pallas_call(
        kernel,
        out_shape=out_shape,
        in_specs=specs,
        out_specs=jax.tree.map(lambda _: VMEM, out_shape),
        scratch_shapes=scratch,
        compiler_params=pltpu.CompilerParams(vmem_limit_bytes=VMEM_LIMIT),
    )(*args)


def gather_tables(tables, to_next, to_previous, source):
    dirs, boxes = lax.axis_size("dir"), lax.axis_size("box")
    return communicate(
        functools.partial(gather_kernel, dirs, boxes), 1, [ANY] * 4, [ANY] * 3,
        [shape(16, 16, 128, dtype=BF16), shape(2, 32, 128), shape(2, 2, 128, 128, dtype=BF16)],
        [DMA((16,)), DMA((16,)), DMA((2,)), DMA((2,)), DMA((2,)), DMA((2,)), DMA],
        tables, to_next, to_previous, source,
    )


def exchange_halos(one, two, three):
    boxes = lax.axis_size("box")
    return communicate(
        functools.partial(halo_kernel, boxes), 2, [ANY] * 3, [ANY] * 3,
        [shape(2, 64, 128), shape(2, 16, 512), shape(4, 8, 512)],
        [DMA((8,)), DMA((8,))],
        one, two, three,
    )


def sum_over_dirs(partial):
    return communicate(
        sum_kernel, 3, [VMEM], VMEM, shape(64, 256),
        [
            pltpu.VMEM((4, 2, 64, 256), F32), pltpu.VMEM((4, 2, 64, 256), F32),
            pltpu.VMEM((3, 2, 64, 256), F32), pltpu.VMEM((2, 64, 256), F32), pltpu.VMEM((64, 256), F32),
            DMA((5,)), DMA((5,)),
        ],
        partial,
    )


def shuffle_table():
    index = np.arange(512)
    x, y, z = index // 128, index // 16 % 8, index % 16
    target = 256 * (y % 2) + 128 * (z % 2) + 32 * x + 8 * (y // 2) + z // 2
    return (target[:, None] == index[None, :]).astype(np.float32)


def turn_table(angles):
    rows = jnp.transpose(angles, (2, 1, 0)).reshape(-1, 8)
    return jnp.concatenate([jnp.cos(rows), jnp.sin(rows)], axis=1)


def to_lanes(table, copies):
    flat = jnp.transpose(table, (0, 1, 3, 2)).reshape(64, -1)
    return jnp.tile(flat, (1, copies))


def shards(
    source, near_blocks, near_mask, radiate, receive, theta_one, theta_two, theta_three, phi_taps,
    shift_one, shift_two, shift_three, trans_one, trans_two, trans_three, far_lists,
):
    dirs, boxes = lax.axis_size("dir"), lax.axis_size("box")
    me, box = lax.axis_index("dir"), lax.axis_index("box")
    where = jnp.stack([me, box, boxes - 1 - box]).astype(jnp.int32)
    layers = source.reshape(64, 2, 2, 4, 2, 128)
    layers = jnp.transpose(layers, (2, 4, 0, 1, 3, 5)).reshape(2, 2, 128, 512)
    taps = phi_taps.reshape(18)
    lists = far_lists.reshape(288)

    windows = jnp.transpose(receive, (2, 1, 3, 0))
    windows = jnp.stack([jnp.roll(windows, 2 - a, axis=0) for a in range(5)], axis=2).reshape(16, 8, 40)
    windows = jnp.pad(windows, ((0, 0), (0, 0), (0, 88)))
    outgoing = jnp.transpose(radiate[:, :, 0], (1, 2, 0)).reshape(1, 8, 128)
    tables = jnp.concatenate([windows, jnp.broadcast_to(outgoing, (16, 8, 128))], axis=1)
    turn_one, turn_two = turn_table(shift_one), turn_table(shift_two)
    own_one = jnp.pad(turn_one, ((0, 0), (0, 112)))
    own_two = jnp.pad(turn_two, ((0, 0), (0, 112)))
    to_next = jnp.pad(jnp.concatenate([turn_one, turn_two[96:]], axis=1), ((0, 0), (0, 96)))
    to_previous = jnp.pad(jnp.concatenate([turn_one, turn_two[:32]], axis=1), ((0, 0), (0, 96)))
    gathered, rims, halo = gather_tables(tables, to_next, to_previous, layers)

    angles = jnp.transpose(shift_three, (0, 2, 1)).reshape(2, 2, 1, 2, 512)
    angles = jnp.broadcast_to(angles, (2, 2, 2, 2, 512)).reshape(16, 512)
    phase_three = jnp.concatenate([jnp.cos(angles), jnp.sin(angles)], axis=0)
    shuffle = shuffle_table()
    one, two, three, back_two, up_three, phase_two, far_high, far_low = compute(
        upward, 2,
        [
            shape(128, 128), shape(16, 512), shape(8, 512), shape(96, 192), shape(192, 512),
            shape(192, 256), shape(1024, 192, dtype=BF16), shape(1024, 192, dtype=BF16),
        ],
        [pltpu.VMEM((1024, 256), BF16), pltpu.VMEM((192, 1024), BF16), pltpu.VMEM((192, 1024), BF16)],
        where, taps, layers, jnp.asarray(shuffle, BF16), gathered, rims, own_one, own_two, phase_three,
        theta_one, theta_two, theta_two.T, theta_three.T,
    )
    halo_one, halo_two, halo_three = exchange_halos(one, two, three)

    b_real, b_imag = near_blocks[:, 0], near_blocks[:, 1]
    rows = jnp.stack([jnp.stack([b_real, -b_imag], axis=-1), jnp.stack([b_imag, b_real], axis=-1)], axis=2)
    near = compute(
        near_part, 1, shape(8, 2, 8, 128),
        [pltpu.VMEM((2, 10, 216, 128), F32), pltpu.VMEM((27, 8, 128), F32)],
        where, layers, halo, rows.reshape(216, 128), near_mask,
    )
    partial = compute(
        downward, 2, shape(2, 4, 2, 64, 256),
        [
            pltpu.VMEM((5, 8, 8, 8, 128), F32), pltpu.VMEM((25, 6, 8, 512), F32),
            pltpu.VMEM((4, 5, 8, 512), F32),
        ],
        where, lists, one, halo_one, two, halo_two, three, halo_three,
        to_lanes(trans_one, 4), to_lanes(trans_two, 1), to_lanes(trans_three, 1),
        phase_three, back_two, up_three, phase_two, far_high, far_low,
    )
    far = sum_over_dirs(partial)
    out = compute(finish, 0, shape(8, 2, 8, 128), [], far, near, jnp.asarray(shuffle.T, BF16))
    return out.reshape(4, 2, 2, 8, 128)


def solution(mesh):
    placed = (
        P(None, None, None, "box", None),
        P(None, None, "dir", None),
        P(None, "box", None),
        P(None, None, "dir", None),
        P(None, None, None, "dir"),
        P(),
        P(),
        P(),
        P(),
        P(None, None, "dir"),
        P(None, None, "dir"),
        P(None, None, "dir"),
        P(None, None, None, "dir"),
        P(None, None, None, "dir"),
        P(None, None, None, "dir"),
        P(),
    )
    return jax.shard_map(
        shards,
        mesh=mesh,
        in_specs=placed,
        out_specs=P("dir", None, None, "box", None),
        check_vma=False,
    )
```

```python
import functools

import jax
import jax.numpy as jnp
import numpy as np
from jax import lax
from jax.experimental import pallas as pl
from jax.experimental.pallas import tpu as pltpu
from jax.sharding import PartitionSpec as P

MESH = pl.DeviceIdType.MESH
F32 = jnp.float32
BF16 = jnp.bfloat16
VMEM_LIMIT = 56 * 1024 * 1024


def iota(shape, dim):
    return lax.broadcasted_iota(jnp.int32, shape, dim)


def split(a):
    high = a.astype(BF16)
    return high, (a - high.astype(F32)).astype(BF16)


def dot(a, b, dims=((1,), (0,))):
    return lax.dot_general(a, b, (dims, ((), ())), preferred_element_type=F32)


def dot3(a, b, dims=((1,), (0,))):
    a_high, a_low = split(a)
    b_high, b_low = split(b)
    return dot(a_high, b_high, dims) + (dot(a_high, b_low, dims) + dot(a_low, b_high, dims))


def dot_left(a, b, dims=((1,), (0,))):
    a_high, a_low = split(a)
    return dot(a_high, b, dims) + dot(a_low, b, dims)


def dot_right(a, b, dims=((1,), (0,))):
    b_high, b_low = split(b)
    return dot(a, b_high, dims) + dot(a, b_low, dims)


def onehot(condition):
    return jnp.where(condition, 1.0, 0.0).astype(BF16)


def interpolation(taps, level, theta, fine, coarse, wide, first, transposed):
    (fine_p, fine_t), (coarse_p, coarse_t) = fine, coarse
    if transposed:
        spread = onehot(iota((fine_t, fine_p * fine_t), 1) % fine_t == iota((fine_t, fine_p * fine_t), 0))
        tiled = jnp.concatenate([dot_left(theta, spread)] * coarse_p, axis=0)
        fine_dim, coarse_dim = 1, 0
    else:
        spread = onehot(
            iota((coarse_t, coarse_p * coarse_t), 1) % coarse_t == iota((coarse_t, coarse_p * coarse_t), 0)
        )
        tiled = jnp.concatenate([dot_left(theta, spread)] * fine_p, axis=0)
        fine_dim, coarse_dim = 0, 1
    p = iota(tiled.shape, fine_dim) // fine_t
    tap = iota(tiled.shape, coarse_dim) // coarse_t - first(p)
    even = wide(p) % 2 == 0
    weight = jnp.zeros(tiled.shape, F32)
    for j in range(3):
        value = jnp.where(even, taps[level, 0:1, j : j + 1], taps[level, 1:2, j : j + 1])
        weight = jnp.where(tap == j, value, weight)
    return weight * tiled


def turned(x):
    even = iota(x.shape, 1) % 2 == 0
    count = x.shape[1]
    return jnp.where(even, -pltpu.roll(x, count - 1, 1), pltpu.roll(x, 1, 1))


def child_of_box(index):
    return 4 * (index // 32 % 2) + 2 * (index // 8 % 2) + index % 2


def parent_of_box(index):
    return index // 64 * 8 + index // 16 % 2 * 4 + index // 2 % 4


def shifted_rows(block, shift, valid):
    moved = pltpu.roll(block, (-shift) % 8, 0) if shift % 8 else block
    return jnp.where(valid, moved, 0.0)


def cosines(angles):
    return jnp.concatenate([jnp.cos(angles), jnp.sin(angles)], axis=0)


def remote(source, target, send, receive, peer):
    return pltpu.make_async_remote_copy(
        src_ref=source, dst_ref=target, send_sem=send, recv_sem=receive, device_id=peer, device_id_type=MESH
    )


def whole(
    dirs, boxes,
    source, near_blocks, mask, radiate, receive, theta_one, theta_two, theta_two_t, theta_three_t, taps,
    shift_one, shift_two, shift_three, trans_one, trans_two, trans_three, lists, shuffle,
    out_ref,
    message, gathered, rim_out, rims, leaf_halo, halo_one, halo_two, halo_three, one, two, three,
    leaf, shape_high, shape_low, far_high, far_low, products, rolled, near,
    table_one, table_two, table_three, ext_one, ext_two, ext_three,
    partial, got_core, held, got_x, held_x, got_z,
    send, receive_sem, rim_send, rim_receive, leaf_send, leaf_receive, halo_send, halo_receive,
    sum_send, sum_receive,
):
    me, box = lax.axis_index("dir"), lax.axis_index("box")
    has = {-1: box > 0, 1: box < boxes - 1, -2: box > 1, 2: box < boxes - 2}
    beside = {e: {"box": lax.rem(box + boxes + e, boxes)} for e in has}
    peers = {e: {"dir": lax.rem(me + e, dirs)} for e in range(1, dirs)}

    barrier = pltpu.get_barrier_semaphore()
    count = dirs - 1
    for e in range(1, dirs):
        pl.semaphore_signal(barrier, inc=1, device_id=peers[e], device_id_type=MESH)
    for e in has:
        @pl.when(has[e])
        def _(e=e):
            pl.semaphore_signal(barrier, inc=1, device_id=beside[e], device_id_type=MESH)

        count = count + jnp.where(has[e], 1, 0)

    taken = [receive[c, :, u, :].astype(F32) for c in range(2) for u in range(4)]
    lane = iota((64, 128), 1)
    sent = [dot(radiate[c], onehot(lane == 2 * iota((64, 128), 0) + c)) for c in range(2)]
    tile = jnp.concatenate([jnp.concatenate(taken, axis=1), sent[0] + sent[1]], axis=0).astype(BF16)
    message[...] = tile
    gathered[0] = tile
    angles_one = jnp.concatenate([shift_one[:, a, :] for a in range(2)], axis=1)
    angles_two = jnp.concatenate([shift_two[:, a, :] for a in range(4)], axis=1)
    pad = jnp.zeros((8, 64), F32)
    rim_out[0] = jnp.concatenate([angles_one, angles_two[:, 96:], pad], axis=1)
    rim_out[1] = jnp.concatenate([angles_one, angles_two[:, :32], pad], axis=1)

    up_one = interpolation(
        taps, 0, theta_one[...], (6, 16), (5, 8), lambda p: p, lambda p: p // 2, False
    )
    up_two = interpolation(
        taps, 1, theta_two[...], (6, 32), (6, 16), lambda p: p + 1, lambda p: (p + 1) // 2, False
    )
    back_two = interpolation(
        taps, 1, theta_two_t[...], (6, 32), (6, 16), lambda p: p + 1, lambda p: (p + 1) // 2, True
    )
    up_three = interpolation(
        taps, 2, theta_three_t[...], (8, 64), (6, 32), lambda p: p, lambda p: p // 2, True
    )
    for r in range(2):
        for ox in range(2):
            mixed = dot(source[r, ox], shuffle[...]).astype(BF16)
            for o in range(4):
                row = 128 * (4 * ox + o)
                leaf[row : row + 128, 128 * r : 128 * r + 128] = mixed[:, 128 * o : 128 * o + 128]
    for a in range(8):
        table_three[:, 64 * a : 64 * a + 64] = trans_three[:, a, :]
    for a in range(4):
        table_two[:, 32 * a : 32 * a + 32] = trans_two[:, a, :]
    for c in range(2):
        total = jnp.zeros((32, 128), F32)
        for a in range(2):
            place = onehot(iota((16, 128), 1) % 32 == 16 * a + iota((16, 128), 0))
            total = total + dot_left(trans_one[c, :, a, :], place, ((0,), (0,)))
        table_one[c] = total
    zero = jnp.zeros((8, 128), F32)
    for shift in range(5):
        for x in range(8):
            for y in (0, 1, 6, 7):
                ext_one[shift, x, y] = zero
    zero = jnp.zeros((8, 512), F32)
    for x in range(6):
        for shift in range(5):
            ext_two[shift, x] = zero
            ext_two[20 + shift, x] = zero
    for x in range(5):
        ext_three[3, x] = zero
    for side, e in enumerate((-1, 1)):
        @pl.when(jnp.logical_not(has[e]))
        def _(side=side):
            leaf_halo[side] = jnp.zeros((2, 128, 128), BF16)
            halo_one[side] = jnp.zeros((64, 128), F32)
            halo_two[side] = jnp.zeros((16, 512), F32)
    for slot, e in enumerate((-2, -1, 1, 2)):
        @pl.when(jnp.logical_not(has[e]))
        def _(slot=slot):
            halo_three[slot] = jnp.zeros((8, 512), F32)

    pl.semaphore_wait(barrier, count)
    table_copies = [
        remote(rim_out.at[0], rims.at[0], rim_send.at[0], rim_receive.at[0], peers[1]),
        remote(rim_out.at[1], rims.at[1], rim_send.at[1], rim_receive.at[1], peers[dirs - 1]),
    ]
    for e in range(1, dirs):
        table_copies.append(
            remote(message, gathered.at[dirs - e], send.at[e], receive_sem.at[dirs - e], peers[e])
        )
    for copy in table_copies:
        copy.start()
    leaf_copies = [
        (1, remote(
            source.at[:, 1, :, pl.ds(384, 128)], leaf_halo.at[0], leaf_send.at[0], leaf_receive.at[0], beside[1]
        )),
        (-1, remote(
            source.at[:, 0, :, pl.ds(0, 128)], leaf_halo.at[1], leaf_send.at[1], leaf_receive.at[1], beside[-1]
        )),
    ]
    for e, copy in leaf_copies:
        pl.when(has[e])(copy.start)

    lane = iota((64, 128), 1)
    double = dot(near_blocks[...], onehot(lane // 2 == iota((64, 128), 0))).astype(BF16)
    row, column = iota((216, 216), 0), iota((216, 216), 1)
    same = 8 * (row // 8) + 4 * (row % 2) + row % 8 // 2
    other = 8 * (row // 8) + 4 * (1 - row % 2) + row % 8 // 2
    kept = dot(onehot(column == same), double)
    crossed = dot(onehot(column == other), double)
    crossed = jnp.where(iota((216, 128), 0) % 2 == 0, -crossed, crossed)
    blocks = jnp.where(iota((216, 128), 1) % 2 == 0, kept, crossed).astype(BF16)
    lane = iota((8, 128), 1)
    for k in range(27):
        dy, dz = k // 3 % 3 - 1, k % 3 - 1
        y, z = lane // 16 + dy, lane % 16 + dz
        valid = (y >= 0) & (y < 8) & (z >= 0) & (z < 16)
        values = jnp.where(valid, mask[k].astype(F32), 0.0)
        rolled[k] = pltpu.roll(values, (16 * dy + dz) % 128, 1)
    for r in range(2):
        for ox in range(2):
            layers = dot(blocks, source[r, ox])
            for x in range(4):
                products[r, 1 + 2 * x + ox] = layers[:, 128 * x : 128 * x + 128]
    for e, copy in leaf_copies:
        pl.when(has[e])(copy.wait_send)
        pl.when(has[-e])(copy.wait_recv)
    for r in range(2):
        for side in range(2):
            products[r, 9 * side] = dot(blocks, leaf_halo[side, r])
    for r in range(2):
        for x in range(8):
            total = jnp.zeros((8, 128), F32)
            for inner in range(9):
                dy, dz = inner // 3 - 1, inner % 3 - 1
                term = jnp.zeros((8, 128), F32)
                for dx in range(3):
                    k = 9 * dx + inner
                    term = term + products[r, x + dx, 8 * k : 8 * k + 8, :] * rolled[k, x : x + 1, :]
                total = total + pltpu.roll(term, (-16 * dy - dz) % 128, 1)
            near[r, x] = total

    for copy in table_copies:
        copy.wait_send()
    for copy in table_copies:
        copy.wait_recv()
    pad = jnp.zeros((8, 32), F32)
    angles = jnp.concatenate([rims[0, :, 0:32], angles_one, rims[1, :, 0:32], pad], axis=1)
    turns = cosines(angles).T
    tables = gathered[...].astype(F32)
    sources = jnp.concatenate([tables[(a - 2) % 16, 8:16] for a in range(5)], axis=0)
    send_real = dot_left(up_one, sources.astype(BF16))
    send_turned = turned(send_real)
    even = iota((96, 128), 1) % 2 == 0
    for o in range(8):
        moved = turns[:96, o : o + 1] * send_real + turns[:96, 8 + o : 9 + o] * send_turned
        swapped = jnp.where(even, pltpu.roll(moved, 127, 1), pltpu.roll(moved, 1, 1))
        rows = jnp.concatenate([jnp.where(even, moved, -moved), swapped], axis=0)
        high, low = split(rows)
        shape_high[:, 128 * o : 128 * o + 128] = high
        shape_low[:, 128 * o : 128 * o + 128] = low
    level_one = dot(shape_high[...], leaf[...]) + dot(shape_low[...], leaf[...])
    own = jnp.concatenate(
        [level_one[96 * c + 32 : 96 * c + 64, 128 * r : 128 * r + 128] for c in range(2) for r in range(2)],
        axis=0,
    )
    one[...] = own.T
    halo_copies = [
        (e, remote(origin, target, halo_send.at[i], halo_receive.at[i], beside[e]))
        for i, (e, origin, target) in enumerate([
            (1, one.at[pl.ds(64, 64)], halo_one.at[0]),
            (-1, one.at[pl.ds(0, 64)], halo_one.at[1]),
            (1, two, halo_two.at[0]),
            (-1, two, halo_two.at[1]),
            (2, three, halo_three.at[0]),
            (1, three, halo_three.at[1]),
            (-1, three, halo_three.at[2]),
            (-2, three, halo_three.at[3]),
        ])
    ]
    for e, copy in halo_copies[:2]:
        pl.when(has[e])(copy.start)

    pad = jnp.zeros((8, 64), F32)
    angles = jnp.concatenate([rims[0, :, 32:64], angles_two, rims[1, :, 32:64], pad], axis=1)
    lane = iota((16, 256), 1)
    kind = child_of_box(lane % 128) + 8 * (lane // 128)
    phases = dot_left(cosines(angles).T[:192], onehot(iota((16, 256), 0) == kind))
    cosine_two, sine_two = phases[:, :128], phases[:, 128:]
    parent = onehot(parent_of_box(iota((16, 128), 1)) == iota((16, 128), 0))
    real = dot3(up_two, level_one[:96])
    imag = dot3(up_two, level_one[96:])
    parts = []
    for c in range(2):
        for r in range(2):
            x, y = real[:, 128 * r : 128 * r + 128], imag[:, 128 * r : 128 * r + 128]
            value = x * cosine_two - y * sine_two if c == 0 else y * cosine_two + x * sine_two
            parts.append(dot_right(parent, value, ((1,), (1,))))
    for index in range(4):
        two[:, 128 * index : 128 * index + 128] = parts[index][:, 32:160]
    for e, copy in halo_copies[2:4]:
        pl.when(has[e])(copy.start)
    level_two = jnp.concatenate(parts, axis=0)
    upper = dot3(level_two, up_three)
    turns_three = cosines(jnp.concatenate([shift_three[:, a, :] for a in range(8)], axis=1))
    row, column = iota((16, 8), 0), iota((16, 8), 1)
    expand = onehot(column == 4 * (row // 8) + 2 * (row // 4 % 2) + row % 2)
    cosine_three = dot_right(expand, turns_three[:8])
    sine_three = dot_right(expand, turns_three[8:])
    parts = []
    for c in range(2):
        for r in range(2):
            x, y = upper[16 * r : 16 * r + 16], upper[32 + 16 * r : 48 + 16 * r]
            parts.append(x * cosine_three - y * sine_three if c == 0 else y * cosine_three + x * sine_three)
    row = iota((8, 64), 1)
    together = onehot(row // 16 * 2 + row // 2 % 2 == iota((8, 64), 0))
    three[...] = dot_right(together, jnp.concatenate(parts, axis=0))
    for e, copy in halo_copies[4:]:
        pl.when(has[e])(copy.start)

    stacked = jnp.concatenate([tables[e, 0:8] for e in range(16)], axis=0)
    row, lane = iota((128, 640), 0), iota((128, 640), 1)
    azimuth = (me + 14 + lane // 128) % 16
    pick = onehot(row == 64 * (lane % 2) + 16 * (lane % 8 // 2) + azimuth)
    sender = (row // 8 + me) % 16
    placed = jnp.where(lane % 128 // 8 == sender, dot(stacked.astype(BF16), pick), 0.0)
    summed = placed[0:8]
    for e in range(1, 16):
        summed = summed + placed[8 * e : 8 * e + 8]
    targets = jnp.concatenate([summed[:, 128 * a : 128 * a + 128] for a in range(5)], axis=0)
    take_real = dot_left(up_one, targets.astype(BF16))
    take_turned = turned(take_real)
    for o in range(8):
        moved = turns[:96, o : o + 1] * take_real - turns[:96, 8 + o : 9 + o] * take_turned
        columns = jnp.concatenate([moved, turned(moved)], axis=0)
        high, low = split(columns.T)
        far_high[128 * o : 128 * o + 128, :] = high
        far_low[128 * o : 128 * o + 128, :] = low

    for e, copy in halo_copies[:2]:
        pl.when(has[-e])(copy.wait_recv)
    z = iota((8, 128), 0)
    for shift in range(5):
        dz = shift - 2
        valid = (z + dz >= 0) & (z + dz < 8)
        for x in range(8):
            for y in range(4):
                row = 8 * y + 32 * (x % 2)
                if x < 2 or x > 5:
                    block = halo_one[x // 4, row : row + 8, :]
                else:
                    block = one[32 * (x - 2) + 8 * y : 32 * (x - 2) + 8 * y + 8, :]
                ext_one[shift, x, y + 2] = shifted_rows(block, dz, valid)
    real = jnp.zeros((4, 4, 8, 128), F32)
    imag = jnp.zeros((4, 4, 8, 128), F32)
    for k in range(32):
        dx, dy, dz = lists[0, 0, k], lists[0, 1, k], lists[0, 2, k]
        window = ext_one[dz + 2, pl.ds(dx + 2, 4), pl.ds(dy + 2, 4)]
        real = real + window * table_one[0, k : k + 1, :]
        imag = imag + window * table_one[1, k : k + 1, :]
    imag = imag.reshape(128, 128)
    turned_imag = pltpu.roll(imag, 64, 1)
    field = real.reshape(128, 128) + jnp.where(iota((128, 128), 1) < 64, -turned_imag, turned_imag)
    field_one = field.T
    for e, copy in halo_copies[2:4]:
        pl.when(has[-e])(copy.wait_recv)
    y, z = iota((8, 512), 0) // 4, iota((8, 512), 0) % 4
    for shift in range(5, 20):
        dy, dz = shift // 5 - 2, shift % 5 - 2
        valid = (y + dy >= 0) & (y + dy < 2) & (z + dz >= 0) & (z + dz < 4)
        for x in range(6):
            row = 8 * (x % 2)
            if x < 2 or x > 3:
                block = halo_two[x // 3, row : row + 8, :]
            else:
                block = two[row : row + 8, :]
            ext_two[shift, x] = shifted_rows(block, 4 * dy + dz, valid)
    reals = [jnp.zeros((2, 8, 128), F32) for _ in range(4)]
    for k in range(32):
        dx, dy, dz = lists[1, 0, k], lists[1, 1, k], lists[1, 2, k]
        window = ext_two[5 * dy + dz + 12, pl.ds(dx + 2, 2)]
        x = table_two[2 * k : 2 * k + 1, :]
        y = table_two[2 * k + 1 : 2 * k + 2, :]
        parts = [window[:, :, 128 * i : 128 * i + 128] for i in range(4)]
        for r in range(2):
            reals[r] = reals[r] + (x * parts[r] - y * parts[2 + r])
            reals[2 + r] = reals[2 + r] + (x * parts[2 + r] + y * parts[r])
    side = jnp.zeros((64, 32), F32)
    field_two = jnp.concatenate([side, jnp.concatenate(reals, axis=0).reshape(64, 128), side], axis=1)
    for e, copy in halo_copies[4:]:
        pl.when(has[-e])(copy.wait_recv)
    z = iota((8, 512), 0) % 2
    for x in range(5):
        block = three[...] if x == 2 else halo_three[x - x // 3]
        for shift in range(3):
            dz = shift - 1
            ext_three[shift, x] = shifted_rows(block, dz, (z + dz >= 0) & (z + dz < 2))
    real = jnp.zeros((8, 512), F32)
    imag = jnp.zeros((8, 512), F32)
    for k in range(32):
        dx, dy, dz = lists[2, 0, k], lists[2, 1, k], lists[2, 2, k]
        inside = (dy == 0) & (dz >= -1) & (dz <= 1)
        window = ext_three[jnp.where(inside, dz + 1, 3), dx + 2]
        real = real + window * table_three[2 * k : 2 * k + 1, :]
        imag = imag + window * table_three[2 * k + 1 : 2 * k + 2, :]
    imag = pltpu.roll(imag, 4, 0)
    incoming = real + jnp.where(iota((8, 512), 0) < 4, -imag, imag)

    row = iota((64, 8), 0)
    apart = onehot(row // 16 * 2 + row // 2 % 2 == iota((64, 8), 1))
    spread = dot_right(apart, incoming)
    parts = []
    for c in range(2):
        for r in range(2):
            x, y = spread[16 * r : 16 * r + 16], spread[32 + 16 * r : 48 + 16 * r]
            parts.append(x * cosine_three + y * sine_three if c == 0 else y * cosine_three - x * sine_three)
    level_two = field_two + dot3(jnp.concatenate(parts, axis=0), up_three, ((1,), (1,)))
    columns = level_two.T
    spread = [dot_left(columns[:, 16 * i : 16 * i + 16], parent) for i in range(4)]
    real = jnp.concatenate([spread[r] * cosine_two + spread[2 + r] * sine_two for r in range(2)], axis=1)
    imag = jnp.concatenate([spread[2 + r] * cosine_two - spread[r] * sine_two for r in range(2)], axis=1)
    pad = jnp.zeros((32, 256), F32)
    level_one = []
    for c, value in enumerate((real, imag)):
        field = jnp.concatenate([field_one[64 * c + 32 * r : 64 * c + 32 * r + 32] for r in range(2)], axis=1)
        level_one.append(dot3(back_two, value) + jnp.concatenate([pad, field, pad], axis=0))
    high, low = split(jnp.concatenate(level_one, axis=0))

    x, z, core = me // 4, me // 2 % 2, me % 2
    sibling = {"dir": me + 1 - 2 * core}
    across = {"dir": me + 2 - 4 * z}
    others = [peers[4 * e] for e in range(1, 4)]
    to_core = [
        remote(partial.at[i, 1 - core], got_core.at[i], sum_send.at[i, 0], sum_receive.at[i, 0], sibling)
        for i in range(4)
    ]
    to_x = [
        [
            remote(
                held.at[i, lax.rem(x + e, 4)], got_x.at[i, 3 - e], sum_send.at[i, e], sum_receive.at[i, 4 - e],
                others[e - 1],
            )
            for e in range(1, 4)
        ]
        for i in range(4)
    ]
    to_z = [
        remote(held_x.at[i, 1 - z], got_z.at[i], sum_send.at[i, 4], sum_receive.at[i, 4], across)
        for i in range(4)
    ]

    def after_core(i):
        to_core[i].wait_recv()
        held[i] = partial[i, core] + got_core[i]
        for copy in to_x[i]:
            copy.start()

    for i in range(4):
        for o in (2 * i, 2 * i + 1):
            rows = slice(128 * o, 128 * o + 128)
            total = dot(far_high[rows], high) + (dot(far_high[rows], low) + dot(far_low[rows], high))
            for owner in range(16):
                partial[i, owner % 2, owner // 4, owner // 2 % 2, 8 * (o % 2) : 8 * (o % 2) + 8, :] = total[
                    8 * owner : 8 * owner + 8
                ]
        to_core[i].start()
        if i > 0:
            after_core(i - 1)
    after_core(3)
    for i in range(4):
        for copy in to_x[i]:
            copy.wait_recv()
        held_x[i] = held[i, x] + (got_x[i, 0] + got_x[i, 1] + got_x[i, 2])
        to_z[i].start()
    for e, copy in halo_copies:
        pl.when(has[e])(copy.wait_send)
    for i in range(4):
        to_core[i].wait_send()
        for copy in to_x[i]:
            copy.wait_send()
    far = []
    for i in range(4):
        to_z[i].wait_recv()
        far.append(held_x[i, z] + got_z[i])
    for i in range(4):
        to_z[i].wait_send()
    rows = []
    for r in range(2):
        for ox in range(2):
            pieces = [
                far[2 * ox + o // 2][8 * (o % 2) : 8 * (o % 2) + 8, 128 * r : 128 * r + 128] for o in range(4)
            ]
            rows.append(jnp.concatenate(pieces, axis=1))
    high, low = split(jnp.concatenate(rows, axis=0))
    both = dot(jnp.concatenate([high, low], axis=0), shuffle[...], ((1,), (1,)))
    far = both[:32] + both[32:]
    for r in range(2):
        for ox in range(2):
            for x in range(4):
                row = 8 * (2 * r + ox)
                out_ref[:, r, 2 * x + ox, :] = (
                    near[r, 2 * x + ox] + far[row : row + 8, 128 * x : 128 * x + 128]
                )


VMEM = pl.BlockSpec(memory_space=pltpu.VMEM)
SMEM = pl.BlockSpec(memory_space=pltpu.SMEM)
DMA = pltpu.SemaphoreType.DMA


def held_in(*dims, dtype=F32):
    return pltpu.VMEM(dims, dtype)


def shuffle_table():
    index = np.arange(512)
    x, y, z = index // 128, index // 16 % 8, index % 16
    target = 256 * (y % 2) + 128 * (z % 2) + 32 * x + 8 * (y // 2) + z // 2
    return (target[:, None] == index[None, :]).astype(np.float32)


def shards(
    source, near_blocks, near_mask, radiate, receive, theta_one, theta_two, theta_three, phi_taps,
    shift_one, shift_two, shift_three, trans_one, trans_two, trans_three, far_lists,
):
    dirs, boxes = lax.axis_size("dir"), lax.axis_size("box")
    layers = source.reshape(64, 2, 2, 4, 2, 128)
    layers = jnp.transpose(layers, (2, 4, 0, 1, 3, 5)).reshape(2, 2, 128, 512)
    args = (
        layers, near_blocks.reshape(216, 64), near_mask, radiate[:, :, 0], jnp.transpose(receive, (0, 1, 3, 2)),
        theta_one, theta_two, theta_two.T, theta_three.T, phi_taps,
        jnp.transpose(shift_one, (0, 2, 1)), jnp.transpose(shift_two, (0, 2, 1)),
        jnp.transpose(shift_three, (0, 2, 1)), jnp.transpose(trans_one, (1, 2, 3, 0)),
        jnp.transpose(trans_two, (0, 1, 3, 2)).reshape(64, 4, 32),
        jnp.transpose(trans_three, (0, 1, 3, 2)).reshape(64, 8, 64),
        jnp.transpose(far_lists, (0, 2, 1)), jnp.asarray(shuffle_table(), BF16),
    )
    specs = [VMEM] * len(args)
    specs[16] = SMEM
    out = pl.pallas_call(
        functools.partial(whole, dirs, boxes),
        out_shape=jax.ShapeDtypeStruct((8, 2, 8, 128), F32),
        in_specs=specs,
        out_specs=VMEM,
        scratch_shapes=[
            held_in(16, 128, dtype=BF16), held_in(16, 16, 128, dtype=BF16), held_in(2, 8, 128), held_in(2, 8, 128),
            held_in(2, 2, 128, 128, dtype=BF16), held_in(2, 64, 128), held_in(2, 16, 512), held_in(4, 8, 512),
            held_in(128, 128), held_in(16, 512), held_in(8, 512),
            held_in(1024, 256, dtype=BF16), held_in(192, 1024, dtype=BF16), held_in(192, 1024, dtype=BF16),
            held_in(1024, 192, dtype=BF16), held_in(1024, 192, dtype=BF16),
            held_in(2, 10, 216, 128), held_in(27, 8, 128), held_in(2, 8, 8, 128),
            held_in(2, 32, 128), held_in(64, 128), held_in(64, 512),
            held_in(5, 8, 8, 8, 128), held_in(25, 6, 8, 512), held_in(4, 5, 8, 512),
            held_in(4, 2, 4, 2, 16, 256), held_in(4, 4, 2, 16, 256), held_in(4, 4, 2, 16, 256),
            held_in(4, 3, 2, 16, 256), held_in(4, 2, 16, 256), held_in(4, 16, 256),
            DMA((16,)), DMA((16,)), DMA((2,)), DMA((2,)), DMA((2,)), DMA((2,)), DMA((8,)), DMA((8,)),
            DMA((4, 5)), DMA((4, 5)),
        ],
        compiler_params=pltpu.CompilerParams(
            collective_id=1, has_side_effects=True, vmem_limit_bytes=VMEM_LIMIT
        ),
    )(*args)
    return out.reshape(4, 2, 2, 8, 128)


def solution(mesh):
    placed = (
        P(None, None, None, "box", None),
        P(None, None, "dir", None),
        P(None, "box", None),
        P(None, None, "dir", None),
        P(None, None, None, "dir"),
        P(),
        P(),
        P(),
        P(),
        P(None, None, "dir"),
        P(None, None, "dir"),
        P(None, None, "dir"),
        P(None, None, None, "dir"),
        P(None, None, None, "dir"),
        P(None, None, None, "dir"),
        P(),
    )
    return jax.shard_map(
        shards,
        mesh=mesh,
        in_specs=placed,
        out_specs=P("dir", None, None, "box", None),
        check_vma=False,
    )
```

```python
import functools

import jax
import jax.numpy as jnp
import numpy as np
from jax import lax
from jax.experimental import pallas as pl
from jax.experimental.pallas import tpu as pltpu
from jax.sharding import PartitionSpec as P

MESH = pl.DeviceIdType.MESH
F32 = jnp.float32
BF16 = jnp.bfloat16
VMEM_LIMIT = 56 * 1024 * 1024
INPUTS = 17


def iota(shape, dim):
    return lax.broadcasted_iota(jnp.int32, shape, dim)


def split(a):
    high = a.astype(BF16)
    return high, (a - high.astype(F32)).astype(BF16)


def dot(a, b, dims=((1,), (0,))):
    return lax.dot_general(a, b, (dims, ((), ())), preferred_element_type=F32)


def dot3(a, b, dims=((1,), (0,))):
    a_high, a_low = split(a)
    b_high, b_low = split(b)
    return dot(a_high, b_high, dims) + (dot(a_high, b_low, dims) + dot(a_low, b_high, dims))


def dot_left(a, b, dims=((1,), (0,))):
    a_high, a_low = split(a)
    return dot(a_high, b, dims) + dot(a_low, b, dims)


def dot_right(a, b, dims=((1,), (0,))):
    b_high, b_low = split(b)
    return dot(a, b_high, dims) + dot(a, b_low, dims)


def onehot(condition):
    return jnp.where(condition, 1.0, 0.0).astype(BF16)


def interpolation(taps, level, theta, fine, coarse, wide, first, transposed):
    (fine_p, fine_t), (coarse_p, coarse_t) = fine, coarse
    if transposed:
        spread = onehot(iota((fine_t, fine_p * fine_t), 1) % fine_t == iota((fine_t, fine_p * fine_t), 0))
        tiled = jnp.concatenate([dot_left(theta, spread)] * coarse_p, axis=0)
        fine_dim, coarse_dim = 1, 0
    else:
        spread = onehot(
            iota((coarse_t, coarse_p * coarse_t), 1) % coarse_t == iota((coarse_t, coarse_p * coarse_t), 0)
        )
        tiled = jnp.concatenate([dot_left(theta, spread, ((0,), (0,)))] * fine_p, axis=0)
        fine_dim, coarse_dim = 0, 1
    p = iota(tiled.shape, fine_dim) // fine_t
    tap = iota(tiled.shape, coarse_dim) // coarse_t - first(p)
    even = wide(p) % 2 == 0
    weight = jnp.zeros(tiled.shape, F32)
    for j in range(3):
        value = jnp.where(even, taps[level, 0:1, j : j + 1], taps[level, 1:2, j : j + 1])
        weight = jnp.where(tap == j, value, weight)
    return weight * tiled


def turned(x):
    even = iota(x.shape, 1) % 2 == 0
    count = x.shape[1]
    return jnp.where(even, -pltpu.roll(x, count - 1, 1), pltpu.roll(x, 1, 1))


def child_of_box(index):
    return 4 * (index // 32 % 2) + 2 * (index // 8 % 2) + index % 2


def parent_of_box(index):
    return index // 64 * 8 + index // 16 % 2 * 4 + index // 2 % 4


def shifted_rows(block, shift, valid):
    moved = pltpu.roll(block, (-shift) % 8, 0) if shift % 8 else block
    return jnp.where(valid, moved, 0.0)


def cosines(angles):
    return jnp.concatenate([jnp.cos(angles), jnp.sin(angles)], axis=0)


def remote(source, target, send, receive, peer):
    return pltpu.make_async_remote_copy(
        src_ref=source, dst_ref=target, send_sem=send, recv_sem=receive, device_id=peer, device_id_type=MESH
    )


def whole(dirs, boxes, *refs):
    outside, out_ref, inside = refs[:INPUTS], refs[INPUTS], refs[INPUTS + 1 : 2 * INPUTS + 1]
    (
        leaf_rows, near_blocks, mask, radiate, receive, theta_one, theta_two, theta_three, taps,
        shift_one, shift_two, shift_three, trans_one, trans_two, trans_three, lists, shuffle,
    ) = inside
    (
        in_sem, wide_rows, source, message, gathered, rim_out, rims, leaf_halo, halo_one, halo_two, halo_three,
        one, two, three, leaf, shape_high, shape_low, far_high, far_low, products, rolled, near,
        table_one, table_two, table_three, ext_one, ext_two, ext_three,
        partial, got_core, held, got_x, held_x, got_z,
        send, receive_sem, rim_send, rim_receive, leaf_send, leaf_receive, halo_send, halo_receive,
        sum_send, sum_receive,
    ) = refs[2 * INPUTS + 1 :]
    me, box = lax.axis_index("dir"), lax.axis_index("box")
    has = {-1: box > 0, 1: box < boxes - 1, -2: box > 1, 2: box < boxes - 2}
    beside = {e: {"box": lax.rem(box + boxes + e, boxes)} for e in has}
    peers = {e: {"dir": lax.rem(me + e, dirs)} for e in range(1, dirs)}

    barrier = pltpu.get_barrier_semaphore()
    count = dirs - 1
    for e in range(1, dirs):
        pl.semaphore_signal(barrier, inc=1, device_id=peers[e], device_id_type=MESH)
    for e in has:
        @pl.when(has[e])
        def _(e=e):
            pl.semaphore_signal(barrier, inc=1, device_id=beside[e], device_id_type=MESH)

        count = count + jnp.where(has[e], 1, 0)

    loads = [pltpu.make_async_copy(outside[i], inside[i], in_sem.at[i]) for i in range(INPUTS)]
    early = (3, 4, 9, 10)
    for i in early:
        loads[i].start()
    for i in range(INPUTS):
        if i not in early:
            loads[i].start()
    for i in early:
        loads[i].wait()

    taken = [receive[c, :, u, :].astype(F32) for c in range(2) for u in range(4)]
    lane = iota((64, 128), 1)
    sent = [dot(radiate[c], onehot(lane == 2 * iota((64, 128), 0) + c)) for c in range(2)]
    tile = jnp.concatenate([jnp.concatenate(taken, axis=1), sent[0] + sent[1]], axis=0).astype(BF16)
    message[...] = tile
    gathered[0] = tile
    angles_one = jnp.concatenate([shift_one[:, a, :] for a in range(2)], axis=1)
    angles_two = jnp.concatenate([shift_two[:, a, :] for a in range(4)], axis=1)
    pad = jnp.zeros((8, 64), F32)
    rim_out[0] = jnp.concatenate([angles_one, angles_two[:, 96:], pad], axis=1)
    rim_out[1] = jnp.concatenate([angles_one, angles_two[:, :32], pad], axis=1)

    for i in range(INPUTS):
        if i not in early:
            loads[i].wait()
    up_one = interpolation(
        taps, 0, theta_one[...], (6, 16), (5, 8), lambda p: p, lambda p: p // 2, False
    )
    up_two = interpolation(
        taps, 1, theta_two[...], (6, 32), (6, 16), lambda p: p + 1, lambda p: (p + 1) // 2, False
    )
    back_two = interpolation(
        taps, 1, theta_two[...], (6, 32), (6, 16), lambda p: p + 1, lambda p: (p + 1) // 2, True
    )
    up_three = interpolation(
        taps, 2, theta_three[...], (8, 64), (6, 32), lambda p: p, lambda p: p // 2, True
    )
    wide_rows[...] = leaf_rows[...].astype(F32)
    for r in range(2):
        for x in range(8):
            layer = wide_rows[pl.ds(8 * r + x, 128, stride=16), :].astype(BF16)
            source[r, x % 2, :, 128 * (x // 2) : 128 * (x // 2) + 128] = layer
    for r in range(2):
        for ox in range(2):
            mixed = dot(source[r, ox], shuffle[...]).astype(BF16)
            for o in range(4):
                row = 128 * (4 * ox + o)
                leaf[row : row + 128, 128 * r : 128 * r + 128] = mixed[:, 128 * o : 128 * o + 128]
    for a in range(8):
        table_three[:, 64 * a : 64 * a + 64] = trans_three[:, a, :]
    for a in range(4):
        table_two[:, 32 * a : 32 * a + 32] = trans_two[:, a, :]
    for c in range(2):
        total = jnp.zeros((32, 128), F32)
        for a in range(2):
            place = onehot(iota((16, 128), 1) % 32 == 16 * a + iota((16, 128), 0))
            total = total + dot_left(trans_one[c, :, a, :], place, ((0,), (0,)))
        table_one[c] = total
    zero = jnp.zeros((8, 128), F32)
    for shift in range(5):
        for x in range(8):
            for y in (0, 1, 6, 7):
                ext_one[shift, x, y] = zero
    zero = jnp.zeros((8, 512), F32)
    for x in range(6):
        for shift in range(5):
            ext_two[shift, x] = zero
            ext_two[20 + shift, x] = zero
    for x in range(5):
        ext_three[3, x] = zero
    for side, e in enumerate((-1, 1)):
        @pl.when(jnp.logical_not(has[e]))
        def _(side=side):
            leaf_halo[side] = jnp.zeros((2, 128, 128), BF16)
            halo_one[side] = jnp.zeros((64, 128), F32)
            halo_two[side] = jnp.zeros((16, 512), F32)
    for slot, e in enumerate((-2, -1, 1, 2)):
        @pl.when(jnp.logical_not(has[e]))
        def _(slot=slot):
            halo_three[slot] = jnp.zeros((8, 512), F32)

    pl.semaphore_wait(barrier, count)
    table_copies = [
        remote(rim_out.at[0], rims.at[0], rim_send.at[0], rim_receive.at[0], peers[1]),
        remote(rim_out.at[1], rims.at[1], rim_send.at[1], rim_receive.at[1], peers[dirs - 1]),
    ]
    for e in range(1, dirs):
        table_copies.append(
            remote(message, gathered.at[dirs - e], send.at[e], receive_sem.at[dirs - e], peers[e])
        )
    for copy in table_copies:
        copy.start()
    leaf_copies = [
        (1, remote(
            source.at[:, 1, :, pl.ds(384, 128)], leaf_halo.at[0], leaf_send.at[0], leaf_receive.at[0], beside[1]
        )),
        (-1, remote(
            source.at[:, 0, :, pl.ds(0, 128)], leaf_halo.at[1], leaf_send.at[1], leaf_receive.at[1], beside[-1]
        )),
    ]
    for e, copy in leaf_copies:
        pl.when(has[e])(copy.start)

    lane = iota((64, 128), 1)
    double = dot(near_blocks[...], onehot(lane // 2 == iota((64, 128), 0))).astype(BF16)
    row, column = iota((216, 216), 0), iota((216, 216), 1)
    same = 8 * (row // 8) + 4 * (row % 2) + row % 8 // 2
    other = 8 * (row // 8) + 4 * (1 - row % 2) + row % 8 // 2
    kept = dot(onehot(column == same), double)
    crossed = dot(onehot(column == other), double)
    crossed = jnp.where(iota((216, 128), 0) % 2 == 0, -crossed, crossed)
    blocks = jnp.where(iota((216, 128), 1) % 2 == 0, kept, crossed).astype(BF16)
    lane = iota((8, 128), 1)
    for k in range(27):
        dy, dz = k // 3 % 3 - 1, k % 3 - 1
        y, z = lane // 16 + dy, lane % 16 + dz
        valid = (y >= 0) & (y < 8) & (z >= 0) & (z < 16)
        values = jnp.where(valid, mask[k].astype(F32), 0.0)
        rolled[k] = pltpu.roll(values, (16 * dy + dz) % 128, 1)
    for r in range(2):
        for ox in range(2):
            layers = dot(blocks, source[r, ox])
            for x in range(4):
                products[r, 1 + 2 * x + ox] = layers[:, 128 * x : 128 * x + 128]
    for e, copy in leaf_copies:
        pl.when(has[e])(copy.wait_send)
        pl.when(has[-e])(copy.wait_recv)
    for r in range(2):
        for side in range(2):
            products[r, 9 * side] = dot(blocks, leaf_halo[side, r])
    for r in range(2):
        for x in range(8):
            total = jnp.zeros((8, 128), F32)
            for inner in range(9):
                dy, dz = inner // 3 - 1, inner % 3 - 1
                term = jnp.zeros((8, 128), F32)
                for dx in range(3):
                    k = 9 * dx + inner
                    term = term + products[r, x + dx, 8 * k : 8 * k + 8, :] * rolled[k, x : x + 1, :]
                total = total + pltpu.roll(term, (-16 * dy - dz) % 128, 1)
            near[r, x] = total

    for copy in table_copies:
        copy.wait_send()
    for copy in table_copies:
        copy.wait_recv()
    pad = jnp.zeros((8, 32), F32)
    angles = jnp.concatenate([rims[0, :, 0:32], angles_one, rims[1, :, 0:32], pad], axis=1)
    turns = cosines(angles).T
    tables = gathered[...].astype(F32)
    sources = jnp.concatenate([tables[(a - 2) % 16, 8:16] for a in range(5)], axis=0)
    send_real = dot_left(up_one, sources.astype(BF16))
    send_turned = turned(send_real)
    even = iota((96, 128), 1) % 2 == 0
    for o in range(8):
        moved = turns[:96, o : o + 1] * send_real + turns[:96, 8 + o : 9 + o] * send_turned
        swapped = jnp.where(even, pltpu.roll(moved, 127, 1), pltpu.roll(moved, 1, 1))
        rows = jnp.concatenate([jnp.where(even, moved, -moved), swapped], axis=0)
        high, low = split(rows)
        shape_high[:, 128 * o : 128 * o + 128] = high
        shape_low[:, 128 * o : 128 * o + 128] = low
    level_one = dot(shape_high[...], leaf[...]) + dot(shape_low[...], leaf[...])
    own = jnp.concatenate(
        [level_one[96 * c + 32 : 96 * c + 64, 128 * r : 128 * r + 128] for c in range(2) for r in range(2)],
        axis=0,
    )
    one[...] = own.T
    halo_copies = [
        (e, remote(origin, target, halo_send.at[i], halo_receive.at[i], beside[e]))
        for i, (e, origin, target) in enumerate([
            (1, one.at[pl.ds(64, 64)], halo_one.at[0]),
            (-1, one.at[pl.ds(0, 64)], halo_one.at[1]),
            (1, two, halo_two.at[0]),
            (-1, two, halo_two.at[1]),
            (2, three, halo_three.at[0]),
            (1, three, halo_three.at[1]),
            (-1, three, halo_three.at[2]),
            (-2, three, halo_three.at[3]),
        ])
    ]
    for e, copy in halo_copies[:2]:
        pl.when(has[e])(copy.start)

    pad = jnp.zeros((8, 64), F32)
    angles = jnp.concatenate([rims[0, :, 32:64], angles_two, rims[1, :, 32:64], pad], axis=1)
    lane = iota((16, 256), 1)
    kind = child_of_box(lane % 128) + 8 * (lane // 128)
    phases = dot_left(cosines(angles).T[:192], onehot(iota((16, 256), 0) == kind))
    cosine_two, sine_two = phases[:, :128], phases[:, 128:]
    parent = onehot(parent_of_box(iota((16, 128), 1)) == iota((16, 128), 0))
    real = dot3(up_two, level_one[:96])
    imag = dot3(up_two, level_one[96:])
    parts = []
    for c in range(2):
        for r in range(2):
            x, y = real[:, 128 * r : 128 * r + 128], imag[:, 128 * r : 128 * r + 128]
            value = x * cosine_two - y * sine_two if c == 0 else y * cosine_two + x * sine_two
            parts.append(dot_right(parent, value, ((1,), (1,))))
    for index in range(4):
        two[:, 128 * index : 128 * index + 128] = parts[index][:, 32:160]
    for e, copy in halo_copies[2:4]:
        pl.when(has[e])(copy.start)
    level_two = jnp.concatenate(parts, axis=0)
    upper = dot3(level_two, up_three)
    turns_three = cosines(jnp.concatenate([shift_three[:, a, :] for a in range(8)], axis=1))
    row, column = iota((16, 8), 0), iota((16, 8), 1)
    expand = onehot(column == 4 * (row // 8) + 2 * (row // 4 % 2) + row % 2)
    cosine_three = dot_right(expand, turns_three[:8])
    sine_three = dot_right(expand, turns_three[8:])
    parts = []
    for c in range(2):
        for r in range(2):
            x, y = upper[16 * r : 16 * r + 16], upper[32 + 16 * r : 48 + 16 * r]
            parts.append(x * cosine_three - y * sine_three if c == 0 else y * cosine_three + x * sine_three)
    row = iota((8, 64), 1)
    together = onehot(row // 16 * 2 + row // 2 % 2 == iota((8, 64), 0))
    three[...] = dot_right(together, jnp.concatenate(parts, axis=0))
    for e, copy in halo_copies[4:]:
        pl.when(has[e])(copy.start)

    stacked = jnp.concatenate([tables[e, 0:8] for e in range(16)], axis=0)
    row, lane = iota((128, 640), 0), iota((128, 640), 1)
    azimuth = (me + 14 + lane // 128) % 16
    pick = onehot(row == 64 * (lane % 2) + 16 * (lane % 8 // 2) + azimuth)
    sender = (row // 8 + me) % 16
    placed = jnp.where(lane % 128 // 8 == sender, dot(stacked.astype(BF16), pick), 0.0)
    summed = placed[0:8]
    for e in range(1, 16):
        summed = summed + placed[8 * e : 8 * e + 8]
    targets = jnp.concatenate([summed[:, 128 * a : 128 * a + 128] for a in range(5)], axis=0)
    take_real = dot_left(up_one, targets.astype(BF16))
    take_turned = turned(take_real)
    for o in range(8):
        moved = turns[:96, o : o + 1] * take_real - turns[:96, 8 + o : 9 + o] * take_turned
        columns = jnp.concatenate([moved, turned(moved)], axis=0)
        high, low = split(columns.T)
        far_high[128 * o : 128 * o + 128, :] = high
        far_low[128 * o : 128 * o + 128, :] = low

    for e, copy in halo_copies[:2]:
        pl.when(has[-e])(copy.wait_recv)
    z = iota((8, 128), 0)
    for shift in range(5):
        dz = shift - 2
        valid = (z + dz >= 0) & (z + dz < 8)
        for x in range(8):
            for y in range(4):
                row = 8 * y + 32 * (x % 2)
                if x < 2 or x > 5:
                    block = halo_one[x // 4, row : row + 8, :]
                else:
                    block = one[32 * (x - 2) + 8 * y : 32 * (x - 2) + 8 * y + 8, :]
                ext_one[shift, x, y + 2] = shifted_rows(block, dz, valid)
    real = jnp.zeros((4, 4, 8, 128), F32)
    imag = jnp.zeros((4, 4, 8, 128), F32)
    for k in range(32):
        dx, dy, dz = lists[0, 0, k], lists[0, 1, k], lists[0, 2, k]
        window = ext_one[dz + 2, pl.ds(dx + 2, 4), pl.ds(dy + 2, 4)]
        real = real + window * table_one[0, k : k + 1, :]
        imag = imag + window * table_one[1, k : k + 1, :]
    imag = imag.reshape(128, 128)
    turned_imag = pltpu.roll(imag, 64, 1)
    field = real.reshape(128, 128) + jnp.where(iota((128, 128), 1) < 64, -turned_imag, turned_imag)
    field_one = field.T
    for e, copy in halo_copies[2:4]:
        pl.when(has[-e])(copy.wait_recv)
    y, z = iota((8, 512), 0) // 4, iota((8, 512), 0) % 4
    for shift in range(5, 20):
        dy, dz = shift // 5 - 2, shift % 5 - 2
        valid = (y + dy >= 0) & (y + dy < 2) & (z + dz >= 0) & (z + dz < 4)
        for x in range(6):
            row = 8 * (x % 2)
            if x < 2 or x > 3:
                block = halo_two[x // 3, row : row + 8, :]
            else:
                block = two[row : row + 8, :]
            ext_two[shift, x] = shifted_rows(block, 4 * dy + dz, valid)
    reals = [jnp.zeros((2, 8, 128), F32) for _ in range(4)]
    for k in range(32):
        dx, dy, dz = lists[1, 0, k], lists[1, 1, k], lists[1, 2, k]
        window = ext_two[5 * dy + dz + 12, pl.ds(dx + 2, 2)]
        x = table_two[2 * k : 2 * k + 1, :]
        y = table_two[2 * k + 1 : 2 * k + 2, :]
        parts = [window[:, :, 128 * i : 128 * i + 128] for i in range(4)]
        for r in range(2):
            reals[r] = reals[r] + (x * parts[r] - y * parts[2 + r])
            reals[2 + r] = reals[2 + r] + (x * parts[2 + r] + y * parts[r])
    side = jnp.zeros((64, 32), F32)
    field_two = jnp.concatenate([side, jnp.concatenate(reals, axis=0).reshape(64, 128), side], axis=1)
    for e, copy in halo_copies[4:]:
        pl.when(has[-e])(copy.wait_recv)
    z = iota((8, 512), 0) % 2
    for x in range(5):
        block = three[...] if x == 2 else halo_three[x - x // 3]
        for shift in range(3):
            dz = shift - 1
            ext_three[shift, x] = shifted_rows(block, dz, (z + dz >= 0) & (z + dz < 2))
    real = jnp.zeros((8, 512), F32)
    imag = jnp.zeros((8, 512), F32)
    for k in range(32):
        dx, dy, dz = lists[2, 0, k], lists[2, 1, k], lists[2, 2, k]
        inside = (dy == 0) & (dz >= -1) & (dz <= 1)
        window = ext_three[jnp.where(inside, dz + 1, 3), dx + 2]
        real = real + window * table_three[2 * k : 2 * k + 1, :]
        imag = imag + window * table_three[2 * k + 1 : 2 * k + 2, :]
    imag = pltpu.roll(imag, 4, 0)
    incoming = real + jnp.where(iota((8, 512), 0) < 4, -imag, imag)

    row = iota((64, 8), 0)
    apart = onehot(row // 16 * 2 + row // 2 % 2 == iota((64, 8), 1))
    spread = dot_right(apart, incoming)
    parts = []
    for c in range(2):
        for r in range(2):
            x, y = spread[16 * r : 16 * r + 16], spread[32 + 16 * r : 48 + 16 * r]
            parts.append(x * cosine_three + y * sine_three if c == 0 else y * cosine_three - x * sine_three)
    level_two = field_two + dot3(jnp.concatenate(parts, axis=0), up_three, ((1,), (1,)))
    columns = level_two.T
    spread = [dot_left(columns[:, 16 * i : 16 * i + 16], parent) for i in range(4)]
    real = jnp.concatenate([spread[r] * cosine_two + spread[2 + r] * sine_two for r in range(2)], axis=1)
    imag = jnp.concatenate([spread[2 + r] * cosine_two - spread[r] * sine_two for r in range(2)], axis=1)
    pad = jnp.zeros((32, 256), F32)
    level_one = []
    for c, value in enumerate((real, imag)):
        field = jnp.concatenate([field_one[64 * c + 32 * r : 64 * c + 32 * r + 32] for r in range(2)], axis=1)
        level_one.append(dot3(back_two, value) + jnp.concatenate([pad, field, pad], axis=0))
    high, low = split(jnp.concatenate(level_one, axis=0))

    x, z, core = me // 4, me // 2 % 2, me % 2
    sibling = {"dir": me + 1 - 2 * core}
    across = {"dir": me + 2 - 4 * z}
    others = [peers[4 * e] for e in range(1, 4)]
    to_core = [
        remote(partial.at[i, 1 - core], got_core.at[i], sum_send.at[i, 0], sum_receive.at[i, 0], sibling)
        for i in range(4)
    ]
    to_x = [
        [
            remote(
                held.at[i, lax.rem(x + e, 4)], got_x.at[i, 3 - e], sum_send.at[i, e], sum_receive.at[i, 4 - e],
                others[e - 1],
            )
            for e in range(1, 4)
        ]
        for i in range(4)
    ]
    to_z = [
        remote(held_x.at[i, 1 - z], got_z.at[i], sum_send.at[i, 4], sum_receive.at[i, 4], across)
        for i in range(4)
    ]

    def after_core(i):
        to_core[i].wait_recv()
        held[i] = partial[i, core] + got_core[i]
        for copy in to_x[i]:
            copy.start()

    for i in range(4):
        for o in (2 * i, 2 * i + 1):
            rows = slice(128 * o, 128 * o + 128)
            total = dot(far_high[rows], high) + (dot(far_high[rows], low) + dot(far_low[rows], high))
            for owner in range(16):
                partial[i, owner % 2, owner // 4, owner // 2 % 2, 8 * (o % 2) : 8 * (o % 2) + 8, :] = total[
                    8 * owner : 8 * owner + 8
                ]
        to_core[i].start()
        if i > 0:
            after_core(i - 1)
    after_core(3)
    for i in range(4):
        for copy in to_x[i]:
            copy.wait_recv()
        held_x[i] = held[i, x] + (got_x[i, 0] + got_x[i, 1] + got_x[i, 2])
        to_z[i].start()
    for e, copy in halo_copies:
        pl.when(has[e])(copy.wait_send)
    for i in range(4):
        to_core[i].wait_send()
        for copy in to_x[i]:
            copy.wait_send()
    far = []
    for i in range(4):
        to_z[i].wait_recv()
        far.append(held_x[i, z] + got_z[i])
    for i in range(4):
        to_z[i].wait_send()
    rows = []
    for r in range(2):
        for ox in range(2):
            pieces = [
                far[2 * ox + o // 2][8 * (o % 2) : 8 * (o % 2) + 8, 128 * r : 128 * r + 128] for o in range(4)
            ]
            rows.append(jnp.concatenate(pieces, axis=1))
    high, low = split(jnp.concatenate(rows, axis=0))
    both = dot(jnp.concatenate([high, low], axis=0), shuffle[...], ((1,), (1,)))
    far = both[:32] + both[32:]
    for r in range(2):
        for ox in range(2):
            for x in range(4):
                row = 8 * (2 * r + ox)
                out_ref[:, r, 2 * x + ox, :] = (
                    near[r, 2 * x + ox] + far[row : row + 8, 128 * x : 128 * x + 128]
                )


VMEM = pl.BlockSpec(memory_space=pltpu.VMEM)
HBM = pl.BlockSpec(memory_space=pltpu.HBM)
DMA = pltpu.SemaphoreType.DMA


def held_in(*dims, dtype=F32):
    return pltpu.VMEM(dims, dtype)


def shuffle_table():
    index = np.arange(512)
    x, y, z = index // 128, index // 16 % 8, index % 16
    target = 256 * (y % 2) + 128 * (z % 2) + 32 * x + 8 * (y // 2) + z // 2
    return (target[:, None] == index[None, :]).astype(np.float32)


def shards(
    source, near_blocks, near_mask, radiate, receive, theta_one, theta_two, theta_three, phi_taps,
    shift_one, shift_two, shift_three, trans_one, trans_two, trans_three, far_lists,
):
    dirs, boxes = lax.axis_size("dir"), lax.axis_size("box")
    args = (
        source.reshape(2048, 128), near_blocks.reshape(216, 64), near_mask, radiate[:, :, 0], jnp.transpose(receive, (0, 1, 3, 2)),
        theta_one.T, theta_two.T, theta_three.T, phi_taps,
        jnp.transpose(shift_one, (0, 2, 1)), jnp.transpose(shift_two, (0, 2, 1)),
        jnp.transpose(shift_three, (0, 2, 1)), jnp.transpose(trans_one, (1, 2, 3, 0)),
        jnp.transpose(trans_two, (0, 1, 3, 2)).reshape(64, 4, 32),
        jnp.transpose(trans_three, (0, 1, 3, 2)).reshape(64, 8, 64),
        jnp.transpose(far_lists, (0, 2, 1)), jnp.asarray(shuffle_table(), BF16),
    )
    copies = [pltpu.VMEM(a.shape, a.dtype) for a in args]
    copies[15] = pltpu.SMEM(args[15].shape, args[15].dtype)
    out = pl.pallas_call(
        functools.partial(whole, dirs, boxes),
        out_shape=jax.ShapeDtypeStruct((8, 2, 8, 128), F32),
        in_specs=[HBM] * INPUTS,
        out_specs=VMEM,
        scratch_shapes=copies
        + [
            DMA((INPUTS,)), held_in(2048, 128), held_in(2, 2, 128, 512, dtype=BF16),
            held_in(16, 128, dtype=BF16), held_in(16, 16, 128, dtype=BF16), held_in(2, 8, 128), held_in(2, 8, 128),
            held_in(2, 2, 128, 128, dtype=BF16), held_in(2, 64, 128), held_in(2, 16, 512), held_in(4, 8, 512),
            held_in(128, 128), held_in(16, 512), held_in(8, 512),
            held_in(1024, 256, dtype=BF16), held_in(192, 1024, dtype=BF16), held_in(192, 1024, dtype=BF16),
            held_in(1024, 192, dtype=BF16), held_in(1024, 192, dtype=BF16),
            held_in(2, 10, 216, 128), held_in(27, 8, 128), held_in(2, 8, 8, 128),
            held_in(2, 32, 128), held_in(64, 128), held_in(64, 512),
            held_in(5, 8, 8, 8, 128), held_in(25, 6, 8, 512), held_in(4, 5, 8, 512),
            held_in(4, 2, 4, 2, 16, 256), held_in(4, 4, 2, 16, 256), held_in(4, 4, 2, 16, 256),
            held_in(4, 3, 2, 16, 256), held_in(4, 2, 16, 256), held_in(4, 16, 256),
            DMA((16,)), DMA((16,)), DMA((2,)), DMA((2,)), DMA((2,)), DMA((2,)), DMA((8,)), DMA((8,)),
            DMA((4, 5)), DMA((4, 5)),
        ],
        compiler_params=pltpu.CompilerParams(
            collective_id=1, has_side_effects=True, vmem_limit_bytes=VMEM_LIMIT
        ),
    )(*args)
    return out.reshape(4, 2, 2, 8, 128)


def solution(mesh):
    placed = (
        P(None, None, None, "box", None),
        P(None, None, "dir", None),
        P(None, "box", None),
        P(None, None, "dir", None),
        P(None, None, None, "dir"),
        P(),
        P(),
        P(),
        P(),
        P(None, None, "dir"),
        P(None, None, "dir"),
        P(None, None, "dir"),
        P(None, None, None, "dir"),
        P(None, None, None, "dir"),
        P(None, None, None, "dir"),
        P(),
    )
    return jax.shard_map(
        shards,
        mesh=mesh,
        in_specs=placed,
        out_specs=P("dir", None, None, "box", None),
        check_vma=False,
    )
```

```python
import functools

import jax
import jax.numpy as jnp
import numpy as np
from jax import lax
from jax.experimental import pallas as pl
from jax.experimental.pallas import tpu as pltpu
from jax.sharding import PartitionSpec as P

MESH = pl.DeviceIdType.MESH
F32 = jnp.float32
BF16 = jnp.bfloat16
VMEM_LIMIT = 56 * 1024 * 1024
INPUTS = 17


def iota(shape, dim):
    return lax.broadcasted_iota(jnp.int32, shape, dim)


def split(a):
    high = a.astype(BF16)
    return high, (a - high.astype(F32)).astype(BF16)


def dot(a, b, dims=((1,), (0,))):
    return lax.dot_general(a, b, (dims, ((), ())), preferred_element_type=F32)


def dot3(a, b, dims=((1,), (0,))):
    a_high, a_low = split(a)
    b_high, b_low = split(b)
    return dot(a_high, b_high, dims) + (dot(a_high, b_low, dims) + dot(a_low, b_high, dims))


def dot_left(a, b, dims=((1,), (0,))):
    a_high, a_low = split(a)
    return dot(a_high, b, dims) + dot(a_low, b, dims)


def dot_right(a, b, dims=((1,), (0,))):
    b_high, b_low = split(b)
    return dot(a, b_high, dims) + dot(a, b_low, dims)


def onehot(condition):
    return jnp.where(condition, 1.0, 0.0).astype(BF16)


def interpolation(taps, level, theta, fine, coarse, wide, first, transposed):
    (fine_p, fine_t), (coarse_p, coarse_t) = fine, coarse
    if transposed:
        spread = onehot(iota((fine_t, fine_p * fine_t), 1) % fine_t == iota((fine_t, fine_p * fine_t), 0))
        tiled = jnp.concatenate([dot_left(theta, spread)] * coarse_p, axis=0)
        fine_dim, coarse_dim = 1, 0
    else:
        spread = onehot(
            iota((coarse_t, coarse_p * coarse_t), 1) % coarse_t == iota((coarse_t, coarse_p * coarse_t), 0)
        )
        tiled = jnp.concatenate([dot_left(theta, spread, ((0,), (0,)))] * fine_p, axis=0)
        fine_dim, coarse_dim = 0, 1
    p = iota(tiled.shape, fine_dim) // fine_t
    tap = iota(tiled.shape, coarse_dim) // coarse_t - first(p)
    even = wide(p) % 2 == 0
    weight = jnp.zeros(tiled.shape, F32)
    for j in range(3):
        value = jnp.where(even, taps[level, 0:1, j : j + 1], taps[level, 1:2, j : j + 1])
        weight = jnp.where(tap == j, value, weight)
    return weight * tiled


def turned(x):
    even = iota(x.shape, 1) % 2 == 0
    count = x.shape[1]
    return jnp.where(even, -pltpu.roll(x, count - 1, 1), pltpu.roll(x, 1, 1))


def child_of_box(index):
    return 4 * (index // 32 % 2) + 2 * (index // 8 % 2) + index % 2


def parent_of_box(index):
    return index // 64 * 8 + index // 16 % 2 * 4 + index // 2 % 4


def shifted_rows(block, shift, valid):
    moved = pltpu.roll(block, (-shift) % 8, 0) if shift % 8 else block
    return jnp.where(valid, moved, 0.0)


def cosines(angles):
    return jnp.concatenate([jnp.cos(angles), jnp.sin(angles)], axis=0)


def remote(source, target, send, receive, peer):
    return pltpu.make_async_remote_copy(
        src_ref=source, dst_ref=target, send_sem=send, recv_sem=receive, device_id=peer, device_id_type=MESH
    )


def whole(dirs, boxes, *refs):
    outside, out_ref, inside = refs[:INPUTS], refs[INPUTS], refs[INPUTS + 1 : 2 * INPUTS + 1]
    (
        leaf_rows, near_blocks, mask, radiate, receive, theta_one, theta_two, theta_three, taps,
        shift_one, shift_two, shift_three, trans_one, trans_two, trans_three, lists, shuffle,
    ) = inside
    (
        in_sem, wide_rows, source, message, gathered, rim_out, rims, leaf_halo, halo_one, halo_two, halo_three,
        one, two, three, leaf, shape_high, shape_low, far_high, far_low, products, rolled, near,
        table_one, table_two, table_three, ext_one, ext_two, ext_three,
        partial, got_core, held, coded, got_coded,
        send, receive_sem, rim_send, rim_receive, leaf_send, leaf_receive, halo_send, halo_receive,
        sum_send, sum_receive,
    ) = refs[2 * INPUTS + 1 :]
    me, box = lax.axis_index("dir"), lax.axis_index("box")
    has = {-1: box > 0, 1: box < boxes - 1, -2: box > 1, 2: box < boxes - 2}
    beside = {e: {"box": lax.rem(box + boxes + e, boxes)} for e in has}
    place_x, place_z, core = me // 4, me // 2 % 2, me % 2
    places = [(dx, dz, dc) for dz in (1, 0) for dx in (2, 1, 3, 0) for dc in (1, 0)][: dirs - 1]
    number = {p: 4 * lax.rem(place_x + p[0], 4) + 2 * ((place_z + p[1]) % 2) + (core + p[2]) % 2 for p in places}
    peers = {p: {"dir": number[p]} for p in places}
    slot = {p: 4 * p[0] + 2 * p[1] + p[2] for p in places}
    back = {p: slot[((4 - p[0]) % 4, p[1], p[2])] for p in places}
    after, before = {"dir": lax.rem(me + 1, dirs)}, {"dir": lax.rem(me + dirs - 1, dirs)}

    barrier = pltpu.get_barrier_semaphore()
    count = dirs - 1
    for p in places:
        pl.semaphore_signal(barrier, inc=1, device_id=peers[p], device_id_type=MESH)
    for e in has:
        @pl.when(has[e])
        def _(e=e):
            pl.semaphore_signal(barrier, inc=1, device_id=beside[e], device_id_type=MESH)

        count = count + jnp.where(has[e], 1, 0)

    loads = [pltpu.make_async_copy(outside[i], inside[i], in_sem.at[i]) for i in range(INPUTS)]
    early = (3, 4, 9, 10)
    for i in early:
        loads[i].start()
    for i in range(INPUTS):
        if i not in early:
            loads[i].start()
    for i in early:
        loads[i].wait()

    taken = [receive[c, :, u, :].astype(F32) for c in range(2) for u in range(4)]
    lane = iota((64, 128), 1)
    sent = [dot(radiate[c], onehot(lane == 2 * iota((64, 128), 0) + c)) for c in range(2)]
    tile = jnp.concatenate([jnp.concatenate(taken, axis=1), sent[0] + sent[1]], axis=0).astype(BF16)
    message[...] = tile
    gathered[0] = tile
    angles_one = jnp.concatenate([shift_one[:, a, :] for a in range(2)], axis=1)
    angles_two = jnp.concatenate([shift_two[:, a, :] for a in range(4)], axis=1)
    pad = jnp.zeros((8, 64), F32)
    rim_out[0] = jnp.concatenate([angles_one, angles_two[:, 96:], pad], axis=1)
    rim_out[1] = jnp.concatenate([angles_one, angles_two[:, :32], pad], axis=1)

    for i in range(INPUTS):
        if i not in early:
            loads[i].wait()
    up_one = interpolation(
        taps, 0, theta_one[...], (6, 16), (5, 8), lambda p: p, lambda p: p // 2, False
    )
    up_two = interpolation(
        taps, 1, theta_two[...], (6, 32), (6, 16), lambda p: p + 1, lambda p: (p + 1) // 2, False
    )
    back_two = interpolation(
        taps, 1, theta_two[...], (6, 32), (6, 16), lambda p: p + 1, lambda p: (p + 1) // 2, True
    )
    up_three = interpolation(
        taps, 2, theta_three[...], (8, 64), (6, 32), lambda p: p, lambda p: p // 2, True
    )
    wide_rows[...] = leaf_rows[...].astype(F32)
    for r in range(2):
        for x in range(8):
            layer = wide_rows[pl.ds(8 * r + x, 128, stride=16), :].astype(BF16)
            source[r, x % 2, :, 128 * (x // 2) : 128 * (x // 2) + 128] = layer
    for r in range(2):
        for ox in range(2):
            mixed = dot(source[r, ox], shuffle[...]).astype(BF16)
            for o in range(4):
                row = 128 * (4 * ox + o)
                leaf[row : row + 128, 128 * r : 128 * r + 128] = mixed[:, 128 * o : 128 * o + 128]
    for a in range(8):
        table_three[:, 64 * a : 64 * a + 64] = trans_three[:, a, :]
    for a in range(4):
        table_two[:, 32 * a : 32 * a + 32] = trans_two[:, a, :]
    for c in range(2):
        total = jnp.zeros((32, 128), F32)
        for a in range(2):
            place = onehot(iota((16, 128), 1) % 32 == 16 * a + iota((16, 128), 0))
            total = total + dot_left(trans_one[c, :, a, :], place, ((0,), (0,)))
        table_one[c] = total
    zero = jnp.zeros((8, 128), F32)
    for shift in range(5):
        for x in range(8):
            for y in (0, 1, 6, 7):
                ext_one[shift, x, y] = zero
    zero = jnp.zeros((8, 512), F32)
    for x in range(6):
        for shift in range(5):
            ext_two[shift, x] = zero
            ext_two[20 + shift, x] = zero
    for x in range(5):
        ext_three[3, x] = zero
    for side, e in enumerate((-1, 1)):
        @pl.when(jnp.logical_not(has[e]))
        def _(side=side):
            leaf_halo[side] = jnp.zeros((2, 128, 128), BF16)
            halo_one[side] = jnp.zeros((64, 128), F32)
            halo_two[side] = jnp.zeros((16, 512), F32)
    for layer, e in enumerate((-2, -1, 1, 2)):
        @pl.when(jnp.logical_not(has[e]))
        def _(layer=layer):
            halo_three[layer] = jnp.zeros((8, 512), F32)

    pl.semaphore_wait(barrier, count)
    table_copies = [
        remote(rim_out.at[0], rims.at[0], rim_send.at[0], rim_receive.at[0], after),
        remote(rim_out.at[1], rims.at[1], rim_send.at[1], rim_receive.at[1], before),
    ]
    for p in places:
        table_copies.append(
            remote(message, gathered.at[back[p]], send.at[back[p]], receive_sem.at[back[p]], peers[p])
        )
    for copy in table_copies:
        copy.start()
    leaf_copies = [
        (1, remote(
            source.at[:, 1, :, pl.ds(384, 128)], leaf_halo.at[0], leaf_send.at[0], leaf_receive.at[0], beside[1]
        )),
        (-1, remote(
            source.at[:, 0, :, pl.ds(0, 128)], leaf_halo.at[1], leaf_send.at[1], leaf_receive.at[1], beside[-1]
        )),
    ]
    for e, copy in leaf_copies:
        pl.when(has[e])(copy.start)

    lane = iota((64, 128), 1)
    double = dot(near_blocks[...], onehot(lane // 2 == iota((64, 128), 0))).astype(BF16)
    row, column = iota((216, 216), 0), iota((216, 216), 1)
    same = 8 * (row // 8) + 4 * (row % 2) + row % 8 // 2
    other = 8 * (row // 8) + 4 * (1 - row % 2) + row % 8 // 2
    kept = dot(onehot(column == same), double)
    crossed = dot(onehot(column == other), double)
    crossed = jnp.where(iota((216, 128), 0) % 2 == 0, -crossed, crossed)
    blocks = jnp.where(iota((216, 128), 1) % 2 == 0, kept, crossed).astype(BF16)
    lane = iota((8, 128), 1)
    for k in range(27):
        dy, dz = k // 3 % 3 - 1, k % 3 - 1
        y, z = lane // 16 + dy, lane % 16 + dz
        valid = (y >= 0) & (y < 8) & (z >= 0) & (z < 16)
        values = jnp.where(valid, mask[k].astype(F32), 0.0)
        rolled[k] = pltpu.roll(values, (16 * dy + dz) % 128, 1)
    for r in range(2):
        for ox in range(2):
            layers = dot(blocks, source[r, ox])
            for x in range(4):
                products[r, 1 + 2 * x + ox] = layers[:, 128 * x : 128 * x + 128]
    for e, copy in leaf_copies:
        pl.when(has[e])(copy.wait_send)
        pl.when(has[-e])(copy.wait_recv)
    for r in range(2):
        for side in range(2):
            products[r, 9 * side] = dot(blocks, leaf_halo[side, r])
    for r in range(2):
        for x in range(8):
            total = jnp.zeros((8, 128), F32)
            for inner in range(9):
                dy, dz = inner // 3 - 1, inner % 3 - 1
                term = jnp.zeros((8, 128), F32)
                for dx in range(3):
                    k = 9 * dx + inner
                    term = term + products[r, x + dx, 8 * k : 8 * k + 8, :] * rolled[k, x : x + 1, :]
                total = total + pltpu.roll(term, (-16 * dy - dz) % 128, 1)
            near[r, x] = total

    for copy in table_copies:
        copy.wait_send()
    for copy in table_copies:
        copy.wait_recv()
    pad = jnp.zeros((8, 32), F32)
    angles = jnp.concatenate([rims[0, :, 0:32], angles_one, rims[1, :, 0:32], pad], axis=1)
    turns = cosines(angles).T
    sources = []
    for a in range(5):
        owner = lax.rem(me + dirs - 2 + a, dirs)
        at = 4 * lax.rem(owner // 4 + 4 - place_x, 4) + 2 * ((owner // 2 + place_z) % 2) + (owner + core) % 2
        sources.append(gathered[at].astype(F32)[8:16])
    sources = jnp.concatenate(sources, axis=0)
    send_real = dot_left(up_one, sources.astype(BF16))
    send_turned = turned(send_real)
    even = iota((96, 128), 1) % 2 == 0
    for o in range(8):
        moved = turns[:96, o : o + 1] * send_real + turns[:96, 8 + o : 9 + o] * send_turned
        swapped = jnp.where(even, pltpu.roll(moved, 127, 1), pltpu.roll(moved, 1, 1))
        rows = jnp.concatenate([jnp.where(even, moved, -moved), swapped], axis=0)
        high, low = split(rows)
        shape_high[:, 128 * o : 128 * o + 128] = high
        shape_low[:, 128 * o : 128 * o + 128] = low
    level_one = dot(shape_high[...], leaf[...]) + dot(shape_low[...], leaf[...])
    own = jnp.concatenate(
        [level_one[96 * c + 32 : 96 * c + 64, 128 * r : 128 * r + 128] for c in range(2) for r in range(2)],
        axis=0,
    )
    one[...] = own.T
    halo_copies = [
        (e, remote(origin, target, halo_send.at[i], halo_receive.at[i], beside[e]))
        for i, (e, origin, target) in enumerate([
            (1, one.at[pl.ds(64, 64)], halo_one.at[0]),
            (-1, one.at[pl.ds(0, 64)], halo_one.at[1]),
            (1, two, halo_two.at[0]),
            (-1, two, halo_two.at[1]),
            (2, three, halo_three.at[0]),
            (1, three, halo_three.at[1]),
            (-1, three, halo_three.at[2]),
            (-2, three, halo_three.at[3]),
        ])
    ]
    for e, copy in halo_copies[:2]:
        pl.when(has[e])(copy.start)

    pad = jnp.zeros((8, 64), F32)
    angles = jnp.concatenate([rims[0, :, 32:64], angles_two, rims[1, :, 32:64], pad], axis=1)
    lane = iota((16, 256), 1)
    kind = child_of_box(lane % 128) + 8 * (lane // 128)
    phases = dot_left(cosines(angles).T[:192], onehot(iota((16, 256), 0) == kind))
    cosine_two, sine_two = phases[:, :128], phases[:, 128:]
    parent = onehot(parent_of_box(iota((16, 128), 1)) == iota((16, 128), 0))
    real = dot3(up_two, level_one[:96])
    imag = dot3(up_two, level_one[96:])
    parts = []
    for c in range(2):
        for r in range(2):
            x, y = real[:, 128 * r : 128 * r + 128], imag[:, 128 * r : 128 * r + 128]
            value = x * cosine_two - y * sine_two if c == 0 else y * cosine_two + x * sine_two
            parts.append(dot_right(parent, value, ((1,), (1,))))
    for index in range(4):
        two[:, 128 * index : 128 * index + 128] = parts[index][:, 32:160]
    for e, copy in halo_copies[2:4]:
        pl.when(has[e])(copy.start)
    level_two = jnp.concatenate(parts, axis=0)
    upper = dot3(level_two, up_three)
    turns_three = cosines(jnp.concatenate([shift_three[:, a, :] for a in range(8)], axis=1))
    row, column = iota((16, 8), 0), iota((16, 8), 1)
    expand = onehot(column == 4 * (row // 8) + 2 * (row // 4 % 2) + row % 2)
    cosine_three = dot_right(expand, turns_three[:8])
    sine_three = dot_right(expand, turns_three[8:])
    parts = []
    for c in range(2):
        for r in range(2):
            x, y = upper[16 * r : 16 * r + 16], upper[32 + 16 * r : 48 + 16 * r]
            parts.append(x * cosine_three - y * sine_three if c == 0 else y * cosine_three + x * sine_three)
    row = iota((8, 64), 1)
    together = onehot(row // 16 * 2 + row // 2 % 2 == iota((8, 64), 0))
    three[...] = dot_right(together, jnp.concatenate(parts, axis=0))
    for e, copy in halo_copies[4:]:
        pl.when(has[e])(copy.start)

    tables = gathered[...].astype(F32)
    stacked = jnp.concatenate([tables[e, 0:8] for e in range(16)], axis=0)
    row, lane = iota((128, 640), 0), iota((128, 640), 1)
    azimuth = (me + 14 + lane // 128) % 16
    pick = onehot(row == 64 * (lane % 2) + 16 * (lane % 8 // 2) + azimuth)
    placed = dot(stacked.astype(BF16), pick)
    owner = iota((8, 640), 1) % 128 // 8
    summed = jnp.where(owner == me, placed[0:8], 0.0)
    for p in places:
        summed = jnp.where(owner == number[p], placed[8 * slot[p] : 8 * slot[p] + 8], summed)
    targets = jnp.concatenate([summed[:, 128 * a : 128 * a + 128] for a in range(5)], axis=0)
    take_real = dot_left(up_one, targets.astype(BF16))
    take_turned = turned(take_real)
    for o in range(8):
        moved = turns[:96, o : o + 1] * take_real - turns[:96, 8 + o : 9 + o] * take_turned
        columns = jnp.concatenate([moved, turned(moved)], axis=0)
        high, low = split(columns.T)
        far_high[128 * o : 128 * o + 128, :] = high
        far_low[128 * o : 128 * o + 128, :] = low

    for e, copy in halo_copies[:2]:
        pl.when(has[-e])(copy.wait_recv)
    z = iota((8, 128), 0)
    for shift in range(5):
        dz = shift - 2
        valid = (z + dz >= 0) & (z + dz < 8)
        for x in range(8):
            for y in range(4):
                row = 8 * y + 32 * (x % 2)
                if x < 2 or x > 5:
                    block = halo_one[x // 4, row : row + 8, :]
                else:
                    block = one[32 * (x - 2) + 8 * y : 32 * (x - 2) + 8 * y + 8, :]
                ext_one[shift, x, y + 2] = shifted_rows(block, dz, valid)
    real = jnp.zeros((4, 4, 8, 128), F32)
    imag = jnp.zeros((4, 4, 8, 128), F32)
    for k in range(32):
        dx, dy, dz = lists[0, 0, k], lists[0, 1, k], lists[0, 2, k]
        window = ext_one[dz + 2, pl.ds(dx + 2, 4), pl.ds(dy + 2, 4)]
        real = real + window * table_one[0, k : k + 1, :]
        imag = imag + window * table_one[1, k : k + 1, :]
    imag = imag.reshape(128, 128)
    turned_imag = pltpu.roll(imag, 64, 1)
    field = real.reshape(128, 128) + jnp.where(iota((128, 128), 1) < 64, -turned_imag, turned_imag)
    field_one = field.T
    for e, copy in halo_copies[2:4]:
        pl.when(has[-e])(copy.wait_recv)
    y, z = iota((8, 512), 0) // 4, iota((8, 512), 0) % 4
    for shift in range(5, 20):
        dy, dz = shift // 5 - 2, shift % 5 - 2
        valid = (y + dy >= 0) & (y + dy < 2) & (z + dz >= 0) & (z + dz < 4)
        for x in range(6):
            row = 8 * (x % 2)
            if x < 2 or x > 3:
                block = halo_two[x // 3, row : row + 8, :]
            else:
                block = two[row : row + 8, :]
            ext_two[shift, x] = shifted_rows(block, 4 * dy + dz, valid)
    reals = [jnp.zeros((2, 8, 128), F32) for _ in range(4)]
    for k in range(32):
        dx, dy, dz = lists[1, 0, k], lists[1, 1, k], lists[1, 2, k]
        window = ext_two[5 * dy + dz + 12, pl.ds(dx + 2, 2)]
        x = table_two[2 * k : 2 * k + 1, :]
        y = table_two[2 * k + 1 : 2 * k + 2, :]
        parts = [window[:, :, 128 * i : 128 * i + 128] for i in range(4)]
        for r in range(2):
            reals[r] = reals[r] + (x * parts[r] - y * parts[2 + r])
            reals[2 + r] = reals[2 + r] + (x * parts[2 + r] + y * parts[r])
    side = jnp.zeros((64, 32), F32)
    field_two = jnp.concatenate([side, jnp.concatenate(reals, axis=0).reshape(64, 128), side], axis=1)
    for e, copy in halo_copies[4:]:
        pl.when(has[-e])(copy.wait_recv)
    z = iota((8, 512), 0) % 2
    for x in range(5):
        block = three[...] if x == 2 else halo_three[x - x // 3]
        for shift in range(3):
            dz = shift - 1
            ext_three[shift, x] = shifted_rows(block, dz, (z + dz >= 0) & (z + dz < 2))
    real = jnp.zeros((8, 512), F32)
    imag = jnp.zeros((8, 512), F32)
    for k in range(32):
        dx, dy, dz = lists[2, 0, k], lists[2, 1, k], lists[2, 2, k]
        inside = (dy == 0) & (dz >= -1) & (dz <= 1)
        window = ext_three[jnp.where(inside, dz + 1, 3), dx + 2]
        real = real + window * table_three[2 * k : 2 * k + 1, :]
        imag = imag + window * table_three[2 * k + 1 : 2 * k + 2, :]
    imag = pltpu.roll(imag, 4, 0)
    incoming = real + jnp.where(iota((8, 512), 0) < 4, -imag, imag)

    row = iota((64, 8), 0)
    apart = onehot(row // 16 * 2 + row // 2 % 2 == iota((64, 8), 1))
    spread = dot_right(apart, incoming)
    parts = []
    for c in range(2):
        for r in range(2):
            x, y = spread[16 * r : 16 * r + 16], spread[32 + 16 * r : 48 + 16 * r]
            parts.append(x * cosine_three + y * sine_three if c == 0 else y * cosine_three - x * sine_three)
    level_two = field_two + dot3(jnp.concatenate(parts, axis=0), up_three, ((1,), (1,)))
    columns = level_two.T
    spread = [dot_left(columns[:, 16 * i : 16 * i + 16], parent) for i in range(4)]
    real = jnp.concatenate([spread[r] * cosine_two + spread[2 + r] * sine_two for r in range(2)], axis=1)
    imag = jnp.concatenate([spread[2 + r] * cosine_two - spread[r] * sine_two for r in range(2)], axis=1)
    pad = jnp.zeros((32, 256), F32)
    level_one = []
    for c, value in enumerate((real, imag)):
        field = jnp.concatenate([field_one[64 * c + 32 * r : 64 * c + 32 * r + 32] for r in range(2)], axis=1)
        level_one.append(dot3(back_two, value) + jnp.concatenate([pad, field, pad], axis=0))
    high, low = split(jnp.concatenate(level_one, axis=0))

    sibling = peers[(0, 0, 1)]
    to_core = [
        remote(partial.at[i, 1 - core], got_core.at[i], sum_send.at[i], sum_receive.at[i], sibling)
        for i in range(4)
    ]
    owners = [p for p in places if p[2] == 0]
    to_owner = [
        remote(coded.at[j], got_coded.at[owners.index(((4 - p[0]) % 4, p[1], 0))], sum_send.at[4 + j],
               sum_receive.at[4 + owners.index(((4 - p[0]) % 4, p[1], 0))], peers[p])
        for j, p in enumerate(owners)
    ]

    def after_core(i):
        to_core[i].wait_recv()
        held[:, :, 16 * i : 16 * i + 16, :] = partial[i, core] + got_core[i]

    for i in range(4):
        for o in (2 * i, 2 * i + 1):
            rows = slice(128 * o, 128 * o + 128)
            total = dot(far_high[rows], high) + (dot(far_high[rows], low) + dot(far_low[rows], high))
            for owner in range(16):
                partial[i, owner % 2, owner // 4, owner // 2 % 2, 8 * (o % 2) : 8 * (o % 2) + 8, :] = total[
                    8 * owner : 8 * owner + 8
                ]
        to_core[i].start()
        if i > 0:
            after_core(i - 1)
    after_core(3)
    for j, p in enumerate(owners):
        block = held[lax.rem(place_x + p[0], 4), (place_z + p[1]) % 2]
        largest = jnp.max(jnp.abs(block), axis=0, keepdims=True)
        power = jnp.ceil(jnp.log2(jnp.maximum(largest, 1e-25)))
        values = jnp.floor(block * (32000.0 / jnp.exp2(power)) + 0.5)
        coded[j, 0:64] = values.astype(jnp.int32).astype(jnp.int16)
        coded[j, 64:80] = jnp.broadcast_to(power, (16, 256)).astype(jnp.int32).astype(jnp.int16)
        to_owner[j].start()
    for e, copy in halo_copies:
        pl.when(has[e])(copy.wait_send)
    for copy in to_core + to_owner:
        copy.wait_send()
    far = held[place_x, place_z]
    for copy in to_owner:
        copy.wait_recv()
    for j in range(len(owners)):
        power = got_coded[j, 64:80].astype(jnp.int32).astype(F32)[0:1]
        values = got_coded[j, 0:64].astype(jnp.int32).astype(F32)
        far = far + values * (jnp.exp2(power) / 32000.0)
    rows = []
    for r in range(2):
        for ox in range(2):
            pieces = [
                far[32 * ox + 8 * o : 32 * ox + 8 * o + 8, 128 * r : 128 * r + 128] for o in range(4)
            ]
            rows.append(jnp.concatenate(pieces, axis=1))
    high, low = split(jnp.concatenate(rows, axis=0))
    both = dot(jnp.concatenate([high, low], axis=0), shuffle[...], ((1,), (1,)))
    far = both[:32] + both[32:]
    for r in range(2):
        for ox in range(2):
            for x in range(4):
                row = 8 * (2 * r + ox)
                out_ref[:, r, 2 * x + ox, :] = (
                    near[r, 2 * x + ox] + far[row : row + 8, 128 * x : 128 * x + 128]
                )


VMEM = pl.BlockSpec(memory_space=pltpu.VMEM)
HBM = pl.BlockSpec(memory_space=pltpu.HBM)
DMA = pltpu.SemaphoreType.DMA


def held_in(*dims, dtype=F32):
    return pltpu.VMEM(dims, dtype)


def shuffle_table():
    index = np.arange(512)
    x, y, z = index // 128, index // 16 % 8, index % 16
    target = 256 * (y % 2) + 128 * (z % 2) + 32 * x + 8 * (y // 2) + z // 2
    return (target[:, None] == index[None, :]).astype(np.float32)


def shards(
    source, near_blocks, near_mask, radiate, receive, theta_one, theta_two, theta_three, phi_taps,
    shift_one, shift_two, shift_three, trans_one, trans_two, trans_three, far_lists,
):
    dirs, boxes = lax.axis_size("dir"), lax.axis_size("box")
    args = (
        source.reshape(2048, 128), near_blocks.reshape(216, 64), near_mask, radiate[:, :, 0], jnp.transpose(receive, (0, 1, 3, 2)),
        theta_one.T, theta_two.T, theta_three.T, phi_taps,
        jnp.transpose(shift_one, (0, 2, 1)), jnp.transpose(shift_two, (0, 2, 1)),
        jnp.transpose(shift_three, (0, 2, 1)), jnp.transpose(trans_one, (1, 2, 3, 0)),
        jnp.transpose(trans_two, (0, 1, 3, 2)).reshape(64, 4, 32),
        jnp.transpose(trans_three, (0, 1, 3, 2)).reshape(64, 8, 64),
        jnp.transpose(far_lists, (0, 2, 1)), jnp.asarray(shuffle_table(), BF16),
    )
    copies = [pltpu.VMEM(a.shape, a.dtype) for a in args]
    copies[15] = pltpu.SMEM(args[15].shape, args[15].dtype)
    out = pl.pallas_call(
        functools.partial(whole, dirs, boxes),
        out_shape=jax.ShapeDtypeStruct((8, 2, 8, 128), F32),
        in_specs=[HBM] * INPUTS,
        out_specs=VMEM,
        scratch_shapes=copies
        + [
            DMA((INPUTS,)), held_in(2048, 128), held_in(2, 2, 128, 512, dtype=BF16),
            held_in(16, 128, dtype=BF16), held_in(16, 16, 128, dtype=BF16), held_in(2, 8, 128), held_in(2, 8, 128),
            held_in(2, 2, 128, 128, dtype=BF16), held_in(2, 64, 128), held_in(2, 16, 512), held_in(4, 8, 512),
            held_in(128, 128), held_in(16, 512), held_in(8, 512),
            held_in(1024, 256, dtype=BF16), held_in(192, 1024, dtype=BF16), held_in(192, 1024, dtype=BF16),
            held_in(1024, 192, dtype=BF16), held_in(1024, 192, dtype=BF16),
            held_in(2, 10, 216, 128), held_in(27, 8, 128), held_in(2, 8, 8, 128),
            held_in(2, 32, 128), held_in(64, 128), held_in(64, 512),
            held_in(5, 8, 8, 8, 128), held_in(25, 6, 8, 512), held_in(4, 5, 8, 512),
            held_in(4, 2, 4, 2, 16, 256), held_in(4, 4, 2, 16, 256), held_in(4, 2, 64, 256),
            held_in(7, 80, 256, dtype=jnp.int16), held_in(7, 80, 256, dtype=jnp.int16),
            DMA((16,)), DMA((16,)), DMA((2,)), DMA((2,)), DMA((2,)), DMA((2,)), DMA((8,)), DMA((8,)),
            DMA((11,)), DMA((11,)),
        ],
        compiler_params=pltpu.CompilerParams(
            collective_id=1, has_side_effects=True, vmem_limit_bytes=VMEM_LIMIT
        ),
    )(*args)
    return out.reshape(4, 2, 2, 8, 128)


def solution(mesh):
    placed = (
        P(None, None, None, "box", None),
        P(None, None, "dir", None),
        P(None, "box", None),
        P(None, None, "dir", None),
        P(None, None, None, "dir"),
        P(),
        P(),
        P(),
        P(),
        P(None, None, "dir"),
        P(None, None, "dir"),
        P(None, None, "dir"),
        P(None, None, None, "dir"),
        P(None, None, None, "dir"),
        P(None, None, None, "dir"),
        P(),
    )
    return jax.shard_map(
        shards,
        mesh=mesh,
        in_specs=placed,
        out_specs=P("dir", None, None, "box", None),
        check_vma=False,
    )
```

```python
import functools

import jax
import jax.numpy as jnp
import numpy as np
from jax import lax
from jax.experimental import pallas as pl
from jax.experimental.pallas import tpu as pltpu
from jax.sharding import PartitionSpec as P

MESH = pl.DeviceIdType.MESH
F32 = jnp.float32
BF16 = jnp.bfloat16
VMEM_LIMIT = 56 * 1024 * 1024
INPUTS = 17


def iota(shape, dim):
    return lax.broadcasted_iota(jnp.int32, shape, dim)


def split(a):
    high = a.astype(BF16)
    return high, (a - high.astype(F32)).astype(BF16)


def dot(a, b, dims=((1,), (0,))):
    return lax.dot_general(a, b, (dims, ((), ())), preferred_element_type=F32)


def dot3(a, b, dims=((1,), (0,))):
    a_high, a_low = split(a)
    b_high, b_low = split(b)
    return dot(a_high, b_high, dims) + (dot(a_high, b_low, dims) + dot(a_low, b_high, dims))


def dot_left(a, b, dims=((1,), (0,))):
    a_high, a_low = split(a)
    return dot(a_high, b, dims) + dot(a_low, b, dims)


def dot_right(a, b, dims=((1,), (0,))):
    b_high, b_low = split(b)
    return dot(a, b_high, dims) + dot(a, b_low, dims)


def onehot(condition):
    return jnp.where(condition, 1.0, 0.0).astype(BF16)


def interpolation(taps, level, theta, fine, coarse, wide, first, transposed):
    (fine_p, fine_t), (coarse_p, coarse_t) = fine, coarse
    if transposed:
        spread = onehot(iota((fine_t, fine_p * fine_t), 1) % fine_t == iota((fine_t, fine_p * fine_t), 0))
        tiled = jnp.concatenate([dot_left(theta, spread)] * coarse_p, axis=0)
        fine_dim, coarse_dim = 1, 0
    else:
        spread = onehot(
            iota((coarse_t, coarse_p * coarse_t), 1) % coarse_t == iota((coarse_t, coarse_p * coarse_t), 0)
        )
        tiled = jnp.concatenate([dot_left(theta, spread, ((0,), (0,)))] * fine_p, axis=0)
        fine_dim, coarse_dim = 0, 1
    p = iota(tiled.shape, fine_dim) // fine_t
    tap = iota(tiled.shape, coarse_dim) // coarse_t - first(p)
    even = wide(p) % 2 == 0
    weight = jnp.zeros(tiled.shape, F32)
    for j in range(3):
        value = jnp.where(even, taps[level, 0:1, j : j + 1], taps[level, 1:2, j : j + 1])
        weight = jnp.where(tap == j, value, weight)
    return weight * tiled


def turned(x):
    even = iota(x.shape, 1) % 2 == 0
    count = x.shape[1]
    return jnp.where(even, -pltpu.roll(x, count - 1, 1), pltpu.roll(x, 1, 1))


def child_of_box(index):
    return 4 * (index // 32 % 2) + 2 * (index // 8 % 2) + index % 2


def parent_of_box(index):
    return index // 64 * 8 + index // 16 % 2 * 4 + index // 2 % 4


def shifted_rows(block, shift, valid):
    moved = pltpu.roll(block, (-shift) % 8, 0) if shift % 8 else block
    return jnp.where(valid, moved, 0.0)


def cosines(angles):
    return jnp.concatenate([jnp.cos(angles), jnp.sin(angles)], axis=0)


def remote(source, target, send, receive, peer):
    return pltpu.make_async_remote_copy(
        src_ref=source, dst_ref=target, send_sem=send, recv_sem=receive, device_id=peer, device_id_type=MESH
    )


def whole(dirs, boxes, *refs):
    outside, out_ref, inside = refs[:INPUTS], refs[INPUTS], refs[INPUTS + 1 : 2 * INPUTS + 1]
    (
        leaf_rows, near_blocks, mask, radiate, receive, theta_one, theta_two, theta_three, taps,
        shift_one, shift_two, shift_three, trans_one, trans_two, trans_three, lists, shuffle,
    ) = inside
    (
        in_sem, wide_rows, source, message, gathered, rim_out, rims, leaf_halo, halo_one, halo_two, halo_three,
        one, two, three, leaf, shape_high, shape_low, far_high, far_low, products, rolled, near,
        table_one, table_two, table_three, ext_one, ext_two, ext_three,
        partial, got_core, held, coded, got_coded,
        send, receive_sem, rim_send, rim_receive, leaf_send, leaf_receive, halo_send, halo_receive,
        sum_send, sum_receive,
    ) = refs[2 * INPUTS + 1 :]
    me, box = lax.axis_index("dir"), lax.axis_index("box")
    has = {-1: box > 0, 1: box < boxes - 1, -2: box > 1, 2: box < boxes - 2}
    beside = {e: {"box": lax.rem(box + boxes + e, boxes)} for e in has}
    place_x, place_z, core = me // 4, me // 2 % 2, me % 2
    places = [(dx, dz, dc) for dz in (1, 0) for dx in (2, 1, 3, 0) for dc in (1, 0)][: dirs - 1]
    number = {p: 4 * lax.rem(place_x + p[0], 4) + 2 * ((place_z + p[1]) % 2) + (core + p[2]) % 2 for p in places}
    peers = {p: {"dir": number[p]} for p in places}
    slot = {p: 4 * p[0] + 2 * p[1] + p[2] for p in places}
    back = {p: slot[((4 - p[0]) % 4, p[1], p[2])] for p in places}
    after, before = {"dir": lax.rem(me + 1, dirs)}, {"dir": lax.rem(me + dirs - 1, dirs)}

    barrier = pltpu.get_barrier_semaphore()
    count = dirs - 1
    for p in places:
        pl.semaphore_signal(barrier, inc=1, device_id=peers[p], device_id_type=MESH)
    for e in has:
        @pl.when(has[e])
        def _(e=e):
            pl.semaphore_signal(barrier, inc=1, device_id=beside[e], device_id_type=MESH)

        count = count + jnp.where(has[e], 1, 0)

    loads = [pltpu.make_async_copy(outside[i], inside[i], in_sem.at[i]) for i in range(INPUTS)]
    early = (3, 4, 9, 10)
    for i in early:
        loads[i].start()
    for i in range(INPUTS):
        if i not in early:
            loads[i].start()
    for i in early:
        loads[i].wait()

    taken = [receive[c, :, u, :].astype(F32) for c in range(2) for u in range(4)]
    lane = iota((64, 128), 1)
    sent = [dot(radiate[c], onehot(lane == 2 * iota((64, 128), 0) + c)) for c in range(2)]
    tile = jnp.concatenate([jnp.concatenate(taken, axis=1), sent[0] + sent[1]], axis=0).astype(BF16)
    message[...] = tile
    gathered[0] = tile
    angles_one = jnp.concatenate([shift_one[:, a, :] for a in range(2)], axis=1)
    angles_two = jnp.concatenate([shift_two[:, a, :] for a in range(4)], axis=1)
    pad = jnp.zeros((8, 64), F32)
    rim_out[0] = jnp.concatenate([angles_one, angles_two[:, 96:], pad], axis=1)
    rim_out[1] = jnp.concatenate([angles_one, angles_two[:, :32], pad], axis=1)

    for i in range(INPUTS):
        if i not in early:
            loads[i].wait()
    up_one = interpolation(
        taps, 0, theta_one[...], (6, 16), (5, 8), lambda p: p, lambda p: p // 2, False
    )
    up_two = interpolation(
        taps, 1, theta_two[...], (6, 32), (6, 16), lambda p: p + 1, lambda p: (p + 1) // 2, False
    )
    back_two = interpolation(
        taps, 1, theta_two[...], (6, 32), (6, 16), lambda p: p + 1, lambda p: (p + 1) // 2, True
    )
    up_three = interpolation(
        taps, 2, theta_three[...], (8, 64), (6, 32), lambda p: p, lambda p: p // 2, True
    )
    wide_rows[...] = leaf_rows[...].astype(F32)
    for r in range(2):
        for x in range(8):
            layer = wide_rows[pl.ds(8 * r + x, 128, stride=16), :].astype(BF16)
            source[r, x % 2, :, 128 * (x // 2) : 128 * (x // 2) + 128] = layer
    for r in range(2):
        for ox in range(2):
            mixed = dot(source[r, ox], shuffle[...]).astype(BF16)
            for o in range(4):
                row = 128 * (4 * ox + o)
                leaf[row : row + 128, 128 * r : 128 * r + 128] = mixed[:, 128 * o : 128 * o + 128]
    for a in range(8):
        table_three[:, 64 * a : 64 * a + 64] = trans_three[:, a, :]
    for a in range(4):
        table_two[:, 32 * a : 32 * a + 32] = trans_two[:, a, :]
    for c in range(2):
        total = jnp.zeros((32, 128), F32)
        for a in range(2):
            place = onehot(iota((16, 128), 1) % 32 == 16 * a + iota((16, 128), 0))
            total = total + dot_left(trans_one[c, :, a, :], place, ((0,), (0,)))
        table_one[c] = total
    zero = jnp.zeros((8, 128), F32)
    for shift in range(5):
        for x in range(8):
            for y in (0, 1, 6, 7):
                ext_one[shift, x, y] = zero
    zero = jnp.zeros((8, 512), F32)
    for x in range(6):
        for shift in range(5):
            ext_two[shift, x] = zero
            ext_two[20 + shift, x] = zero
    for x in range(5):
        ext_three[3, x] = zero
    for side, e in enumerate((-1, 1)):
        @pl.when(jnp.logical_not(has[e]))
        def _(side=side):
            leaf_halo[side] = jnp.zeros((2, 128, 128), BF16)
            halo_one[side] = jnp.zeros((64, 128), F32)
            halo_two[side] = jnp.zeros((16, 512), F32)
    for layer, e in enumerate((-2, -1, 1, 2)):
        @pl.when(jnp.logical_not(has[e]))
        def _(layer=layer):
            halo_three[layer] = jnp.zeros((8, 512), F32)

    pl.semaphore_wait(barrier, count)
    table_copies = [
        remote(rim_out.at[0], rims.at[0], rim_send.at[0], rim_receive.at[0], after),
        remote(rim_out.at[1], rims.at[1], rim_send.at[1], rim_receive.at[1], before),
    ]
    for p in places:
        table_copies.append(
            remote(message, gathered.at[back[p]], send.at[back[p]], receive_sem.at[back[p]], peers[p])
        )
    for copy in table_copies:
        copy.start()
    leaf_copies = [
        (1, remote(
            source.at[:, 1, :, pl.ds(384, 128)], leaf_halo.at[0], leaf_send.at[0], leaf_receive.at[0], beside[1]
        )),
        (-1, remote(
            source.at[:, 0, :, pl.ds(0, 128)], leaf_halo.at[1], leaf_send.at[1], leaf_receive.at[1], beside[-1]
        )),
    ]
    for e, copy in leaf_copies:
        pl.when(has[e])(copy.start)

    lane = iota((64, 128), 1)
    double = dot(near_blocks[...], onehot(lane // 2 == iota((64, 128), 0))).astype(BF16)
    row, column = iota((216, 216), 0), iota((216, 216), 1)
    same = 8 * (row // 8) + 4 * (row % 2) + row % 8 // 2
    other = 8 * (row // 8) + 4 * (1 - row % 2) + row % 8 // 2
    kept = dot(onehot(column == same), double)
    crossed = dot(onehot(column == other), double)
    crossed = jnp.where(iota((216, 128), 0) % 2 == 0, -crossed, crossed)
    blocks = jnp.where(iota((216, 128), 1) % 2 == 0, kept, crossed).astype(BF16)
    lane = iota((8, 128), 1)
    for k in range(27):
        dy, dz = k // 3 % 3 - 1, k % 3 - 1
        y, z = lane // 16 + dy, lane % 16 + dz
        valid = (y >= 0) & (y < 8) & (z >= 0) & (z < 16)
        values = jnp.where(valid, mask[k].astype(F32), 0.0)
        rolled[k] = pltpu.roll(values, (16 * dy + dz) % 128, 1)
    for r in range(2):
        for ox in range(2):
            layers = dot(blocks, source[r, ox])
            for x in range(4):
                products[r, 1 + 2 * x + ox] = layers[:, 128 * x : 128 * x + 128]
    for e, copy in leaf_copies:
        pl.when(has[e])(copy.wait_send)
        pl.when(has[-e])(copy.wait_recv)
    for r in range(2):
        for side in range(2):
            products[r, 9 * side] = dot(blocks, leaf_halo[side, r])
    for r in range(2):
        for x in range(8):
            total = jnp.zeros((8, 128), F32)
            for inner in range(9):
                dy, dz = inner // 3 - 1, inner % 3 - 1
                term = jnp.zeros((8, 128), F32)
                for dx in range(3):
                    k = 9 * dx + inner
                    term = term + products[r, x + dx, 8 * k : 8 * k + 8, :] * rolled[k, x : x + 1, :]
                total = total + pltpu.roll(term, (-16 * dy - dz) % 128, 1)
            near[r, x] = total

    for copy in table_copies:
        copy.wait_send()
    for copy in table_copies:
        copy.wait_recv()
    pad = jnp.zeros((8, 32), F32)
    angles = jnp.concatenate([rims[0, :, 0:32], angles_one, rims[1, :, 0:32], pad], axis=1)
    turns = cosines(angles).T
    sources = []
    for a in range(5):
        owner = lax.rem(me + dirs - 2 + a, dirs)
        at = 4 * lax.rem(owner // 4 + 4 - place_x, 4) + 2 * ((owner // 2 + place_z) % 2) + (owner + core) % 2
        sources.append(gathered[at].astype(F32)[8:16])
    sources = jnp.concatenate(sources, axis=0)
    send_real = dot_left(up_one, sources.astype(BF16))
    send_turned = turned(send_real)
    even = iota((96, 128), 1) % 2 == 0
    for o in range(8):
        moved = turns[:96, o : o + 1] * send_real + turns[:96, 8 + o : 9 + o] * send_turned
        swapped = jnp.where(even, pltpu.roll(moved, 127, 1), pltpu.roll(moved, 1, 1))
        rows = jnp.concatenate([jnp.where(even, moved, -moved), swapped], axis=0)
        high, low = split(rows)
        shape_high[:, 128 * o : 128 * o + 128] = high
        shape_low[:, 128 * o : 128 * o + 128] = low
    level_one = dot(shape_high[...], leaf[...]) + dot(shape_low[...], leaf[...])
    own = jnp.concatenate(
        [level_one[96 * c + 32 : 96 * c + 64, 128 * r : 128 * r + 128] for c in range(2) for r in range(2)],
        axis=0,
    )
    one[...] = own.T
    halo_copies = [
        (e, remote(origin, target, halo_send.at[i], halo_receive.at[i], beside[e]))
        for i, (e, origin, target) in enumerate([
            (1, one.at[pl.ds(64, 64)], halo_one.at[0]),
            (-1, one.at[pl.ds(0, 64)], halo_one.at[1]),
            (1, two, halo_two.at[0]),
            (-1, two, halo_two.at[1]),
            (2, three, halo_three.at[0]),
            (1, three, halo_three.at[1]),
            (-1, three, halo_three.at[2]),
            (-2, three, halo_three.at[3]),
        ])
    ]
    for e, copy in halo_copies[:2]:
        pl.when(has[e])(copy.start)

    pad = jnp.zeros((8, 64), F32)
    angles = jnp.concatenate([rims[0, :, 32:64], angles_two, rims[1, :, 32:64], pad], axis=1)
    lane = iota((16, 256), 1)
    kind = child_of_box(lane % 128) + 8 * (lane // 128)
    phases = dot_left(cosines(angles).T[:192], onehot(iota((16, 256), 0) == kind))
    cosine_two, sine_two = phases[:, :128], phases[:, 128:]
    parent = onehot(parent_of_box(iota((16, 128), 1)) == iota((16, 128), 0))
    real = dot3(up_two, level_one[:96])
    imag = dot3(up_two, level_one[96:])
    parts = []
    for c in range(2):
        for r in range(2):
            x, y = real[:, 128 * r : 128 * r + 128], imag[:, 128 * r : 128 * r + 128]
            value = x * cosine_two - y * sine_two if c == 0 else y * cosine_two + x * sine_two
            parts.append(dot_right(parent, value, ((1,), (1,))))
    for index in range(4):
        two[:, 128 * index : 128 * index + 128] = parts[index][:, 32:160]
    for e, copy in halo_copies[2:4]:
        pl.when(has[e])(copy.start)
    level_two = jnp.concatenate(parts, axis=0)
    upper = dot3(level_two, up_three)
    turns_three = cosines(jnp.concatenate([shift_three[:, a, :] for a in range(8)], axis=1))
    row, column = iota((16, 8), 0), iota((16, 8), 1)
    expand = onehot(column == 4 * (row // 8) + 2 * (row // 4 % 2) + row % 2)
    cosine_three = dot_right(expand, turns_three[:8])
    sine_three = dot_right(expand, turns_three[8:])
    parts = []
    for c in range(2):
        for r in range(2):
            x, y = upper[16 * r : 16 * r + 16], upper[32 + 16 * r : 48 + 16 * r]
            parts.append(x * cosine_three - y * sine_three if c == 0 else y * cosine_three + x * sine_three)
    row = iota((8, 64), 1)
    together = onehot(row // 16 * 2 + row // 2 % 2 == iota((8, 64), 0))
    three[...] = dot_right(together, jnp.concatenate(parts, axis=0))
    for e, copy in halo_copies[4:]:
        pl.when(has[e])(copy.start)

    tables = gathered[...].astype(F32)
    stacked = jnp.concatenate([tables[e, 0:8] for e in range(16)], axis=0)
    row, lane = iota((128, 640), 0), iota((128, 640), 1)
    azimuth = (me + 14 + lane // 128) % 16
    pick = onehot(row == 64 * (lane % 2) + 16 * (lane % 8 // 2) + azimuth)
    placed = dot(stacked.astype(BF16), pick)
    owner = iota((8, 640), 1) % 128 // 8
    summed = jnp.where(owner == me, placed[0:8], 0.0)
    for p in places:
        summed = jnp.where(owner == number[p], placed[8 * slot[p] : 8 * slot[p] + 8], summed)
    targets = jnp.concatenate([summed[:, 128 * a : 128 * a + 128] for a in range(5)], axis=0)
    take_real = dot_left(up_one, targets.astype(BF16))
    take_turned = turned(take_real)
    for o in range(8):
        moved = turns[:96, o : o + 1] * take_real - turns[:96, 8 + o : 9 + o] * take_turned
        columns = jnp.concatenate([moved, turned(moved)], axis=0)
        high, low = split(columns.T)
        far_high[128 * o : 128 * o + 128, :] = high
        far_low[128 * o : 128 * o + 128, :] = low

    for e, copy in halo_copies[:2]:
        pl.when(has[-e])(copy.wait_recv)
    z = iota((8, 128), 0)
    for shift in range(5):
        dz = shift - 2
        valid = (z + dz >= 0) & (z + dz < 8)
        for x in range(8):
            for y in range(4):
                row = 8 * y + 32 * (x % 2)
                if x < 2 or x > 5:
                    block = halo_one[x // 4, row : row + 8, :]
                else:
                    block = one[32 * (x - 2) + 8 * y : 32 * (x - 2) + 8 * y + 8, :]
                ext_one[shift, x, y + 2] = shifted_rows(block, dz, valid)
    real = jnp.zeros((4, 4, 8, 128), F32)
    imag = jnp.zeros((4, 4, 8, 128), F32)
    for k in range(32):
        dx, dy, dz = lists[0, 0, k], lists[0, 1, k], lists[0, 2, k]
        window = ext_one[dz + 2, pl.ds(dx + 2, 4), pl.ds(dy + 2, 4)]
        real = real + window * table_one[0, k : k + 1, :]
        imag = imag + window * table_one[1, k : k + 1, :]
    imag = imag.reshape(128, 128)
    turned_imag = pltpu.roll(imag, 64, 1)
    field = real.reshape(128, 128) + jnp.where(iota((128, 128), 1) < 64, -turned_imag, turned_imag)
    field_one = field.T
    for e, copy in halo_copies[2:4]:
        pl.when(has[-e])(copy.wait_recv)
    y, z = iota((8, 512), 0) // 4, iota((8, 512), 0) % 4
    for shift in range(5, 20):
        dy, dz = shift // 5 - 2, shift % 5 - 2
        valid = (y + dy >= 0) & (y + dy < 2) & (z + dz >= 0) & (z + dz < 4)
        for x in range(6):
            row = 8 * (x % 2)
            if x < 2 or x > 3:
                block = halo_two[x // 3, row : row + 8, :]
            else:
                block = two[row : row + 8, :]
            ext_two[shift, x] = shifted_rows(block, 4 * dy + dz, valid)
    reals = [jnp.zeros((2, 8, 128), F32) for _ in range(4)]
    for k in range(32):
        dx, dy, dz = lists[1, 0, k], lists[1, 1, k], lists[1, 2, k]
        window = ext_two[5 * dy + dz + 12, pl.ds(dx + 2, 2)]
        x = table_two[2 * k : 2 * k + 1, :]
        y = table_two[2 * k + 1 : 2 * k + 2, :]
        parts = [window[:, :, 128 * i : 128 * i + 128] for i in range(4)]
        for r in range(2):
            reals[r] = reals[r] + (x * parts[r] - y * parts[2 + r])
            reals[2 + r] = reals[2 + r] + (x * parts[2 + r] + y * parts[r])
    side = jnp.zeros((64, 32), F32)
    field_two = jnp.concatenate([side, jnp.concatenate(reals, axis=0).reshape(64, 128), side], axis=1)
    for e, copy in halo_copies[4:]:
        pl.when(has[-e])(copy.wait_recv)
    z = iota((8, 512), 0) % 2
    for x in range(5):
        block = three[...] if x == 2 else halo_three[x - x // 3]
        for shift in range(3):
            dz = shift - 1
            ext_three[shift, x] = shifted_rows(block, dz, (z + dz >= 0) & (z + dz < 2))
    real = jnp.zeros((8, 512), F32)
    imag = jnp.zeros((8, 512), F32)
    for k in range(32):
        dx, dy, dz = lists[2, 0, k], lists[2, 1, k], lists[2, 2, k]
        inside = (dy == 0) & (dz >= -1) & (dz <= 1)
        window = ext_three[jnp.where(inside, dz + 1, 3), dx + 2]
        real = real + window * table_three[2 * k : 2 * k + 1, :]
        imag = imag + window * table_three[2 * k + 1 : 2 * k + 2, :]
    imag = pltpu.roll(imag, 4, 0)
    incoming = real + jnp.where(iota((8, 512), 0) < 4, -imag, imag)

    row = iota((64, 8), 0)
    apart = onehot(row // 16 * 2 + row // 2 % 2 == iota((64, 8), 1))
    spread = dot_right(apart, incoming)
    parts = []
    for c in range(2):
        for r in range(2):
            x, y = spread[16 * r : 16 * r + 16], spread[32 + 16 * r : 48 + 16 * r]
            parts.append(x * cosine_three + y * sine_three if c == 0 else y * cosine_three - x * sine_three)
    level_two = field_two + dot3(jnp.concatenate(parts, axis=0), up_three, ((1,), (1,)))
    columns = level_two.T
    spread = [dot_left(columns[:, 16 * i : 16 * i + 16], parent) for i in range(4)]
    real = jnp.concatenate([spread[r] * cosine_two + spread[2 + r] * sine_two for r in range(2)], axis=1)
    imag = jnp.concatenate([spread[2 + r] * cosine_two - spread[r] * sine_two for r in range(2)], axis=1)
    pad = jnp.zeros((32, 256), F32)
    level_one = []
    for c, value in enumerate((real, imag)):
        field = jnp.concatenate([field_one[64 * c + 32 * r : 64 * c + 32 * r + 32] for r in range(2)], axis=1)
        level_one.append(dot3(back_two, value) + jnp.concatenate([pad, field, pad], axis=0))
    high, low = split(jnp.concatenate(level_one, axis=0))

    sibling = peers[(0, 0, 1)]
    to_core = [
        remote(partial.at[i, 1 - core], got_core.at[i], sum_send.at[i], sum_receive.at[i], sibling)
        for i in range(4)
    ]
    across = peers[(0, 1, 0)]
    along = (2, 1, 3)
    to_x = []
    for part in range(2):
        for j, e in enumerate(along):
            there = 3 * part + along.index(4 - e)
            to_x.append(remote(
                coded.at[3 * part + j], got_coded.at[there], sum_send.at[4 + there], sum_receive.at[4 + there],
                peers[(e, 0, 0)],
            ))
    to_z = remote(coded.at[6], got_coded.at[6], sum_send.at[10], sum_receive.at[10], across)

    def encode(j, block):
        largest = jnp.max(jnp.abs(block), axis=0, keepdims=True)
        power = jnp.ceil(jnp.log2(jnp.maximum(largest, 1e-25)))
        values = jnp.floor(block * (32000.0 / jnp.exp2(power)) + 0.5)
        coded[j, 0:64] = values.astype(jnp.int32).astype(jnp.int16)
        coded[j, 64:80] = jnp.broadcast_to(power, (16, 256)).astype(jnp.int32).astype(jnp.int16)

    def decode(j):
        power = got_coded[j, 64:80].astype(jnp.int32).astype(F32)[0:1]
        return got_coded[j, 0:64].astype(jnp.int32).astype(F32) * (jnp.exp2(power) / 32000.0)

    def after_core(i):
        to_core[i].wait_recv()
        held[:, :, 16 * i : 16 * i + 16, :] = partial[i, core] + got_core[i]

    for i in range(4):
        for o in (2 * i, 2 * i + 1):
            rows = slice(128 * o, 128 * o + 128)
            total = dot(far_high[rows], high) + (dot(far_high[rows], low) + dot(far_low[rows], high))
            for owner in range(16):
                partial[i, owner % 2, owner // 4, owner // 2 % 2, 8 * (o % 2) : 8 * (o % 2) + 8, :] = total[
                    8 * owner : 8 * owner + 8
                ]
        to_core[i].start()
        if i > 0:
            after_core(i - 1)
    after_core(3)
    for part in range(2):
        half = 1 - place_z if part == 0 else place_z
        for j, e in enumerate(along):
            encode(3 * part + j, held[lax.rem(place_x + e, 4), half])
            to_x[3 * part + j].start()
    for copy in to_x[:3]:
        copy.wait_recv()
    encode(6, held[place_x, 1 - place_z] + (decode(0) + decode(1) + decode(2)))
    to_z.start()
    for copy in to_x[3:]:
        copy.wait_recv()
    far = held[place_x, place_z] + (decode(3) + decode(4) + decode(5))
    for e, copy in halo_copies:
        pl.when(has[e])(copy.wait_send)
    for copy in to_core + to_x:
        copy.wait_send()
    to_z.wait()
    far = far + decode(6)
    rows = []
    for r in range(2):
        for ox in range(2):
            pieces = [
                far[32 * ox + 8 * o : 32 * ox + 8 * o + 8, 128 * r : 128 * r + 128] for o in range(4)
            ]
            rows.append(jnp.concatenate(pieces, axis=1))
    high, low = split(jnp.concatenate(rows, axis=0))
    both = dot(jnp.concatenate([high, low], axis=0), shuffle[...], ((1,), (1,)))
    far = both[:32] + both[32:]
    for r in range(2):
        for ox in range(2):
            for x in range(4):
                row = 8 * (2 * r + ox)
                out_ref[:, r, 2 * x + ox, :] = (
                    near[r, 2 * x + ox] + far[row : row + 8, 128 * x : 128 * x + 128]
                )


VMEM = pl.BlockSpec(memory_space=pltpu.VMEM)
HBM = pl.BlockSpec(memory_space=pltpu.HBM)
DMA = pltpu.SemaphoreType.DMA


def held_in(*dims, dtype=F32):
    return pltpu.VMEM(dims, dtype)


def shuffle_table():
    index = np.arange(512)
    x, y, z = index // 128, index // 16 % 8, index % 16
    target = 256 * (y % 2) + 128 * (z % 2) + 32 * x + 8 * (y // 2) + z // 2
    return (target[:, None] == index[None, :]).astype(np.float32)


def shards(
    source, near_blocks, near_mask, radiate, receive, theta_one, theta_two, theta_three, phi_taps,
    shift_one, shift_two, shift_three, trans_one, trans_two, trans_three, far_lists,
):
    dirs, boxes = lax.axis_size("dir"), lax.axis_size("box")
    args = (
        source.reshape(2048, 128), near_blocks.reshape(216, 64), near_mask, radiate[:, :, 0], jnp.transpose(receive, (0, 1, 3, 2)),
        theta_one.T, theta_two.T, theta_three.T, phi_taps,
        jnp.transpose(shift_one, (0, 2, 1)), jnp.transpose(shift_two, (0, 2, 1)),
        jnp.transpose(shift_three, (0, 2, 1)), jnp.transpose(trans_one, (1, 2, 3, 0)),
        jnp.transpose(trans_two, (0, 1, 3, 2)).reshape(64, 4, 32),
        jnp.transpose(trans_three, (0, 1, 3, 2)).reshape(64, 8, 64),
        jnp.transpose(far_lists, (0, 2, 1)), jnp.asarray(shuffle_table(), BF16),
    )
    copies = [pltpu.VMEM(a.shape, a.dtype) for a in args]
    copies[15] = pltpu.SMEM(args[15].shape, args[15].dtype)
    out = pl.pallas_call(
        functools.partial(whole, dirs, boxes),
        out_shape=jax.ShapeDtypeStruct((8, 2, 8, 128), F32),
        in_specs=[HBM] * INPUTS,
        out_specs=VMEM,
        scratch_shapes=copies
        + [
            DMA((INPUTS,)), held_in(2048, 128), held_in(2, 2, 128, 512, dtype=BF16),
            held_in(16, 128, dtype=BF16), held_in(16, 16, 128, dtype=BF16), held_in(2, 8, 128), held_in(2, 8, 128),
            held_in(2, 2, 128, 128, dtype=BF16), held_in(2, 64, 128), held_in(2, 16, 512), held_in(4, 8, 512),
            held_in(128, 128), held_in(16, 512), held_in(8, 512),
            held_in(1024, 256, dtype=BF16), held_in(192, 1024, dtype=BF16), held_in(192, 1024, dtype=BF16),
            held_in(1024, 192, dtype=BF16), held_in(1024, 192, dtype=BF16),
            held_in(2, 10, 216, 128), held_in(27, 8, 128), held_in(2, 8, 8, 128),
            held_in(2, 32, 128), held_in(64, 128), held_in(64, 512),
            held_in(5, 8, 8, 8, 128), held_in(25, 6, 8, 512), held_in(4, 5, 8, 512),
            held_in(4, 2, 4, 2, 16, 256), held_in(4, 4, 2, 16, 256), held_in(4, 2, 64, 256),
            held_in(7, 80, 256, dtype=jnp.int16), held_in(7, 80, 256, dtype=jnp.int16),
            DMA((16,)), DMA((16,)), DMA((2,)), DMA((2,)), DMA((2,)), DMA((2,)), DMA((8,)), DMA((8,)),
            DMA((11,)), DMA((11,)),
        ],
        compiler_params=pltpu.CompilerParams(
            collective_id=1, has_side_effects=True, vmem_limit_bytes=VMEM_LIMIT
        ),
    )(*args)
    return out.reshape(4, 2, 2, 8, 128)


def solution(mesh):
    placed = (
        P(None, None, None, "box", None),
        P(None, None, "dir", None),
        P(None, "box", None),
        P(None, None, "dir", None),
        P(None, None, None, "dir"),
        P(),
        P(),
        P(),
        P(),
        P(None, None, "dir"),
        P(None, None, "dir"),
        P(None, None, "dir"),
        P(None, None, None, "dir"),
        P(None, None, None, "dir"),
        P(None, None, None, "dir"),
        P(),
    )
    return jax.shard_map(
        shards,
        mesh=mesh,
        in_specs=placed,
        out_specs=P("dir", None, None, "box", None),
        check_vma=False,
    )
```

```python
import functools

import jax
import jax.numpy as jnp
import numpy as np
from jax import lax
from jax.experimental import pallas as pl
from jax.experimental.pallas import tpu as pltpu
from jax.sharding import PartitionSpec as P

MESH = pl.DeviceIdType.MESH
F32 = jnp.float32
BF16 = jnp.bfloat16
VMEM_LIMIT = 56 * 1024 * 1024
INPUTS = 17


def iota(shape, dim):
    return lax.broadcasted_iota(jnp.int32, shape, dim)


def split(a):
    high = a.astype(BF16)
    return high, (a - high.astype(F32)).astype(BF16)


def dot(a, b, dims=((1,), (0,))):
    return lax.dot_general(a, b, (dims, ((), ())), preferred_element_type=F32)


def dot3(a, b, dims=((1,), (0,))):
    a_high, a_low = split(a)
    b_high, b_low = split(b)
    return dot(a_high, b_high, dims) + (dot(a_high, b_low, dims) + dot(a_low, b_high, dims))


def dot_left(a, b, dims=((1,), (0,))):
    a_high, a_low = split(a)
    return dot(a_high, b, dims) + dot(a_low, b, dims)


def dot_right(a, b, dims=((1,), (0,))):
    b_high, b_low = split(b)
    return dot(a, b_high, dims) + dot(a, b_low, dims)


def onehot(condition):
    return jnp.where(condition, 1.0, 0.0).astype(BF16)


def interpolation(taps, level, theta, fine, coarse, wide, first, transposed):
    (fine_p, fine_t), (coarse_p, coarse_t) = fine, coarse
    if transposed:
        spread = onehot(iota((fine_t, fine_p * fine_t), 1) % fine_t == iota((fine_t, fine_p * fine_t), 0))
        tiled = jnp.concatenate([dot_left(theta, spread)] * coarse_p, axis=0)
        fine_dim, coarse_dim = 1, 0
    else:
        spread = onehot(
            iota((coarse_t, coarse_p * coarse_t), 1) % coarse_t == iota((coarse_t, coarse_p * coarse_t), 0)
        )
        tiled = jnp.concatenate([dot_left(theta, spread, ((0,), (0,)))] * fine_p, axis=0)
        fine_dim, coarse_dim = 0, 1
    p = iota(tiled.shape, fine_dim) // fine_t
    tap = iota(tiled.shape, coarse_dim) // coarse_t - first(p)
    even = wide(p) % 2 == 0
    weight = jnp.zeros(tiled.shape, F32)
    for j in range(3):
        value = jnp.where(even, taps[level, 0:1, j : j + 1], taps[level, 1:2, j : j + 1])
        weight = jnp.where(tap == j, value, weight)
    return weight * tiled


def turned(x):
    even = iota(x.shape, 1) % 2 == 0
    count = x.shape[1]
    return jnp.where(even, -pltpu.roll(x, count - 1, 1), pltpu.roll(x, 1, 1))


def child_of_box(index):
    return 4 * (index // 32 % 2) + 2 * (index // 8 % 2) + index % 2


def parent_of_box(index):
    return index // 64 * 8 + index // 16 % 2 * 4 + index // 2 % 4


def shifted_rows(block, shift, valid):
    moved = pltpu.roll(block, (-shift) % 8, 0) if shift % 8 else block
    return jnp.where(valid, moved, 0.0)


def cosines(angles):
    return jnp.concatenate([jnp.cos(angles), jnp.sin(angles)], axis=0)


def remote(source, target, send, receive, peer):
    return pltpu.make_async_remote_copy(
        src_ref=source, dst_ref=target, send_sem=send, recv_sem=receive, device_id=peer, device_id_type=MESH
    )


def whole(dirs, boxes, *refs):
    outside, out_ref, inside = refs[:INPUTS], refs[INPUTS], refs[INPUTS + 1 : 2 * INPUTS + 1]
    (
        leaf_rows, near_blocks, mask, radiate, receive, theta_one, theta_two, theta_three, taps,
        shift_one, shift_two, shift_three, trans_one, trans_two, trans_three, lists, shuffle,
    ) = inside
    (
        in_sem, wide_rows, source, message, gathered, rim_out, rims, leaf_halo, halo_one, halo_two, halo_three,
        one, two, three, leaf, shape_high, shape_low, far_high, far_low, products, rolled, near,
        table_one, table_two, table_three, ext_one, ext_two, ext_three,
        partial, got_core, held, coded, got_coded,
        send, receive_sem, rim_send, rim_receive, leaf_send, leaf_receive, halo_send, halo_receive,
        sum_send, sum_receive,
    ) = refs[2 * INPUTS + 1 :]
    me, box = lax.axis_index("dir"), lax.axis_index("box")
    has = {-1: box > 0, 1: box < boxes - 1, -2: box > 1, 2: box < boxes - 2}
    beside = {e: {"box": lax.rem(box + boxes + e, boxes)} for e in has}
    place_x, place_z, core = me // 4, me // 2 % 2, me % 2
    places = [(dx, dz, dc) for dz in (1, 0) for dx in (2, 1, 3, 0) for dc in (1, 0)][: dirs - 1]
    number = {p: 4 * lax.rem(place_x + p[0], 4) + 2 * ((place_z + p[1]) % 2) + (core + p[2]) % 2 for p in places}
    peers = {p: {"dir": number[p]} for p in places}
    slot = {p: 4 * p[0] + 2 * p[1] + p[2] for p in places}
    back = {p: slot[((4 - p[0]) % 4, p[1], p[2])] for p in places}
    after, before = {"dir": lax.rem(me + 1, dirs)}, {"dir": lax.rem(me + dirs - 1, dirs)}

    barrier = pltpu.get_barrier_semaphore()
    count = dirs - 1
    for p in places:
        pl.semaphore_signal(barrier, inc=1, device_id=peers[p], device_id_type=MESH)
    for e in has:
        @pl.when(has[e])
        def _(e=e):
            pl.semaphore_signal(barrier, inc=1, device_id=beside[e], device_id_type=MESH)

        count = count + jnp.where(has[e], 1, 0)

    loads = [pltpu.make_async_copy(outside[i], inside[i], in_sem.at[i]) for i in range(INPUTS)]
    early = (3, 4, 9, 10)
    for i in early:
        loads[i].start()
    for i in range(INPUTS):
        if i not in early:
            loads[i].start()
    for i in early:
        loads[i].wait()

    taken = [receive[c, :, u, :].astype(F32) for c in range(2) for u in range(4)]
    lane = iota((64, 128), 1)
    sent = [dot(radiate[c], onehot(lane == 2 * iota((64, 128), 0) + c)) for c in range(2)]
    tile = jnp.concatenate([jnp.concatenate(taken, axis=1), sent[0] + sent[1]], axis=0).astype(BF16)
    message[...] = tile
    gathered[0] = tile
    angles_one = jnp.concatenate([shift_one[:, a, :] for a in range(2)], axis=1)
    angles_two = jnp.concatenate([shift_two[:, a, :] for a in range(4)], axis=1)
    pad = jnp.zeros((8, 64), F32)
    rim_out[0] = jnp.concatenate([angles_one, angles_two[:, 96:], pad], axis=1)
    rim_out[1] = jnp.concatenate([angles_one, angles_two[:, :32], pad], axis=1)

    for i in range(INPUTS):
        if i not in early:
            loads[i].wait()
    up_one = interpolation(
        taps, 0, theta_one[...], (6, 16), (5, 8), lambda p: p, lambda p: p // 2, False
    )
    up_two = interpolation(
        taps, 1, theta_two[...], (6, 32), (6, 16), lambda p: p + 1, lambda p: (p + 1) // 2, False
    )
    back_two = interpolation(
        taps, 1, theta_two[...], (6, 32), (6, 16), lambda p: p + 1, lambda p: (p + 1) // 2, True
    )
    up_three = interpolation(
        taps, 2, theta_three[...], (8, 64), (6, 32), lambda p: p, lambda p: p // 2, True
    )
    wide_rows[...] = leaf_rows[...].astype(F32)
    for r in range(2):
        for x in range(8):
            layer = wide_rows[pl.ds(8 * r + x, 128, stride=16), :].astype(BF16)
            source[r, x % 2, :, 128 * (x // 2) : 128 * (x // 2) + 128] = layer
    for r in range(2):
        for ox in range(2):
            mixed = dot(source[r, ox], shuffle[...]).astype(BF16)
            for o in range(4):
                row = 128 * (4 * ox + o)
                leaf[row : row + 128, 128 * r : 128 * r + 128] = mixed[:, 128 * o : 128 * o + 128]
    for a in range(8):
        table_three[:, 64 * a : 64 * a + 64] = trans_three[:, a, :]
    for a in range(4):
        table_two[:, 32 * a : 32 * a + 32] = trans_two[:, a, :]
    for c in range(2):
        total = jnp.zeros((32, 128), F32)
        for a in range(2):
            place = onehot(iota((16, 128), 1) % 32 == 16 * a + iota((16, 128), 0))
            total = total + dot_left(trans_one[c, :, a, :], place, ((0,), (0,)))
        table_one[c] = total
    zero = jnp.zeros((8, 128), F32)
    for shift in range(5):
        for x in range(8):
            for y in (0, 1, 6, 7):
                ext_one[shift, x, y] = zero
    zero = jnp.zeros((8, 512), F32)
    for x in range(6):
        for shift in range(5):
            ext_two[shift, x] = zero
            ext_two[20 + shift, x] = zero
    for x in range(5):
        ext_three[3, x] = zero
    for side, e in enumerate((-1, 1)):
        @pl.when(jnp.logical_not(has[e]))
        def _(side=side):
            leaf_halo[side] = jnp.zeros((2, 128, 128), BF16)
            halo_one[side] = jnp.zeros((64, 128), F32)
            halo_two[side] = jnp.zeros((16, 512), F32)
    for layer, e in enumerate((-2, -1, 1, 2)):
        @pl.when(jnp.logical_not(has[e]))
        def _(layer=layer):
            halo_three[layer] = jnp.zeros((8, 512), F32)

    pl.semaphore_wait(barrier, count)
    table_copies = [
        remote(rim_out.at[0], rims.at[0], rim_send.at[0], rim_receive.at[0], after),
        remote(rim_out.at[1], rims.at[1], rim_send.at[1], rim_receive.at[1], before),
    ]
    for p in places:
        table_copies.append(
            remote(message, gathered.at[back[p]], send.at[back[p]], receive_sem.at[back[p]], peers[p])
        )
    for copy in table_copies:
        copy.start()
    lane = iota((64, 128), 1)
    double = dot(near_blocks[...], onehot(lane // 2 == iota((64, 128), 0))).astype(BF16)
    row, column = iota((216, 216), 0), iota((216, 216), 1)
    same = 8 * (row // 8) + 4 * (row % 2) + row % 8 // 2
    other = 8 * (row // 8) + 4 * (1 - row % 2) + row % 8 // 2
    kept = dot(onehot(column == same), double)
    crossed = dot(onehot(column == other), double)
    crossed = jnp.where(iota((216, 128), 0) % 2 == 0, -crossed, crossed)
    blocks = jnp.where(iota((216, 128), 1) % 2 == 0, kept, crossed).astype(BF16)
    lane = iota((8, 128), 1)
    for k in range(27):
        dy, dz = k // 3 % 3 - 1, k % 3 - 1
        y, z = lane // 16 + dy, lane % 16 + dz
        valid = (y >= 0) & (y < 8) & (z >= 0) & (z < 16)
        values = jnp.where(valid, mask[k].astype(F32), 0.0)
        rolled[k] = pltpu.roll(values, (16 * dy + dz) % 128, 1)
    for r in range(2):
        for ox in range(2):
            layers = dot(blocks, source[r, ox])
            for x in range(4):
                products[r, 1 + 2 * x + ox] = layers[:, 128 * x : 128 * x + 128]
    for copy in table_copies:
        copy.wait_send()
    for copy in table_copies:
        copy.wait_recv()
    pad = jnp.zeros((8, 32), F32)
    angles = jnp.concatenate([rims[0, :, 0:32], angles_one, rims[1, :, 0:32], pad], axis=1)
    turns = cosines(angles).T
    sources = []
    for a in range(5):
        owner = lax.rem(me + dirs - 2 + a, dirs)
        at = 4 * lax.rem(owner // 4 + 4 - place_x, 4) + 2 * ((owner // 2 + place_z) % 2) + (owner + core) % 2
        sources.append(gathered[at].astype(F32)[8:16])
    sources = jnp.concatenate(sources, axis=0)
    send_real = dot_left(up_one, sources.astype(BF16))
    send_turned = turned(send_real)
    even = iota((96, 128), 1) % 2 == 0
    for o in range(8):
        moved = turns[:96, o : o + 1] * send_real + turns[:96, 8 + o : 9 + o] * send_turned
        swapped = jnp.where(even, pltpu.roll(moved, 127, 1), pltpu.roll(moved, 1, 1))
        rows = jnp.concatenate([jnp.where(even, moved, -moved), swapped], axis=0)
        high, low = split(rows)
        shape_high[:, 128 * o : 128 * o + 128] = high
        shape_low[:, 128 * o : 128 * o + 128] = low
    level_one = dot(shape_high[...], leaf[...]) + dot(shape_low[...], leaf[...])
    own = jnp.concatenate(
        [level_one[96 * c + 32 : 96 * c + 64, 128 * r : 128 * r + 128] for c in range(2) for r in range(2)],
        axis=0,
    )
    one[...] = own.T
    halo_copies = [
        (e, remote(origin, target, halo_send.at[i], halo_receive.at[i], beside[e]))
        for i, (e, origin, target) in enumerate([
            (1, one.at[pl.ds(64, 64)], halo_one.at[0]),
            (-1, one.at[pl.ds(0, 64)], halo_one.at[1]),
            (1, two, halo_two.at[0]),
            (-1, two, halo_two.at[1]),
            (2, three, halo_three.at[0]),
            (1, three, halo_three.at[1]),
            (-1, three, halo_three.at[2]),
            (-2, three, halo_three.at[3]),
        ])
    ]
    for e, copy in halo_copies[:2]:
        pl.when(has[e])(copy.start)

    pad = jnp.zeros((8, 64), F32)
    angles = jnp.concatenate([rims[0, :, 32:64], angles_two, rims[1, :, 32:64], pad], axis=1)
    lane = iota((16, 256), 1)
    kind = child_of_box(lane % 128) + 8 * (lane // 128)
    phases = dot_left(cosines(angles).T[:192], onehot(iota((16, 256), 0) == kind))
    cosine_two, sine_two = phases[:, :128], phases[:, 128:]
    parent = onehot(parent_of_box(iota((16, 128), 1)) == iota((16, 128), 0))
    real = dot3(up_two, level_one[:96])
    imag = dot3(up_two, level_one[96:])
    parts = []
    for c in range(2):
        for r in range(2):
            x, y = real[:, 128 * r : 128 * r + 128], imag[:, 128 * r : 128 * r + 128]
            value = x * cosine_two - y * sine_two if c == 0 else y * cosine_two + x * sine_two
            parts.append(dot_right(parent, value, ((1,), (1,))))
    for index in range(4):
        two[:, 128 * index : 128 * index + 128] = parts[index][:, 32:160]
    for e, copy in halo_copies[2:4]:
        pl.when(has[e])(copy.start)
    level_two = jnp.concatenate(parts, axis=0)
    upper = dot3(level_two, up_three)
    turns_three = cosines(jnp.concatenate([shift_three[:, a, :] for a in range(8)], axis=1))
    row, column = iota((16, 8), 0), iota((16, 8), 1)
    expand = onehot(column == 4 * (row // 8) + 2 * (row // 4 % 2) + row % 2)
    cosine_three = dot_right(expand, turns_three[:8])
    sine_three = dot_right(expand, turns_three[8:])
    parts = []
    for c in range(2):
        for r in range(2):
            x, y = upper[16 * r : 16 * r + 16], upper[32 + 16 * r : 48 + 16 * r]
            parts.append(x * cosine_three - y * sine_three if c == 0 else y * cosine_three + x * sine_three)
    row = iota((8, 64), 1)
    together = onehot(row // 16 * 2 + row // 2 % 2 == iota((8, 64), 0))
    three[...] = dot_right(together, jnp.concatenate(parts, axis=0))
    for e, copy in halo_copies[4:]:
        pl.when(has[e])(copy.start)

    leaf_copies = [
        (1, remote(
            source.at[:, 1, :, pl.ds(384, 128)], leaf_halo.at[0], leaf_send.at[0], leaf_receive.at[0], beside[1]
        )),
        (-1, remote(
            source.at[:, 0, :, pl.ds(0, 128)], leaf_halo.at[1], leaf_send.at[1], leaf_receive.at[1], beside[-1]
        )),
    ]
    for e, copy in leaf_copies:
        pl.when(has[e])(copy.start)

    tables = gathered[...].astype(F32)
    stacked = jnp.concatenate([tables[e, 0:8] for e in range(16)], axis=0)
    row, lane = iota((128, 640), 0), iota((128, 640), 1)
    azimuth = (me + 14 + lane // 128) % 16
    pick = onehot(row == 64 * (lane % 2) + 16 * (lane % 8 // 2) + azimuth)
    placed = dot(stacked.astype(BF16), pick)
    owner = iota((8, 640), 1) % 128 // 8
    summed = jnp.where(owner == me, placed[0:8], 0.0)
    for p in places:
        summed = jnp.where(owner == number[p], placed[8 * slot[p] : 8 * slot[p] + 8], summed)
    targets = jnp.concatenate([summed[:, 128 * a : 128 * a + 128] for a in range(5)], axis=0)
    take_real = dot_left(up_one, targets.astype(BF16))
    take_turned = turned(take_real)
    for o in range(8):
        moved = turns[:96, o : o + 1] * take_real - turns[:96, 8 + o : 9 + o] * take_turned
        columns = jnp.concatenate([moved, turned(moved)], axis=0)
        high, low = split(columns.T)
        far_high[128 * o : 128 * o + 128, :] = high
        far_low[128 * o : 128 * o + 128, :] = low

    for e, copy in halo_copies[:2]:
        pl.when(has[-e])(copy.wait_recv)
    z = iota((8, 128), 0)
    for shift in range(5):
        dz = shift - 2
        valid = (z + dz >= 0) & (z + dz < 8)
        for x in range(8):
            for y in range(4):
                row = 8 * y + 32 * (x % 2)
                if x < 2 or x > 5:
                    block = halo_one[x // 4, row : row + 8, :]
                else:
                    block = one[32 * (x - 2) + 8 * y : 32 * (x - 2) + 8 * y + 8, :]
                ext_one[shift, x, y + 2] = shifted_rows(block, dz, valid)
    real = jnp.zeros((4, 4, 8, 128), F32)
    imag = jnp.zeros((4, 4, 8, 128), F32)
    for k in range(32):
        dx, dy, dz = lists[0, 0, k], lists[0, 1, k], lists[0, 2, k]
        window = ext_one[dz + 2, pl.ds(dx + 2, 4), pl.ds(dy + 2, 4)]
        real = real + window * table_one[0, k : k + 1, :]
        imag = imag + window * table_one[1, k : k + 1, :]
    imag = imag.reshape(128, 128)
    turned_imag = pltpu.roll(imag, 64, 1)
    field = real.reshape(128, 128) + jnp.where(iota((128, 128), 1) < 64, -turned_imag, turned_imag)
    field_one = field.T
    for e, copy in halo_copies[2:4]:
        pl.when(has[-e])(copy.wait_recv)
    y, z = iota((8, 512), 0) // 4, iota((8, 512), 0) % 4
    for shift in range(5, 20):
        dy, dz = shift // 5 - 2, shift % 5 - 2
        valid = (y + dy >= 0) & (y + dy < 2) & (z + dz >= 0) & (z + dz < 4)
        for x in range(6):
            row = 8 * (x % 2)
            if x < 2 or x > 3:
                block = halo_two[x // 3, row : row + 8, :]
            else:
                block = two[row : row + 8, :]
            ext_two[shift, x] = shifted_rows(block, 4 * dy + dz, valid)
    reals = [jnp.zeros((2, 8, 128), F32) for _ in range(4)]
    for k in range(32):
        dx, dy, dz = lists[1, 0, k], lists[1, 1, k], lists[1, 2, k]
        window = ext_two[5 * dy + dz + 12, pl.ds(dx + 2, 2)]
        x = table_two[2 * k : 2 * k + 1, :]
        y = table_two[2 * k + 1 : 2 * k + 2, :]
        parts = [window[:, :, 128 * i : 128 * i + 128] for i in range(4)]
        for r in range(2):
            reals[r] = reals[r] + (x * parts[r] - y * parts[2 + r])
            reals[2 + r] = reals[2 + r] + (x * parts[2 + r] + y * parts[r])
    side = jnp.zeros((64, 32), F32)
    field_two = jnp.concatenate([side, jnp.concatenate(reals, axis=0).reshape(64, 128), side], axis=1)
    for e, copy in halo_copies[4:]:
        pl.when(has[-e])(copy.wait_recv)
    z = iota((8, 512), 0) % 2
    for x in range(5):
        block = three[...] if x == 2 else halo_three[x - x // 3]
        for shift in range(3):
            dz = shift - 1
            ext_three[shift, x] = shifted_rows(block, dz, (z + dz >= 0) & (z + dz < 2))
    real = jnp.zeros((8, 512), F32)
    imag = jnp.zeros((8, 512), F32)
    for k in range(32):
        dx, dy, dz = lists[2, 0, k], lists[2, 1, k], lists[2, 2, k]
        inside = (dy == 0) & (dz >= -1) & (dz <= 1)
        window = ext_three[jnp.where(inside, dz + 1, 3), dx + 2]
        real = real + window * table_three[2 * k : 2 * k + 1, :]
        imag = imag + window * table_three[2 * k + 1 : 2 * k + 2, :]
    imag = pltpu.roll(imag, 4, 0)
    incoming = real + jnp.where(iota((8, 512), 0) < 4, -imag, imag)

    row = iota((64, 8), 0)
    apart = onehot(row // 16 * 2 + row // 2 % 2 == iota((64, 8), 1))
    spread = dot_right(apart, incoming)
    parts = []
    for c in range(2):
        for r in range(2):
            x, y = spread[16 * r : 16 * r + 16], spread[32 + 16 * r : 48 + 16 * r]
            parts.append(x * cosine_three + y * sine_three if c == 0 else y * cosine_three - x * sine_three)
    level_two = field_two + dot3(jnp.concatenate(parts, axis=0), up_three, ((1,), (1,)))
    columns = level_two.T
    spread = [dot_left(columns[:, 16 * i : 16 * i + 16], parent) for i in range(4)]
    real = jnp.concatenate([spread[r] * cosine_two + spread[2 + r] * sine_two for r in range(2)], axis=1)
    imag = jnp.concatenate([spread[2 + r] * cosine_two - spread[r] * sine_two for r in range(2)], axis=1)
    pad = jnp.zeros((32, 256), F32)
    level_one = []
    for c, value in enumerate((real, imag)):
        field = jnp.concatenate([field_one[64 * c + 32 * r : 64 * c + 32 * r + 32] for r in range(2)], axis=1)
        level_one.append(dot3(back_two, value) + jnp.concatenate([pad, field, pad], axis=0))
    high, low = split(jnp.concatenate(level_one, axis=0))

    sibling = peers[(0, 0, 1)]
    to_core = [
        remote(partial.at[i, 1 - core], got_core.at[i], sum_send.at[i], sum_receive.at[i], sibling)
        for i in range(4)
    ]
    across = peers[(0, 1, 0)]
    along = (2, 1, 3)
    to_x = []
    for part in range(2):
        for j, e in enumerate(along):
            there = 3 * part + along.index(4 - e)
            to_x.append(remote(
                coded.at[3 * part + j], got_coded.at[there], sum_send.at[4 + there], sum_receive.at[4 + there],
                peers[(e, 0, 0)],
            ))
    to_z = remote(coded.at[6], got_coded.at[6], sum_send.at[10], sum_receive.at[10], across)

    def encode(j, block):
        largest = jnp.max(jnp.abs(block), axis=0, keepdims=True)
        power = jnp.ceil(jnp.log2(jnp.maximum(largest, 1e-25)))
        values = jnp.floor(block * (32000.0 / jnp.exp2(power)) + 0.5)
        coded[j, 0:64] = values.astype(jnp.int32).astype(jnp.int16)
        coded[j, 64:80] = jnp.broadcast_to(power, (16, 256)).astype(jnp.int32).astype(jnp.int16)

    def decode(j):
        power = got_coded[j, 64:80].astype(jnp.int32).astype(F32)[0:1]
        return got_coded[j, 0:64].astype(jnp.int32).astype(F32) * (jnp.exp2(power) / 32000.0)

    def after_core(i):
        to_core[i].wait_recv()
        held[:, :, 16 * i : 16 * i + 16, :] = partial[i, core] + got_core[i]

    for i in range(4):
        for o in (2 * i, 2 * i + 1):
            rows = slice(128 * o, 128 * o + 128)
            total = dot(far_high[rows], high) + (dot(far_high[rows], low) + dot(far_low[rows], high))
            for owner in range(16):
                partial[i, owner % 2, owner // 4, owner // 2 % 2, 8 * (o % 2) : 8 * (o % 2) + 8, :] = total[
                    8 * owner : 8 * owner + 8
                ]
        to_core[i].start()
        if i > 0:
            after_core(i - 1)
    after_core(3)
    for j, e in enumerate(along):
        encode(j, held[lax.rem(place_x + e, 4), 1 - place_z])
        to_x[j].start()
    for j, e in enumerate(along):
        encode(3 + j, held[lax.rem(place_x + e, 4), place_z])
    for copy in to_x[:3]:
        copy.wait_recv()
    encode(6, held[place_x, 1 - place_z] + (decode(0) + decode(1) + decode(2)))
    to_z.start()
    for copy in to_x[3:]:
        copy.start()

    for e, copy in leaf_copies:
        pl.when(has[e])(copy.wait_send)
        pl.when(has[-e])(copy.wait_recv)
    for r in range(2):
        for side in range(2):
            products[r, 9 * side] = dot(blocks, leaf_halo[side, r])
    for r in range(2):
        for x in range(8):
            total = jnp.zeros((8, 128), F32)
            for inner in range(9):
                dy, dz = inner // 3 - 1, inner % 3 - 1
                term = jnp.zeros((8, 128), F32)
                for dx in range(3):
                    k = 9 * dx + inner
                    term = term + products[r, x + dx, 8 * k : 8 * k + 8, :] * rolled[k, x : x + 1, :]
                total = total + pltpu.roll(term, (-16 * dy - dz) % 128, 1)
            near[r, x] = total
    for copy in to_x[3:]:
        copy.wait_recv()
    far = held[place_x, place_z] + (decode(3) + decode(4) + decode(5))
    for e, copy in halo_copies:
        pl.when(has[e])(copy.wait_send)
    for copy in to_core + to_x:
        copy.wait_send()
    to_z.wait()
    far = far + decode(6)
    rows = []
    for r in range(2):
        for ox in range(2):
            pieces = [
                far[32 * ox + 8 * o : 32 * ox + 8 * o + 8, 128 * r : 128 * r + 128] for o in range(4)
            ]
            rows.append(jnp.concatenate(pieces, axis=1))
    high, low = split(jnp.concatenate(rows, axis=0))
    both = dot(jnp.concatenate([high, low], axis=0), shuffle[...], ((1,), (1,)))
    far = both[:32] + both[32:]
    for r in range(2):
        for ox in range(2):
            for x in range(4):
                row = 8 * (2 * r + ox)
                out_ref[:, r, 2 * x + ox, :] = (
                    near[r, 2 * x + ox] + far[row : row + 8, 128 * x : 128 * x + 128]
                )


VMEM = pl.BlockSpec(memory_space=pltpu.VMEM)
HBM = pl.BlockSpec(memory_space=pltpu.HBM)
DMA = pltpu.SemaphoreType.DMA


def held_in(*dims, dtype=F32):
    return pltpu.VMEM(dims, dtype)


def shuffle_table():
    index = np.arange(512)
    x, y, z = index // 128, index // 16 % 8, index % 16
    target = 256 * (y % 2) + 128 * (z % 2) + 32 * x + 8 * (y // 2) + z // 2
    return (target[:, None] == index[None, :]).astype(np.float32)


def shards(
    source, near_blocks, near_mask, radiate, receive, theta_one, theta_two, theta_three, phi_taps,
    shift_one, shift_two, shift_three, trans_one, trans_two, trans_three, far_lists,
):
    dirs, boxes = lax.axis_size("dir"), lax.axis_size("box")
    args = (
        source.reshape(2048, 128), near_blocks.reshape(216, 64), near_mask, radiate[:, :, 0], jnp.transpose(receive, (0, 1, 3, 2)),
        theta_one.T, theta_two.T, theta_three.T, phi_taps,
        jnp.transpose(shift_one, (0, 2, 1)), jnp.transpose(shift_two, (0, 2, 1)),
        jnp.transpose(shift_three, (0, 2, 1)), jnp.transpose(trans_one, (1, 2, 3, 0)),
        jnp.transpose(trans_two, (0, 1, 3, 2)).reshape(64, 4, 32),
        jnp.transpose(trans_three, (0, 1, 3, 2)).reshape(64, 8, 64),
        jnp.transpose(far_lists, (0, 2, 1)), jnp.asarray(shuffle_table(), BF16),
    )
    copies = [pltpu.VMEM(a.shape, a.dtype) for a in args]
    copies[15] = pltpu.SMEM(args[15].shape, args[15].dtype)
    out = pl.pallas_call(
        functools.partial(whole, dirs, boxes),
        out_shape=jax.ShapeDtypeStruct((8, 2, 8, 128), F32),
        in_specs=[HBM] * INPUTS,
        out_specs=VMEM,
        scratch_shapes=copies
        + [
            DMA((INPUTS,)), held_in(2048, 128), held_in(2, 2, 128, 512, dtype=BF16),
            held_in(16, 128, dtype=BF16), held_in(16, 16, 128, dtype=BF16), held_in(2, 8, 128), held_in(2, 8, 128),
            held_in(2, 2, 128, 128, dtype=BF16), held_in(2, 64, 128), held_in(2, 16, 512), held_in(4, 8, 512),
            held_in(128, 128), held_in(16, 512), held_in(8, 512),
            held_in(1024, 256, dtype=BF16), held_in(192, 1024, dtype=BF16), held_in(192, 1024, dtype=BF16),
            held_in(1024, 192, dtype=BF16), held_in(1024, 192, dtype=BF16),
            held_in(2, 10, 216, 128), held_in(27, 8, 128), held_in(2, 8, 8, 128),
            held_in(2, 32, 128), held_in(64, 128), held_in(64, 512),
            held_in(5, 8, 8, 8, 128), held_in(25, 6, 8, 512), held_in(4, 5, 8, 512),
            held_in(4, 2, 4, 2, 16, 256), held_in(4, 4, 2, 16, 256), held_in(4, 2, 64, 256),
            held_in(7, 80, 256, dtype=jnp.int16), held_in(7, 80, 256, dtype=jnp.int16),
            DMA((16,)), DMA((16,)), DMA((2,)), DMA((2,)), DMA((2,)), DMA((2,)), DMA((8,)), DMA((8,)),
            DMA((11,)), DMA((11,)),
        ],
        compiler_params=pltpu.CompilerParams(
            collective_id=1, has_side_effects=True, vmem_limit_bytes=VMEM_LIMIT
        ),
    )(*args)
    return out.reshape(4, 2, 2, 8, 128)


def solution(mesh):
    placed = (
        P(None, None, None, "box", None),
        P(None, None, "dir", None),
        P(None, "box", None),
        P(None, None, "dir", None),
        P(None, None, None, "dir"),
        P(),
        P(),
        P(),
        P(),
        P(None, None, "dir"),
        P(None, None, "dir"),
        P(None, None, "dir"),
        P(None, None, None, "dir"),
        P(None, None, None, "dir"),
        P(None, None, None, "dir"),
        P(),
    )
    return jax.shard_map(
        shards,
        mesh=mesh,
        in_specs=placed,
        out_specs=P("dir", None, None, "box", None),
        check_vma=False,
    )
```

```python
import functools

import jax
import jax.numpy as jnp
import numpy as np
from jax import lax
from jax.experimental import pallas as pl
from jax.experimental.pallas import tpu as pltpu
from jax.sharding import PartitionSpec as P

MESH = pl.DeviceIdType.MESH
F32 = jnp.float32
BF16 = jnp.bfloat16
VMEM_LIMIT = 56 * 1024 * 1024
INPUTS = 17


def iota(shape, dim):
    return lax.broadcasted_iota(jnp.int32, shape, dim)


def split(a):
    high = a.astype(BF16)
    return high, (a - high.astype(F32)).astype(BF16)


def dot(a, b, dims=((1,), (0,))):
    return lax.dot_general(a, b, (dims, ((), ())), preferred_element_type=F32)


def dot3(a, b, dims=((1,), (0,))):
    a_high, a_low = split(a)
    b_high, b_low = split(b)
    return dot(a_high, b_high, dims) + (dot(a_high, b_low, dims) + dot(a_low, b_high, dims))


def dot_left(a, b, dims=((1,), (0,))):
    a_high, a_low = split(a)
    return dot(a_high, b, dims) + dot(a_low, b, dims)


def dot_right(a, b, dims=((1,), (0,))):
    b_high, b_low = split(b)
    return dot(a, b_high, dims) + dot(a, b_low, dims)


def onehot(condition):
    return jnp.where(condition, 1.0, 0.0).astype(BF16)


def interpolation(taps, level, theta, fine, coarse, wide, first, transposed):
    (fine_p, fine_t), (coarse_p, coarse_t) = fine, coarse
    if transposed:
        spread = onehot(iota((fine_t, fine_p * fine_t), 1) % fine_t == iota((fine_t, fine_p * fine_t), 0))
        tiled = jnp.concatenate([dot_left(theta, spread)] * coarse_p, axis=0)
        fine_dim, coarse_dim = 1, 0
    else:
        spread = onehot(
            iota((coarse_t, coarse_p * coarse_t), 1) % coarse_t == iota((coarse_t, coarse_p * coarse_t), 0)
        )
        tiled = jnp.concatenate([dot_left(theta, spread, ((0,), (0,)))] * fine_p, axis=0)
        fine_dim, coarse_dim = 0, 1
    p = iota(tiled.shape, fine_dim) // fine_t
    tap = iota(tiled.shape, coarse_dim) // coarse_t - first(p)
    even = wide(p) % 2 == 0
    weight = jnp.zeros(tiled.shape, F32)
    for j in range(3):
        value = jnp.where(even, taps[level, 0:1, j : j + 1], taps[level, 1:2, j : j + 1])
        weight = jnp.where(tap == j, value, weight)
    return weight * tiled


def turned(x):
    even = iota(x.shape, 1) % 2 == 0
    count = x.shape[1]
    return jnp.where(even, -pltpu.roll(x, count - 1, 1), pltpu.roll(x, 1, 1))


def child_of_box(index):
    return 4 * (index // 32 % 2) + 2 * (index // 8 % 2) + index % 2


def parent_of_box(index):
    return index // 64 * 8 + index // 16 % 2 * 4 + index // 2 % 4


def shifted_rows(block, shift, valid):
    moved = pltpu.roll(block, (-shift) % 8, 0) if shift % 8 else block
    return jnp.where(valid, moved, 0.0)


def cosines(angles):
    return jnp.concatenate([jnp.cos(angles), jnp.sin(angles)], axis=0)


def remote(source, target, send, receive, peer):
    return pltpu.make_async_remote_copy(
        src_ref=source, dst_ref=target, send_sem=send, recv_sem=receive, device_id=peer, device_id_type=MESH
    )


def whole(dirs, boxes, *refs):
    outside, inside = refs[:INPUTS], refs[INPUTS + 2 : 2 * INPUTS + 2]
    far_ref, near_ref = refs[INPUTS], refs[INPUTS + 1]
    (
        leaf_rows, near_blocks, mask, radiate, receive, theta_one, theta_two, theta_three, taps,
        shift_one, shift_two, shift_three, trans_one, trans_two, trans_three, lists, shuffle,
    ) = inside
    (
        in_sem, wide_rows, source, message, gathered, rim_out, rims, leaf_halo, halo_one, halo_two, halo_three,
        one, two, three, leaf, shape_high, shape_low, far_high, far_low, products, rolled, near,
        table_one, table_two, table_three, ext_one, ext_two, ext_three,
        partial, got_core, held, coded, got_coded,
        send, receive_sem, rim_send, rim_receive, leaf_send, leaf_receive, halo_send, halo_receive,
        sum_send, sum_receive, near_sem,
    ) = refs[2 * INPUTS + 2 :]
    me, box = lax.axis_index("dir"), lax.axis_index("box")
    has = {-1: box > 0, 1: box < boxes - 1, -2: box > 1, 2: box < boxes - 2}
    beside = {e: {"box": lax.rem(box + boxes + e, boxes)} for e in has}
    place_x, place_z, core = me // 4, me // 2 % 2, me % 2
    places = [(dx, dz, dc) for dz in (1, 0) for dx in (2, 1, 3, 0) for dc in (1, 0)][: dirs - 1]
    number = {p: 4 * lax.rem(place_x + p[0], 4) + 2 * ((place_z + p[1]) % 2) + (core + p[2]) % 2 for p in places}
    peers = {p: {"dir": number[p]} for p in places}
    slot = {p: 4 * p[0] + 2 * p[1] + p[2] for p in places}
    back = {p: slot[((4 - p[0]) % 4, p[1], p[2])] for p in places}
    after, before = {"dir": lax.rem(me + 1, dirs)}, {"dir": lax.rem(me + dirs - 1, dirs)}

    barrier = pltpu.get_barrier_semaphore()
    count = dirs - 1
    for p in places:
        pl.semaphore_signal(barrier, inc=1, device_id=peers[p], device_id_type=MESH)
    for e in has:
        @pl.when(has[e])
        def _(e=e):
            pl.semaphore_signal(barrier, inc=1, device_id=beside[e], device_id_type=MESH)

        count = count + jnp.where(has[e], 1, 0)

    loads = [pltpu.make_async_copy(outside[i], inside[i], in_sem.at[i]) for i in range(INPUTS)]
    early = (3, 4, 9, 10)
    for i in early:
        loads[i].start()
    for i in range(INPUTS):
        if i not in early:
            loads[i].start()
    for i in early:
        loads[i].wait()

    taken = [receive[c, :, u, :].astype(F32) for c in range(2) for u in range(4)]
    lane = iota((64, 128), 1)
    sent = [dot(radiate[c], onehot(lane == 2 * iota((64, 128), 0) + c)) for c in range(2)]
    tile = jnp.concatenate([jnp.concatenate(taken, axis=1), sent[0] + sent[1]], axis=0).astype(BF16)
    message[...] = tile
    gathered[0] = tile
    angles_one = jnp.concatenate([shift_one[:, a, :] for a in range(2)], axis=1)
    angles_two = jnp.concatenate([shift_two[:, a, :] for a in range(4)], axis=1)
    pad = jnp.zeros((8, 64), F32)
    rim_out[0] = jnp.concatenate([angles_one, angles_two[:, 96:], pad], axis=1)
    rim_out[1] = jnp.concatenate([angles_one, angles_two[:, :32], pad], axis=1)

    for i in range(INPUTS):
        if i not in early:
            loads[i].wait()
    up_one = interpolation(
        taps, 0, theta_one[...], (6, 16), (5, 8), lambda p: p, lambda p: p // 2, False
    )
    up_two = interpolation(
        taps, 1, theta_two[...], (6, 32), (6, 16), lambda p: p + 1, lambda p: (p + 1) // 2, False
    )
    back_two = interpolation(
        taps, 1, theta_two[...], (6, 32), (6, 16), lambda p: p + 1, lambda p: (p + 1) // 2, True
    )
    up_three = interpolation(
        taps, 2, theta_three[...], (8, 64), (6, 32), lambda p: p, lambda p: p // 2, True
    )
    wide_rows[...] = leaf_rows[...].astype(F32)
    for r in range(2):
        for x in range(8):
            layer = wide_rows[pl.ds(8 * r + x, 128, stride=16), :].astype(BF16)
            source[r, x % 2, :, 128 * (x // 2) : 128 * (x // 2) + 128] = layer
    for r in range(2):
        for ox in range(2):
            mixed = dot(source[r, ox], shuffle[...]).astype(BF16)
            for o in range(4):
                row = 128 * (4 * ox + o)
                leaf[row : row + 128, 128 * r : 128 * r + 128] = mixed[:, 128 * o : 128 * o + 128]
    for a in range(8):
        table_three[:, 64 * a : 64 * a + 64] = trans_three[:, a, :]
    for a in range(4):
        table_two[:, 32 * a : 32 * a + 32] = trans_two[:, a, :]
    for c in range(2):
        total = jnp.zeros((32, 128), F32)
        for a in range(2):
            place = onehot(iota((16, 128), 1) % 32 == 16 * a + iota((16, 128), 0))
            total = total + dot_left(trans_one[c, :, a, :], place, ((0,), (0,)))
        table_one[c] = total
    zero = jnp.zeros((8, 128), F32)
    for shift in range(5):
        for x in range(8):
            for y in (0, 1, 6, 7):
                ext_one[shift, x, y] = zero
    zero = jnp.zeros((8, 512), F32)
    for x in range(6):
        for shift in range(5):
            ext_two[shift, x] = zero
            ext_two[20 + shift, x] = zero
    for x in range(5):
        ext_three[3, x] = zero
    for side, e in enumerate((-1, 1)):
        @pl.when(jnp.logical_not(has[e]))
        def _(side=side):
            leaf_halo[side] = jnp.zeros((2, 128, 128), BF16)
            halo_one[side] = jnp.zeros((64, 128), F32)
            halo_two[side] = jnp.zeros((16, 512), F32)
    for layer, e in enumerate((-2, -1, 1, 2)):
        @pl.when(jnp.logical_not(has[e]))
        def _(layer=layer):
            halo_three[layer] = jnp.zeros((8, 512), F32)

    pl.semaphore_wait(barrier, count)
    table_copies = [
        remote(rim_out.at[0], rims.at[0], rim_send.at[0], rim_receive.at[0], after),
        remote(rim_out.at[1], rims.at[1], rim_send.at[1], rim_receive.at[1], before),
    ]
    for p in places:
        table_copies.append(
            remote(message, gathered.at[back[p]], send.at[back[p]], receive_sem.at[back[p]], peers[p])
        )
    for copy in table_copies:
        copy.start()
    lane = iota((64, 128), 1)
    double = dot(near_blocks[...], onehot(lane // 2 == iota((64, 128), 0))).astype(BF16)
    row, column = iota((216, 216), 0), iota((216, 216), 1)
    same = 8 * (row // 8) + 4 * (row % 2) + row % 8 // 2
    other = 8 * (row // 8) + 4 * (1 - row % 2) + row % 8 // 2
    kept = dot(onehot(column == same), double)
    crossed = dot(onehot(column == other), double)
    crossed = jnp.where(iota((216, 128), 0) % 2 == 0, -crossed, crossed)
    blocks = jnp.where(iota((216, 128), 1) % 2 == 0, kept, crossed).astype(BF16)
    lane = iota((8, 128), 1)
    for k in range(27):
        dy, dz = k // 3 % 3 - 1, k % 3 - 1
        y, z = lane // 16 + dy, lane % 16 + dz
        valid = (y >= 0) & (y < 8) & (z >= 0) & (z < 16)
        values = jnp.where(valid, mask[k].astype(F32), 0.0)
        rolled[k] = pltpu.roll(values, (16 * dy + dz) % 128, 1)
    for r in range(2):
        for ox in range(2):
            layers = dot(blocks, source[r, ox])
            for x in range(4):
                products[r, 1 + 2 * x + ox] = layers[:, 128 * x : 128 * x + 128]
    for copy in table_copies:
        copy.wait_send()
    for copy in table_copies:
        copy.wait_recv()
    pad = jnp.zeros((8, 32), F32)
    angles = jnp.concatenate([rims[0, :, 0:32], angles_one, rims[1, :, 0:32], pad], axis=1)
    turns = cosines(angles).T
    sources = []
    for a in range(5):
        owner = lax.rem(me + dirs - 2 + a, dirs)
        at = 4 * lax.rem(owner // 4 + 4 - place_x, 4) + 2 * ((owner // 2 + place_z) % 2) + (owner + core) % 2
        sources.append(gathered[at].astype(F32)[8:16])
    sources = jnp.concatenate(sources, axis=0)
    send_real = dot_left(up_one, sources.astype(BF16))
    send_turned = turned(send_real)
    even = iota((96, 128), 1) % 2 == 0
    for o in range(8):
        moved = turns[:96, o : o + 1] * send_real + turns[:96, 8 + o : 9 + o] * send_turned
        swapped = jnp.where(even, pltpu.roll(moved, 127, 1), pltpu.roll(moved, 1, 1))
        rows = jnp.concatenate([jnp.where(even, moved, -moved), swapped], axis=0)
        high, low = split(rows)
        shape_high[:, 128 * o : 128 * o + 128] = high
        shape_low[:, 128 * o : 128 * o + 128] = low
    level_one = dot(shape_high[...], leaf[...]) + dot(shape_low[...], leaf[...])
    own = jnp.concatenate(
        [level_one[96 * c + 32 : 96 * c + 64, 128 * r : 128 * r + 128] for c in range(2) for r in range(2)],
        axis=0,
    )
    one[...] = own.T
    halo_copies = [
        (e, remote(origin, target, halo_send.at[i], halo_receive.at[i], beside[e]))
        for i, (e, origin, target) in enumerate([
            (1, one.at[pl.ds(64, 64)], halo_one.at[0]),
            (-1, one.at[pl.ds(0, 64)], halo_one.at[1]),
            (1, two, halo_two.at[0]),
            (-1, two, halo_two.at[1]),
            (2, three, halo_three.at[0]),
            (1, three, halo_three.at[1]),
            (-1, three, halo_three.at[2]),
            (-2, three, halo_three.at[3]),
        ])
    ]
    for e, copy in halo_copies[:2]:
        pl.when(has[e])(copy.start)

    pad = jnp.zeros((8, 64), F32)
    angles = jnp.concatenate([rims[0, :, 32:64], angles_two, rims[1, :, 32:64], pad], axis=1)
    lane = iota((16, 256), 1)
    kind = child_of_box(lane % 128) + 8 * (lane // 128)
    phases = dot_left(cosines(angles).T[:192], onehot(iota((16, 256), 0) == kind))
    cosine_two, sine_two = phases[:, :128], phases[:, 128:]
    parent = onehot(parent_of_box(iota((16, 128), 1)) == iota((16, 128), 0))
    real = dot3(up_two, level_one[:96])
    imag = dot3(up_two, level_one[96:])
    parts = []
    for c in range(2):
        for r in range(2):
            x, y = real[:, 128 * r : 128 * r + 128], imag[:, 128 * r : 128 * r + 128]
            value = x * cosine_two - y * sine_two if c == 0 else y * cosine_two + x * sine_two
            parts.append(dot_right(parent, value, ((1,), (1,))))
    for index in range(4):
        two[:, 128 * index : 128 * index + 128] = parts[index][:, 32:160]
    for e, copy in halo_copies[2:4]:
        pl.when(has[e])(copy.start)
    level_two = jnp.concatenate(parts, axis=0)
    upper = dot3(level_two, up_three)
    turns_three = cosines(jnp.concatenate([shift_three[:, a, :] for a in range(8)], axis=1))
    row, column = iota((16, 8), 0), iota((16, 8), 1)
    expand = onehot(column == 4 * (row // 8) + 2 * (row // 4 % 2) + row % 2)
    cosine_three = dot_right(expand, turns_three[:8])
    sine_three = dot_right(expand, turns_three[8:])
    parts = []
    for c in range(2):
        for r in range(2):
            x, y = upper[16 * r : 16 * r + 16], upper[32 + 16 * r : 48 + 16 * r]
            parts.append(x * cosine_three - y * sine_three if c == 0 else y * cosine_three + x * sine_three)
    row = iota((8, 64), 1)
    together = onehot(row // 16 * 2 + row // 2 % 2 == iota((8, 64), 0))
    three[...] = dot_right(together, jnp.concatenate(parts, axis=0))
    for e, copy in halo_copies[4:]:
        pl.when(has[e])(copy.start)

    leaf_copies = [
        (1, remote(
            source.at[:, 1, :, pl.ds(384, 128)], leaf_halo.at[0], leaf_send.at[0], leaf_receive.at[0], beside[1]
        )),
        (-1, remote(
            source.at[:, 0, :, pl.ds(0, 128)], leaf_halo.at[1], leaf_send.at[1], leaf_receive.at[1], beside[-1]
        )),
    ]
    for e, copy in leaf_copies:
        pl.when(has[e])(copy.start)

    tables = gathered[...].astype(F32)
    stacked = jnp.concatenate([tables[e, 0:8] for e in range(16)], axis=0)
    row, lane = iota((128, 640), 0), iota((128, 640), 1)
    azimuth = (me + 14 + lane // 128) % 16
    pick = onehot(row == 64 * (lane % 2) + 16 * (lane % 8 // 2) + azimuth)
    placed = dot(stacked.astype(BF16), pick)
    owner = iota((8, 640), 1) % 128 // 8
    summed = jnp.where(owner == me, placed[0:8], 0.0)
    for p in places:
        summed = jnp.where(owner == number[p], placed[8 * slot[p] : 8 * slot[p] + 8], summed)
    targets = jnp.concatenate([summed[:, 128 * a : 128 * a + 128] for a in range(5)], axis=0)
    take_real = dot_left(up_one, targets.astype(BF16))
    take_turned = turned(take_real)
    for o in range(8):
        moved = turns[:96, o : o + 1] * take_real - turns[:96, 8 + o : 9 + o] * take_turned
        columns = jnp.concatenate([moved, turned(moved)], axis=0)
        high, low = split(columns.T)
        far_high[128 * o : 128 * o + 128, :] = high
        far_low[128 * o : 128 * o + 128, :] = low

    for e, copy in halo_copies[:2]:
        pl.when(has[-e])(copy.wait_recv)
    z = iota((8, 128), 0)
    for shift in range(5):
        dz = shift - 2
        valid = (z + dz >= 0) & (z + dz < 8)
        for x in range(8):
            for y in range(4):
                row = 8 * y + 32 * (x % 2)
                if x < 2 or x > 5:
                    block = halo_one[x // 4, row : row + 8, :]
                else:
                    block = one[32 * (x - 2) + 8 * y : 32 * (x - 2) + 8 * y + 8, :]
                ext_one[shift, x, y + 2] = shifted_rows(block, dz, valid)
    real = jnp.zeros((4, 4, 8, 128), F32)
    imag = jnp.zeros((4, 4, 8, 128), F32)
    for k in range(32):
        dx, dy, dz = lists[0, 0, k], lists[0, 1, k], lists[0, 2, k]
        window = ext_one[dz + 2, pl.ds(dx + 2, 4), pl.ds(dy + 2, 4)]
        real = real + window * table_one[0, k : k + 1, :]
        imag = imag + window * table_one[1, k : k + 1, :]
    imag = imag.reshape(128, 128)
    turned_imag = pltpu.roll(imag, 64, 1)
    field = real.reshape(128, 128) + jnp.where(iota((128, 128), 1) < 64, -turned_imag, turned_imag)
    field_one = field.T
    for e, copy in halo_copies[2:4]:
        pl.when(has[-e])(copy.wait_recv)
    y, z = iota((8, 512), 0) // 4, iota((8, 512), 0) % 4
    for shift in range(5, 20):
        dy, dz = shift // 5 - 2, shift % 5 - 2
        valid = (y + dy >= 0) & (y + dy < 2) & (z + dz >= 0) & (z + dz < 4)
        for x in range(6):
            row = 8 * (x % 2)
            if x < 2 or x > 3:
                block = halo_two[x // 3, row : row + 8, :]
            else:
                block = two[row : row + 8, :]
            ext_two[shift, x] = shifted_rows(block, 4 * dy + dz, valid)
    reals = [jnp.zeros((2, 8, 128), F32) for _ in range(4)]
    for k in range(32):
        dx, dy, dz = lists[1, 0, k], lists[1, 1, k], lists[1, 2, k]
        window = ext_two[5 * dy + dz + 12, pl.ds(dx + 2, 2)]
        x = table_two[2 * k : 2 * k + 1, :]
        y = table_two[2 * k + 1 : 2 * k + 2, :]
        parts = [window[:, :, 128 * i : 128 * i + 128] for i in range(4)]
        for r in range(2):
            reals[r] = reals[r] + (x * parts[r] - y * parts[2 + r])
            reals[2 + r] = reals[2 + r] + (x * parts[2 + r] + y * parts[r])
    side = jnp.zeros((64, 32), F32)
    field_two = jnp.concatenate([side, jnp.concatenate(reals, axis=0).reshape(64, 128), side], axis=1)
    for e, copy in halo_copies[4:]:
        pl.when(has[-e])(copy.wait_recv)
    z = iota((8, 512), 0) % 2
    for x in range(5):
        block = three[...] if x == 2 else halo_three[x - x // 3]
        for shift in range(3):
            dz = shift - 1
            ext_three[shift, x] = shifted_rows(block, dz, (z + dz >= 0) & (z + dz < 2))
    real = jnp.zeros((8, 512), F32)
    imag = jnp.zeros((8, 512), F32)
    for k in range(32):
        dx, dy, dz = lists[2, 0, k], lists[2, 1, k], lists[2, 2, k]
        inside = (dy == 0) & (dz >= -1) & (dz <= 1)
        window = ext_three[jnp.where(inside, dz + 1, 3), dx + 2]
        real = real + window * table_three[2 * k : 2 * k + 1, :]
        imag = imag + window * table_three[2 * k + 1 : 2 * k + 2, :]
    imag = pltpu.roll(imag, 4, 0)
    incoming = real + jnp.where(iota((8, 512), 0) < 4, -imag, imag)

    row = iota((64, 8), 0)
    apart = onehot(row // 16 * 2 + row // 2 % 2 == iota((64, 8), 1))
    spread = dot_right(apart, incoming)
    parts = []
    for c in range(2):
        for r in range(2):
            x, y = spread[16 * r : 16 * r + 16], spread[32 + 16 * r : 48 + 16 * r]
            parts.append(x * cosine_three + y * sine_three if c == 0 else y * cosine_three - x * sine_three)
    level_two = field_two + dot3(jnp.concatenate(parts, axis=0), up_three, ((1,), (1,)))
    columns = level_two.T
    spread = [dot_left(columns[:, 16 * i : 16 * i + 16], parent) for i in range(4)]
    real = jnp.concatenate([spread[r] * cosine_two + spread[2 + r] * sine_two for r in range(2)], axis=1)
    imag = jnp.concatenate([spread[2 + r] * cosine_two - spread[r] * sine_two for r in range(2)], axis=1)
    pad = jnp.zeros((32, 256), F32)
    level_one = []
    for c, value in enumerate((real, imag)):
        field = jnp.concatenate([field_one[64 * c + 32 * r : 64 * c + 32 * r + 32] for r in range(2)], axis=1)
        level_one.append(dot3(back_two, value) + jnp.concatenate([pad, field, pad], axis=0))
    high, low = split(jnp.concatenate(level_one, axis=0))

    sibling = peers[(0, 0, 1)]
    to_core = [
        remote(partial.at[i, 1 - core], got_core.at[i], sum_send.at[i], sum_receive.at[i], sibling)
        for i in range(4)
    ]
    across = peers[(0, 1, 0)]
    along = (2, 1, 3)
    to_x = []
    for part in range(2):
        for j, e in enumerate(along):
            there = 3 * part + along.index(4 - e)
            to_x.append(remote(
                coded.at[3 * part + j], got_coded.at[there], sum_send.at[4 + there], sum_receive.at[4 + there],
                peers[(e, 0, 0)],
            ))
    to_z = remote(coded.at[6], got_coded.at[6], sum_send.at[10], sum_receive.at[10], across)

    def encode(j, block):
        largest = jnp.max(jnp.abs(block), axis=0, keepdims=True)
        power = jnp.ceil(jnp.log2(jnp.maximum(largest, 1e-25)))
        values = jnp.floor(block * (32000.0 / jnp.exp2(power)) + 0.5)
        coded[j, 0:64] = values.astype(jnp.int32).astype(jnp.int16)
        coded[j, 64:80] = jnp.broadcast_to(power, (16, 256)).astype(jnp.int32).astype(jnp.int16)

    def decode(j):
        power = got_coded[j, 64:80].astype(jnp.int32).astype(F32)[0:1]
        return got_coded[j, 0:64].astype(jnp.int32).astype(F32) * (jnp.exp2(power) / 32000.0)

    def after_core(i):
        to_core[i].wait_recv()
        held[:, :, 16 * i : 16 * i + 16, :] = partial[i, core] + got_core[i]

    for i in range(4):
        for o in (2 * i, 2 * i + 1):
            rows = slice(128 * o, 128 * o + 128)
            total = dot(far_high[rows], high) + (dot(far_high[rows], low) + dot(far_low[rows], high))
            for owner in range(16):
                partial[i, owner % 2, owner // 4, owner // 2 % 2, 8 * (o % 2) : 8 * (o % 2) + 8, :] = total[
                    8 * owner : 8 * owner + 8
                ]
        to_core[i].start()
        if i > 0:
            after_core(i - 1)
    after_core(3)
    for j, e in enumerate(along):
        encode(j, held[lax.rem(place_x + e, 4), 1 - place_z])
        to_x[j].start()
    for j, e in enumerate(along):
        encode(3 + j, held[lax.rem(place_x + e, 4), place_z])
    for copy in to_x[:3]:
        copy.wait_recv()
    encode(6, held[place_x, 1 - place_z] + (decode(0) + decode(1) + decode(2)))
    to_z.start()
    for copy in to_x[3:]:
        copy.start()

    for e, copy in leaf_copies:
        pl.when(has[e])(copy.wait_send)
        pl.when(has[-e])(copy.wait_recv)
    for r in range(2):
        for side in range(2):
            products[r, 9 * side] = dot(blocks, leaf_halo[side, r])
    for r in range(2):
        for x in range(8):
            total = jnp.zeros((8, 128), F32)
            for inner in range(9):
                dy, dz = inner // 3 - 1, inner % 3 - 1
                term = jnp.zeros((8, 128), F32)
                for dx in range(3):
                    k = 9 * dx + inner
                    term = term + products[r, x + dx, 8 * k : 8 * k + 8, :] * rolled[k, x : x + 1, :]
                total = total + pltpu.roll(term, (-16 * dy - dz) % 128, 1)
            near[:, r, x, :] = total
    near_copy = pltpu.make_async_copy(near, near_ref, near_sem)
    near_copy.start()
    for copy in to_x[3:]:
        copy.wait_recv()
    far = held[place_x, place_z] + (decode(3) + decode(4) + decode(5))
    for e, copy in halo_copies:
        pl.when(has[e])(copy.wait_send)
    for copy in to_core + to_x:
        copy.wait_send()
    to_z.wait()
    far = far + decode(6)
    rows = []
    for r in range(2):
        for ox in range(2):
            pieces = [
                far[32 * ox + 8 * o : 32 * ox + 8 * o + 8, 128 * r : 128 * r + 128] for o in range(4)
            ]
            rows.append(jnp.concatenate(pieces, axis=1))
    high, low = split(jnp.concatenate(rows, axis=0))
    both = dot(jnp.concatenate([high, low], axis=0), shuffle[...], ((1,), (1,)))
    far = both[:32] + both[32:]
    for r in range(2):
        for ox in range(2):
            for x in range(4):
                row = 8 * (2 * r + ox)
                far_ref[:, r, 2 * x + ox, :] = far[row : row + 8, 128 * x : 128 * x + 128]
    near_copy.wait()


VMEM = pl.BlockSpec(memory_space=pltpu.VMEM)
HBM = pl.BlockSpec(memory_space=pltpu.HBM)
DMA = pltpu.SemaphoreType.DMA


def held_in(*dims, dtype=F32):
    return pltpu.VMEM(dims, dtype)


def shuffle_table():
    index = np.arange(512)
    x, y, z = index // 128, index // 16 % 8, index % 16
    target = 256 * (y % 2) + 128 * (z % 2) + 32 * x + 8 * (y // 2) + z // 2
    return (target[:, None] == index[None, :]).astype(np.float32)


def shards(
    source, near_blocks, near_mask, radiate, receive, theta_one, theta_two, theta_three, phi_taps,
    shift_one, shift_two, shift_three, trans_one, trans_two, trans_three, far_lists,
):
    dirs, boxes = lax.axis_size("dir"), lax.axis_size("box")
    args = (
        source.reshape(2048, 128), near_blocks.reshape(216, 64), near_mask, radiate[:, :, 0], jnp.transpose(receive, (0, 1, 3, 2)),
        theta_one.T, theta_two.T, theta_three.T, phi_taps,
        jnp.transpose(shift_one, (0, 2, 1)), jnp.transpose(shift_two, (0, 2, 1)),
        jnp.transpose(shift_three, (0, 2, 1)), jnp.transpose(trans_one, (1, 2, 3, 0)),
        jnp.transpose(trans_two, (0, 1, 3, 2)).reshape(64, 4, 32),
        jnp.transpose(trans_three, (0, 1, 3, 2)).reshape(64, 8, 64),
        jnp.transpose(far_lists, (0, 2, 1)), jnp.asarray(shuffle_table(), BF16),
    )
    copies = [pltpu.VMEM(a.shape, a.dtype) for a in args]
    copies[15] = pltpu.SMEM(args[15].shape, args[15].dtype)
    far, near = pl.pallas_call(
        functools.partial(whole, dirs, boxes),
        out_shape=[jax.ShapeDtypeStruct((8, 2, 8, 128), F32)] * 2,
        in_specs=[HBM] * INPUTS,
        out_specs=[VMEM, HBM],
        scratch_shapes=copies
        + [
            DMA((INPUTS,)), held_in(2048, 128), held_in(2, 2, 128, 512, dtype=BF16),
            held_in(16, 128, dtype=BF16), held_in(16, 16, 128, dtype=BF16), held_in(2, 8, 128), held_in(2, 8, 128),
            held_in(2, 2, 128, 128, dtype=BF16), held_in(2, 64, 128), held_in(2, 16, 512), held_in(4, 8, 512),
            held_in(128, 128), held_in(16, 512), held_in(8, 512),
            held_in(1024, 256, dtype=BF16), held_in(192, 1024, dtype=BF16), held_in(192, 1024, dtype=BF16),
            held_in(1024, 192, dtype=BF16), held_in(1024, 192, dtype=BF16),
            held_in(2, 10, 216, 128), held_in(27, 8, 128), held_in(8, 2, 8, 128),
            held_in(2, 32, 128), held_in(64, 128), held_in(64, 512),
            held_in(5, 8, 8, 8, 128), held_in(25, 6, 8, 512), held_in(4, 5, 8, 512),
            held_in(4, 2, 4, 2, 16, 256), held_in(4, 4, 2, 16, 256), held_in(4, 2, 64, 256),
            held_in(7, 80, 256, dtype=jnp.int16), held_in(7, 80, 256, dtype=jnp.int16),
            DMA((16,)), DMA((16,)), DMA((2,)), DMA((2,)), DMA((2,)), DMA((2,)), DMA((8,)), DMA((8,)),
            DMA((11,)), DMA((11,)), DMA,
        ],
        compiler_params=pltpu.CompilerParams(
            collective_id=1, has_side_effects=True, vmem_limit_bytes=VMEM_LIMIT
        ),
    )(*args)
    return (far + near).reshape(4, 2, 2, 8, 128)


def solution(mesh):
    placed = (
        P(None, None, None, "box", None),
        P(None, None, "dir", None),
        P(None, "box", None),
        P(None, None, "dir", None),
        P(None, None, None, "dir"),
        P(),
        P(),
        P(),
        P(),
        P(None, None, "dir"),
        P(None, None, "dir"),
        P(None, None, "dir"),
        P(None, None, None, "dir"),
        P(None, None, None, "dir"),
        P(None, None, None, "dir"),
        P(),
    )
    return jax.shard_map(
        shards,
        mesh=mesh,
        in_specs=placed,
        out_specs=P("dir", None, None, "box", None),
        check_vma=False,
    )
```

```python
import functools

import jax
import jax.numpy as jnp
import numpy as np
from jax import lax
from jax.experimental import pallas as pl
from jax.experimental.pallas import tpu as pltpu
from jax.sharding import PartitionSpec as P

MESH = pl.DeviceIdType.MESH
F32 = jnp.float32
BF16 = jnp.bfloat16
VMEM_LIMIT = 56 * 1024 * 1024
INPUTS = 17


def iota(shape, dim):
    return lax.broadcasted_iota(jnp.int32, shape, dim)


def split(a):
    high = a.astype(BF16)
    return high, (a - high.astype(F32)).astype(BF16)


def dot(a, b, dims=((1,), (0,))):
    return lax.dot_general(a, b, (dims, ((), ())), preferred_element_type=F32)


def dot3(a, b, dims=((1,), (0,))):
    a_high, a_low = split(a)
    b_high, b_low = split(b)
    return dot(a_high, b_high, dims) + (dot(a_high, b_low, dims) + dot(a_low, b_high, dims))


def dot_left(a, b, dims=((1,), (0,))):
    a_high, a_low = split(a)
    return dot(a_high, b, dims) + dot(a_low, b, dims)


def dot_right(a, b, dims=((1,), (0,))):
    b_high, b_low = split(b)
    return dot(a, b_high, dims) + dot(a, b_low, dims)


def onehot(condition):
    return jnp.where(condition, 1.0, 0.0).astype(BF16)


def interpolation(taps, level, theta, fine, coarse, wide, first, transposed):
    (fine_p, fine_t), (coarse_p, coarse_t) = fine, coarse
    if transposed:
        spread = onehot(iota((fine_t, fine_p * fine_t), 1) % fine_t == iota((fine_t, fine_p * fine_t), 0))
        tiled = jnp.concatenate([dot_left(theta, spread)] * coarse_p, axis=0)
        fine_dim, coarse_dim = 1, 0
    else:
        spread = onehot(
            iota((coarse_t, coarse_p * coarse_t), 1) % coarse_t == iota((coarse_t, coarse_p * coarse_t), 0)
        )
        tiled = jnp.concatenate([dot_left(theta, spread, ((0,), (0,)))] * fine_p, axis=0)
        fine_dim, coarse_dim = 0, 1
    p = iota(tiled.shape, fine_dim) // fine_t
    tap = iota(tiled.shape, coarse_dim) // coarse_t - first(p)
    even = wide(p) % 2 == 0
    weight = jnp.zeros(tiled.shape, F32)
    for j in range(3):
        value = jnp.where(even, taps[level, 0:1, j : j + 1], taps[level, 1:2, j : j + 1])
        weight = jnp.where(tap == j, value, weight)
    return weight * tiled


def turned(x):
    even = iota(x.shape, 1) % 2 == 0
    count = x.shape[1]
    return jnp.where(even, -pltpu.roll(x, count - 1, 1), pltpu.roll(x, 1, 1))


def child_of_box(index):
    return 4 * (index // 32 % 2) + 2 * (index // 8 % 2) + index % 2


def parent_of_box(index):
    return index // 64 * 8 + index // 16 % 2 * 4 + index // 2 % 4


def shifted_rows(block, shift, valid):
    moved = pltpu.roll(block, (-shift) % 8, 0) if shift % 8 else block
    return jnp.where(valid, moved, 0.0)


def cosines(angles):
    return jnp.concatenate([jnp.cos(angles), jnp.sin(angles)], axis=0)


def remote(source, target, send, receive, peer):
    return pltpu.make_async_remote_copy(
        src_ref=source, dst_ref=target, send_sem=send, recv_sem=receive, device_id=peer, device_id_type=MESH
    )


def whole(dirs, boxes, *refs):
    outside, out_ref, inside = refs[:INPUTS], refs[INPUTS], refs[INPUTS + 1 : 2 * INPUTS + 1]
    (
        leaf_rows, near_blocks, mask, radiate, receive, theta_one, theta_two, theta_three, taps,
        shift_one, shift_two, shift_three, trans_one, trans_two, trans_three, lists, shuffle,
    ) = inside
    (
        in_sem, wide_rows, source, message, gathered, rim_out, rims, leaf_halo, halo_one, halo_two, halo_three,
        one, two, three, leaf, shape_high, shape_low, far_high, far_low, products, rolled, near,
        table_one, table_two, table_three, ext_one, ext_two, ext_three,
        partial, got_core, held, coded, got_coded,
        send, receive_sem, rim_send, rim_receive, leaf_send, leaf_receive, halo_send, halo_receive,
        sum_send, sum_receive,
    ) = refs[2 * INPUTS + 1 :]
    me, box = lax.axis_index("dir"), lax.axis_index("box")
    has = {-1: box > 0, 1: box < boxes - 1, -2: box > 1, 2: box < boxes - 2}
    beside = {e: {"box": lax.rem(box + boxes + e, boxes)} for e in has}
    place_x, place_z, core = me // 4, me // 2 % 2, me % 2
    places = [(dx, dz, dc) for dz in (1, 0) for dx in (2, 1, 3, 0) for dc in (1, 0)][: dirs - 1]
    number = {p: 4 * lax.rem(place_x + p[0], 4) + 2 * ((place_z + p[1]) % 2) + (core + p[2]) % 2 for p in places}
    peers = {p: {"dir": number[p]} for p in places}
    slot = {p: 4 * p[0] + 2 * p[1] + p[2] for p in places}
    back = {p: slot[((4 - p[0]) % 4, p[1], p[2])] for p in places}
    after, before = {"dir": lax.rem(me + 1, dirs)}, {"dir": lax.rem(me + dirs - 1, dirs)}

    barrier = pltpu.get_barrier_semaphore()
    count = dirs - 1
    for p in places:
        pl.semaphore_signal(barrier, inc=1, device_id=peers[p], device_id_type=MESH)
    for e in has:
        @pl.when(has[e])
        def _(e=e):
            pl.semaphore_signal(barrier, inc=1, device_id=beside[e], device_id_type=MESH)

        count = count + jnp.where(has[e], 1, 0)

    loads = [pltpu.make_async_copy(outside[i], inside[i], in_sem.at[i]) for i in range(INPUTS)]
    early = (3, 4, 9, 10)
    for i in early:
        loads[i].start()
    for i in range(INPUTS):
        if i not in early:
            loads[i].start()
    for i in early:
        loads[i].wait()

    taken = [receive[c, :, u, :].astype(F32) for c in range(2) for u in range(4)]
    lane = iota((64, 128), 1)
    sent = [dot(radiate[c], onehot(lane == 2 * iota((64, 128), 0) + c)) for c in range(2)]
    tile = jnp.concatenate([jnp.concatenate(taken, axis=1), sent[0] + sent[1]], axis=0).astype(BF16)
    message[...] = tile
    gathered[0] = tile
    angles_one = jnp.concatenate([shift_one[:, a, :] for a in range(2)], axis=1)
    angles_two = jnp.concatenate([shift_two[:, a, :] for a in range(4)], axis=1)
    pad = jnp.zeros((8, 64), F32)
    rim_out[0] = jnp.concatenate([angles_one, angles_two[:, 96:], pad], axis=1)
    rim_out[1] = jnp.concatenate([angles_one, angles_two[:, :32], pad], axis=1)

    for i in range(INPUTS):
        if i not in early:
            loads[i].wait()
    up_one = interpolation(
        taps, 0, theta_one[...], (6, 16), (5, 8), lambda p: p, lambda p: p // 2, False
    )
    up_two = interpolation(
        taps, 1, theta_two[...], (6, 32), (6, 16), lambda p: p + 1, lambda p: (p + 1) // 2, False
    )
    back_two = interpolation(
        taps, 1, theta_two[...], (6, 32), (6, 16), lambda p: p + 1, lambda p: (p + 1) // 2, True
    )
    up_three = interpolation(
        taps, 2, theta_three[...], (8, 64), (6, 32), lambda p: p, lambda p: p // 2, True
    )
    wide_rows[...] = leaf_rows[...].astype(F32)
    for r in range(2):
        for x in range(8):
            layer = wide_rows[pl.ds(8 * r + x, 128, stride=16), :].astype(BF16)
            source[r, x % 2, :, 128 * (x // 2) : 128 * (x // 2) + 128] = layer
    for r in range(2):
        for ox in range(2):
            mixed = dot(source[r, ox], shuffle[...]).astype(BF16)
            for o in range(4):
                row = 128 * (4 * ox + o)
                leaf[row : row + 128, 128 * r : 128 * r + 128] = mixed[:, 128 * o : 128 * o + 128]
    for a in range(8):
        table_three[:, 64 * a : 64 * a + 64] = trans_three[:, a, :]
    for a in range(4):
        table_two[:, 32 * a : 32 * a + 32] = trans_two[:, a, :]
    for c in range(2):
        total = jnp.zeros((32, 128), F32)
        for a in range(2):
            place = onehot(iota((16, 128), 1) % 32 == 16 * a + iota((16, 128), 0))
            total = total + dot_left(trans_one[c, :, a, :], place, ((0,), (0,)))
        table_one[c] = total
    turns_three = cosines(jnp.concatenate([shift_three[:, a, :] for a in range(8)], axis=1))
    row, column = iota((16, 8), 0), iota((16, 8), 1)
    expand = onehot(column == 4 * (row // 8) + 2 * (row // 4 % 2) + row % 2)
    cosine_three = dot_right(expand, turns_three[:8])
    sine_three = dot_right(expand, turns_three[8:])
    zero = jnp.zeros((8, 128), F32)
    for shift in range(5):
        for x in range(8):
            for y in (0, 1, 6, 7):
                ext_one[shift, x, y] = zero
    zero = jnp.zeros((8, 512), F32)
    for x in range(6):
        for shift in range(5):
            ext_two[shift, x] = zero
            ext_two[20 + shift, x] = zero
    for x in range(5):
        ext_three[3, x] = zero
    for side, e in enumerate((-1, 1)):
        @pl.when(jnp.logical_not(has[e]))
        def _(side=side):
            leaf_halo[side] = jnp.zeros((2, 128, 128), BF16)
            halo_one[side] = jnp.zeros((64, 128), F32)
            halo_two[side] = jnp.zeros((16, 512), F32)
    for layer, e in enumerate((-2, -1, 1, 2)):
        @pl.when(jnp.logical_not(has[e]))
        def _(layer=layer):
            halo_three[layer] = jnp.zeros((8, 512), F32)

    pl.semaphore_wait(barrier, count)
    table_copies = [
        remote(rim_out.at[0], rims.at[0], rim_send.at[0], rim_receive.at[0], after),
        remote(rim_out.at[1], rims.at[1], rim_send.at[1], rim_receive.at[1], before),
    ]
    for p in places:
        table_copies.append(
            remote(message, gathered.at[back[p]], send.at[back[p]], receive_sem.at[back[p]], peers[p])
        )
    for copy in table_copies:
        copy.start()
    lane = iota((64, 128), 1)
    double = dot(near_blocks[...], onehot(lane // 2 == iota((64, 128), 0))).astype(BF16)
    row, column = iota((216, 216), 0), iota((216, 216), 1)
    same = 8 * (row // 8) + 4 * (row % 2) + row % 8 // 2
    other = 8 * (row // 8) + 4 * (1 - row % 2) + row % 8 // 2
    kept = dot(onehot(column == same), double)
    crossed = dot(onehot(column == other), double)
    crossed = jnp.where(iota((216, 128), 0) % 2 == 0, -crossed, crossed)
    blocks = jnp.where(iota((216, 128), 1) % 2 == 0, kept, crossed).astype(BF16)
    lane = iota((8, 128), 1)
    for k in range(27):
        dy, dz = k // 3 % 3 - 1, k % 3 - 1
        y, z = lane // 16 + dy, lane % 16 + dz
        valid = (y >= 0) & (y < 8) & (z >= 0) & (z < 16)
        values = jnp.where(valid, mask[k].astype(F32), 0.0)
        rolled[k] = pltpu.roll(values, (16 * dy + dz) % 128, 1)
    for r in range(2):
        for ox in range(2):
            layers = dot(blocks, source[r, ox])
            for x in range(4):
                products[r, 1 + 2 * x + ox] = layers[:, 128 * x : 128 * x + 128]
    for copy in table_copies:
        copy.wait_send()
    for copy in table_copies:
        copy.wait_recv()
    pad = jnp.zeros((8, 32), F32)
    angles = jnp.concatenate([rims[0, :, 0:32], angles_one, rims[1, :, 0:32], pad], axis=1)
    turns = cosines(angles).T
    sources = []
    for a in range(5):
        owner = lax.rem(me + dirs - 2 + a, dirs)
        at = 4 * lax.rem(owner // 4 + 4 - place_x, 4) + 2 * ((owner // 2 + place_z) % 2) + (owner + core) % 2
        sources.append(gathered[at].astype(F32)[8:16])
    sources = jnp.concatenate(sources, axis=0)
    send_real = dot_left(up_one, sources.astype(BF16))
    send_turned = turned(send_real)
    even = iota((96, 128), 1) % 2 == 0
    for o in range(8):
        moved = turns[:96, o : o + 1] * send_real + turns[:96, 8 + o : 9 + o] * send_turned
        swapped = jnp.where(even, pltpu.roll(moved, 127, 1), pltpu.roll(moved, 1, 1))
        rows = jnp.concatenate([jnp.where(even, moved, -moved), swapped], axis=0)
        high, low = split(rows)
        shape_high[:, 128 * o : 128 * o + 128] = high
        shape_low[:, 128 * o : 128 * o + 128] = low
    pad = jnp.zeros((8, 64), F32)
    angles = jnp.concatenate([rims[0, :, 32:64], angles_two, rims[1, :, 32:64], pad], axis=1)
    lane = iota((16, 256), 1)
    kind = child_of_box(lane % 128) + 8 * (lane // 128)
    phases = dot_left(cosines(angles).T[:192], onehot(iota((16, 256), 0) == kind))
    cosine_two, sine_two = phases[:, :128], phases[:, 128:]
    parent = onehot(parent_of_box(iota((16, 128), 1)) == iota((16, 128), 0))
    level_one = dot(shape_high[...], leaf[...]) + dot(shape_low[...], leaf[...])
    own = jnp.concatenate(
        [level_one[96 * c + 32 : 96 * c + 64, 128 * r : 128 * r + 128] for c in range(2) for r in range(2)],
        axis=0,
    )
    one[...] = own.T
    halo_copies = [
        (e, remote(origin, target, halo_send.at[i], halo_receive.at[i], beside[e]))
        for i, (e, origin, target) in enumerate([
            (1, one.at[pl.ds(64, 64)], halo_one.at[0]),
            (-1, one.at[pl.ds(0, 64)], halo_one.at[1]),
            (1, two, halo_two.at[0]),
            (-1, two, halo_two.at[1]),
            (2, three, halo_three.at[0]),
            (1, three, halo_three.at[1]),
            (-1, three, halo_three.at[2]),
            (-2, three, halo_three.at[3]),
        ])
    ]
    for e, copy in halo_copies[:2]:
        pl.when(has[e])(copy.start)

    real = dot3(up_two, level_one[:96])
    imag = dot3(up_two, level_one[96:])
    parts = []
    for c in range(2):
        for r in range(2):
            x, y = real[:, 128 * r : 128 * r + 128], imag[:, 128 * r : 128 * r + 128]
            value = x * cosine_two - y * sine_two if c == 0 else y * cosine_two + x * sine_two
            parts.append(dot_right(parent, value, ((1,), (1,))))
    for index in range(4):
        two[:, 128 * index : 128 * index + 128] = parts[index][:, 32:160]
    for e, copy in halo_copies[2:4]:
        pl.when(has[e])(copy.start)
    level_two = jnp.concatenate(parts, axis=0)
    upper = dot3(level_two, up_three)
    parts = []
    for c in range(2):
        for r in range(2):
            x, y = upper[16 * r : 16 * r + 16], upper[32 + 16 * r : 48 + 16 * r]
            parts.append(x * cosine_three - y * sine_three if c == 0 else y * cosine_three + x * sine_three)
    row = iota((8, 64), 1)
    together = onehot(row // 16 * 2 + row // 2 % 2 == iota((8, 64), 0))
    three[...] = dot_right(together, jnp.concatenate(parts, axis=0))
    for e, copy in halo_copies[4:]:
        pl.when(has[e])(copy.start)

    leaf_copies = [
        (1, remote(
            source.at[:, 1, :, pl.ds(384, 128)], leaf_halo.at[0], leaf_send.at[0], leaf_receive.at[0], beside[1]
        )),
        (-1, remote(
            source.at[:, 0, :, pl.ds(0, 128)], leaf_halo.at[1], leaf_send.at[1], leaf_receive.at[1], beside[-1]
        )),
    ]
    for e, copy in leaf_copies:
        pl.when(has[e])(copy.start)

    tables = gathered[...].astype(F32)
    stacked = jnp.concatenate([tables[e, 0:8] for e in range(16)], axis=0)
    row, lane = iota((128, 640), 0), iota((128, 640), 1)
    azimuth = (me + 14 + lane // 128) % 16
    pick = onehot(row == 64 * (lane % 2) + 16 * (lane % 8 // 2) + azimuth)
    placed = dot(stacked.astype(BF16), pick)
    owner = iota((8, 640), 1) % 128 // 8
    summed = jnp.where(owner == me, placed[0:8], 0.0)
    for p in places:
        summed = jnp.where(owner == number[p], placed[8 * slot[p] : 8 * slot[p] + 8], summed)
    targets = jnp.concatenate([summed[:, 128 * a : 128 * a + 128] for a in range(5)], axis=0)
    take_real = dot_left(up_one, targets.astype(BF16))
    take_turned = turned(take_real)
    for o in range(8):
        moved = turns[:96, o : o + 1] * take_real - turns[:96, 8 + o : 9 + o] * take_turned
        columns = jnp.concatenate([moved, turned(moved)], axis=0)
        high, low = split(columns.T)
        far_high[128 * o : 128 * o + 128, :] = high
        far_low[128 * o : 128 * o + 128, :] = low

    for e, copy in halo_copies[:2]:
        pl.when(has[-e])(copy.wait_recv)
    z = iota((8, 128), 0)
    for shift in range(5):
        dz = shift - 2
        valid = (z + dz >= 0) & (z + dz < 8)
        for x in range(8):
            for y in range(4):
                row = 8 * y + 32 * (x % 2)
                if x < 2 or x > 5:
                    block = halo_one[x // 4, row : row + 8, :]
                else:
                    block = one[32 * (x - 2) + 8 * y : 32 * (x - 2) + 8 * y + 8, :]
                ext_one[shift, x, y + 2] = shifted_rows(block, dz, valid)
    real = jnp.zeros((4, 4, 8, 128), F32)
    imag = jnp.zeros((4, 4, 8, 128), F32)
    for k in range(32):
        dx, dy, dz = lists[0, 0, k], lists[0, 1, k], lists[0, 2, k]
        window = ext_one[dz + 2, pl.ds(dx + 2, 4), pl.ds(dy + 2, 4)]
        real = real + window * table_one[0, k : k + 1, :]
        imag = imag + window * table_one[1, k : k + 1, :]
    imag = imag.reshape(128, 128)
    turned_imag = pltpu.roll(imag, 64, 1)
    field = real.reshape(128, 128) + jnp.where(iota((128, 128), 1) < 64, -turned_imag, turned_imag)
    field_one = field.T
    for e, copy in halo_copies[2:4]:
        pl.when(has[-e])(copy.wait_recv)
    y, z = iota((8, 512), 0) // 4, iota((8, 512), 0) % 4
    for shift in range(5, 20):
        dy, dz = shift // 5 - 2, shift % 5 - 2
        valid = (y + dy >= 0) & (y + dy < 2) & (z + dz >= 0) & (z + dz < 4)
        for x in range(6):
            row = 8 * (x % 2)
            if x < 2 or x > 3:
                block = halo_two[x // 3, row : row + 8, :]
            else:
                block = two[row : row + 8, :]
            ext_two[shift, x] = shifted_rows(block, 4 * dy + dz, valid)
    reals = [jnp.zeros((2, 8, 128), F32) for _ in range(4)]
    for k in range(32):
        dx, dy, dz = lists[1, 0, k], lists[1, 1, k], lists[1, 2, k]
        window = ext_two[5 * dy + dz + 12, pl.ds(dx + 2, 2)]
        x = table_two[2 * k : 2 * k + 1, :]
        y = table_two[2 * k + 1 : 2 * k + 2, :]
        parts = [window[:, :, 128 * i : 128 * i + 128] for i in range(4)]
        for r in range(2):
            reals[r] = reals[r] + (x * parts[r] - y * parts[2 + r])
            reals[2 + r] = reals[2 + r] + (x * parts[2 + r] + y * parts[r])
    side = jnp.zeros((64, 32), F32)
    field_two = jnp.concatenate([side, jnp.concatenate(reals, axis=0).reshape(64, 128), side], axis=1)
    for e, copy in halo_copies[4:]:
        pl.when(has[-e])(copy.wait_recv)
    z = iota((8, 512), 0) % 2
    for x in range(5):
        block = three[...] if x == 2 else halo_three[x - x // 3]
        for shift in range(3):
            dz = shift - 1
            ext_three[shift, x] = shifted_rows(block, dz, (z + dz >= 0) & (z + dz < 2))
    real = jnp.zeros((8, 512), F32)
    imag = jnp.zeros((8, 512), F32)
    for k in range(32):
        dx, dy, dz = lists[2, 0, k], lists[2, 1, k], lists[2, 2, k]
        inside = (dy == 0) & (dz >= -1) & (dz <= 1)
        window = ext_three[jnp.where(inside, dz + 1, 3), dx + 2]
        real = real + window * table_three[2 * k : 2 * k + 1, :]
        imag = imag + window * table_three[2 * k + 1 : 2 * k + 2, :]
    imag = pltpu.roll(imag, 4, 0)
    incoming = real + jnp.where(iota((8, 512), 0) < 4, -imag, imag)

    row = iota((64, 8), 0)
    apart = onehot(row // 16 * 2 + row // 2 % 2 == iota((64, 8), 1))
    spread = dot_right(apart, incoming)
    parts = []
    for c in range(2):
        for r in range(2):
            x, y = spread[16 * r : 16 * r + 16], spread[32 + 16 * r : 48 + 16 * r]
            parts.append(x * cosine_three + y * sine_three if c == 0 else y * cosine_three - x * sine_three)
    level_two = field_two + dot3(jnp.concatenate(parts, axis=0), up_three, ((1,), (1,)))
    columns = level_two.T
    spread = [dot_left(columns[:, 16 * i : 16 * i + 16], parent) for i in range(4)]
    real = jnp.concatenate([spread[r] * cosine_two + spread[2 + r] * sine_two for r in range(2)], axis=1)
    imag = jnp.concatenate([spread[2 + r] * cosine_two - spread[r] * sine_two for r in range(2)], axis=1)
    pad = jnp.zeros((32, 256), F32)
    level_one = []
    for c, value in enumerate((real, imag)):
        field = jnp.concatenate([field_one[64 * c + 32 * r : 64 * c + 32 * r + 32] for r in range(2)], axis=1)
        level_one.append(dot3(back_two, value) + jnp.concatenate([pad, field, pad], axis=0))
    high, low = split(jnp.concatenate(level_one, axis=0))

    sibling = peers[(0, 0, 1)]
    to_core = [
        remote(partial.at[i, 1 - core], got_core.at[i], sum_send.at[i], sum_receive.at[i], sibling)
        for i in range(4)
    ]
    across = peers[(0, 1, 0)]
    along = (2, 1, 3)
    to_x = []
    for part in range(2):
        for j, e in enumerate(along):
            there = 3 * part + along.index(4 - e)
            to_x.append(remote(
                coded.at[3 * part + j], got_coded.at[there], sum_send.at[4 + there], sum_receive.at[4 + there],
                peers[(e, 0, 0)],
            ))
    to_z = remote(coded.at[6], got_coded.at[6], sum_send.at[10], sum_receive.at[10], across)

    def encode(j, block):
        largest = jnp.max(jnp.abs(block), axis=0, keepdims=True)
        power = jnp.ceil(jnp.log2(jnp.maximum(largest, 1e-25)))
        values = jnp.floor(block * (32000.0 / jnp.exp2(power)) + 0.5)
        coded[j, 0:64] = values.astype(jnp.int32).astype(jnp.int16)
        coded[j, 64:80] = jnp.broadcast_to(power, (16, 256)).astype(jnp.int32).astype(jnp.int16)

    def decode(j):
        power = got_coded[j, 64:80].astype(jnp.int32).astype(F32)[0:1]
        return got_coded[j, 0:64].astype(jnp.int32).astype(F32) * (jnp.exp2(power) / 32000.0)

    def after_core(i):
        to_core[i].wait_recv()
        held[:, :, 16 * i : 16 * i + 16, :] = partial[i, core] + got_core[i]

    for i in range(4):
        for o in (2 * i, 2 * i + 1):
            rows = slice(128 * o, 128 * o + 128)
            total = dot(far_high[rows], high) + (dot(far_high[rows], low) + dot(far_low[rows], high))
            for owner in range(16):
                partial[i, owner % 2, owner // 4, owner // 2 % 2, 8 * (o % 2) : 8 * (o % 2) + 8, :] = total[
                    8 * owner : 8 * owner + 8
                ]
        to_core[i].start()
        if i > 0:
            after_core(i - 1)
    after_core(3)
    for j, e in enumerate(along):
        encode(j, held[lax.rem(place_x + e, 4), 1 - place_z])
        to_x[j].start()
    for j, e in enumerate(along):
        encode(3 + j, held[lax.rem(place_x + e, 4), place_z])
    for copy in to_x[:3]:
        copy.wait_recv()
    encode(6, held[place_x, 1 - place_z] + (decode(0) + decode(1) + decode(2)))
    to_z.start()
    for copy in to_x[3:]:
        copy.start()

    for e, copy in leaf_copies:
        pl.when(has[e])(copy.wait_send)
        pl.when(has[-e])(copy.wait_recv)
    for r in range(2):
        for side in range(2):
            products[r, 9 * side] = dot(blocks, leaf_halo[side, r])
    for r in range(2):
        for x in range(8):
            total = jnp.zeros((8, 128), F32)
            for inner in range(9):
                dy, dz = inner // 3 - 1, inner % 3 - 1
                term = jnp.zeros((8, 128), F32)
                for dx in range(3):
                    k = 9 * dx + inner
                    term = term + products[r, x + dx, 8 * k : 8 * k + 8, :] * rolled[k, x : x + 1, :]
                total = total + pltpu.roll(term, (-16 * dy - dz) % 128, 1)
            near[r, x] = total
    for copy in to_x[3:]:
        copy.wait_recv()
    far = held[place_x, place_z] + (decode(3) + decode(4) + decode(5))
    for e, copy in halo_copies:
        pl.when(has[e])(copy.wait_send)
    for copy in to_core + to_x:
        copy.wait_send()
    to_z.wait()
    far = far + decode(6)
    rows = []
    for r in range(2):
        for ox in range(2):
            pieces = [
                far[32 * ox + 8 * o : 32 * ox + 8 * o + 8, 128 * r : 128 * r + 128] for o in range(4)
            ]
            rows.append(jnp.concatenate(pieces, axis=1))
    high, low = split(jnp.concatenate(rows, axis=0))
    both = dot(jnp.concatenate([high, low], axis=0), shuffle[...], ((1,), (1,)))
    far = both[:32] + both[32:]
    for r in range(2):
        for ox in range(2):
            for x in range(4):
                row = 8 * (2 * r + ox)
                out_ref[:, r, 2 * x + ox, :] = (
                    near[r, 2 * x + ox] + far[row : row + 8, 128 * x : 128 * x + 128]
                )


VMEM = pl.BlockSpec(memory_space=pltpu.VMEM)
HBM = pl.BlockSpec(memory_space=pltpu.HBM)
DMA = pltpu.SemaphoreType.DMA


def held_in(*dims, dtype=F32):
    return pltpu.VMEM(dims, dtype)


def shuffle_table():
    index = np.arange(512)
    x, y, z = index // 128, index // 16 % 8, index % 16
    target = 256 * (y % 2) + 128 * (z % 2) + 32 * x + 8 * (y // 2) + z // 2
    return (target[:, None] == index[None, :]).astype(np.float32)


def shards(
    source, near_blocks, near_mask, radiate, receive, theta_one, theta_two, theta_three, phi_taps,
    shift_one, shift_two, shift_three, trans_one, trans_two, trans_three, far_lists,
):
    dirs, boxes = lax.axis_size("dir"), lax.axis_size("box")
    args = (
        source.reshape(2048, 128), near_blocks.reshape(216, 64), near_mask, radiate[:, :, 0], jnp.transpose(receive, (0, 1, 3, 2)),
        theta_one.T, theta_two.T, theta_three.T, phi_taps,
        jnp.transpose(shift_one, (0, 2, 1)), jnp.transpose(shift_two, (0, 2, 1)),
        jnp.transpose(shift_three, (0, 2, 1)), jnp.transpose(trans_one, (1, 2, 3, 0)),
        jnp.transpose(trans_two, (0, 1, 3, 2)).reshape(64, 4, 32),
        jnp.transpose(trans_three, (0, 1, 3, 2)).reshape(64, 8, 64),
        jnp.transpose(far_lists, (0, 2, 1)), jnp.asarray(shuffle_table(), BF16),
    )
    copies = [pltpu.VMEM(a.shape, a.dtype) for a in args]
    copies[15] = pltpu.SMEM(args[15].shape, args[15].dtype)
    out = pl.pallas_call(
        functools.partial(whole, dirs, boxes),
        out_shape=jax.ShapeDtypeStruct((8, 2, 8, 128), F32),
        in_specs=[HBM] * INPUTS,
        out_specs=VMEM,
        scratch_shapes=copies
        + [
            DMA((INPUTS,)), held_in(2048, 128), held_in(2, 2, 128, 512, dtype=BF16),
            held_in(16, 128, dtype=BF16), held_in(16, 16, 128, dtype=BF16), held_in(2, 8, 128), held_in(2, 8, 128),
            held_in(2, 2, 128, 128, dtype=BF16), held_in(2, 64, 128), held_in(2, 16, 512), held_in(4, 8, 512),
            held_in(128, 128), held_in(16, 512), held_in(8, 512),
            held_in(1024, 256, dtype=BF16), held_in(192, 1024, dtype=BF16), held_in(192, 1024, dtype=BF16),
            held_in(1024, 192, dtype=BF16), held_in(1024, 192, dtype=BF16),
            held_in(2, 10, 216, 128), held_in(27, 8, 128), held_in(2, 8, 8, 128),
            held_in(2, 32, 128), held_in(64, 128), held_in(64, 512),
            held_in(5, 8, 8, 8, 128), held_in(25, 6, 8, 512), held_in(4, 5, 8, 512),
            held_in(4, 2, 4, 2, 16, 256), held_in(4, 4, 2, 16, 256), held_in(4, 2, 64, 256),
            held_in(7, 80, 256, dtype=jnp.int16), held_in(7, 80, 256, dtype=jnp.int16),
            DMA((16,)), DMA((16,)), DMA((2,)), DMA((2,)), DMA((2,)), DMA((2,)), DMA((8,)), DMA((8,)),
            DMA((11,)), DMA((11,)),
        ],
        compiler_params=pltpu.CompilerParams(
            collective_id=1, has_side_effects=True, vmem_limit_bytes=VMEM_LIMIT
        ),
    )(*args)
    return out.reshape(4, 2, 2, 8, 128)


def solution(mesh):
    placed = (
        P(None, None, None, "box", None),
        P(None, None, "dir", None),
        P(None, "box", None),
        P(None, None, "dir", None),
        P(None, None, None, "dir"),
        P(),
        P(),
        P(),
        P(),
        P(None, None, "dir"),
        P(None, None, "dir"),
        P(None, None, "dir"),
        P(None, None, None, "dir"),
        P(None, None, None, "dir"),
        P(None, None, None, "dir"),
        P(),
    )
    return jax.shard_map(
        shards,
        mesh=mesh,
        in_specs=placed,
        out_specs=P("dir", None, None, "box", None),
        check_vma=False,
    )
```
